32 devices in a mesh: batch: 8 (over z, x), height: 4 (over y, core).
Axes of the slice: x: 2, y: 2, z: 4, core: 2. Of those that a mesh axis runs over, the one named last changes fastest.
Arguments:
- activations: bfloat16 [24, 32, 28, 192], P('batch', 'height'), may hold values from -6 to 6
- cotangent: bfloat16 [24, 32, 28, 192], P('batch', 'height'), may hold values from -6 to 6
- extent: int32 [24, 2], P('batch'), may hold values from 12 to 32, as said below
- inproj_weight: float32 [192, 576], P('batch'), may hold values from -0.4375 to 0.4375
- inproj_first: float32 [192, 576], P('batch'), may hold values from -48 to 48
- inproj_second: float32 [192, 576], P('batch'), may hold values from 2.688 to 21.504
- outproj_weight: float32 [192, 192], P('batch'), may hold values from -0.4375 to 0.4375
- outproj_first: float32 [192, 192], P('batch'), may hold values from -96 to 96
- outproj_second: float32 [192, 192], P('batch'), may hold values from 10.752 to 86.016
- expand_weight: float32 [192, 768], P('batch'), may hold values from -0.4375 to 0.4375
- expand_first: float32 [192, 768], P('batch'), may hold values from -24 to 24
- expand_second: float32 [192, 768], P('batch'), may hold values from 0.672 to 5.376
- reduce_weight: float32 [768, 192], P('batch'), may hold values from -0.21875 to 0.21875
- reduce_first: float32 [768, 192], P('batch'), may hold values from -48 to 48
- reduce_second: float32 [768, 192], P('batch'), may hold values from 2.688 to 21.504
- pooling_weight: float32 [3, 9, 192], replicated, may hold values from -2 to 2
- pooling_first: float32 [3, 9, 192], replicated, may hold values from -96 to 96
- pooling_second: float32 [3, 9, 192], replicated, may hold values from 10.752 to 86.016
- relheight_weight: float32 [63, 96], replicated, may hold values from -0.625 to 0.625
- relheight_first: float32 [63, 96], replicated, may hold values from -40 to 40
- relheight_second: float32 [63, 96], replicated, may hold values from 1.72032 to 13.76256
- relwidth_weight: float32 [55, 96], replicated, may hold values from -0.625 to 0.625
- relwidth_first: float32 [55, 96], replicated, may hold values from -40 to 40
- relwidth_second: float32 [55, 96], replicated, may hold values from 1.72032 to 13.76256
- gains_weight: float32 [2, 192], replicated, may hold values from 0.5 to 1.5
- gains_first: float32 [2, 192], replicated, may hold values from -96 to 96
- gains_second: float32 [2, 192], replicated, may hold values from 10.752 to 86.016
- biases_weight: float32 [2112], replicated, may hold values from -0.6 to 0.6
- biases_first: float32 [2112], replicated, may hold values from -80 to 80
- biases_second: float32 [2112], replicated, may hold values from 6.88128 to 55.05024
Outputs:
- output: bfloat16 [24, 32, 28, 192], P('batch', 'height')
- input_grad: float32 [24, 32, 28, 192], P('batch', 'height')
- inproj_new: float32 [192, 576], P('batch')
- inproj_moment: float32 [192, 576], P('batch')
- inproj_square: float32 [192, 576], P('batch')
- inproj_half: bfloat16 [192, 576], P('batch')
- outproj_new: float32 [192, 192], P('batch')
- outproj_moment: float32 [192, 192], P('batch')
- outproj_square: float32 [192, 192], P('batch')
- outproj_half: bfloat16 [192, 192], P('batch')
- expand_new: float32 [192, 768], P('batch')
- expand_moment: float32 [192, 768], P('batch')
- expand_square: float32 [192, 768], P('batch')
- expand_half: bfloat16 [192, 768], P('batch')
- reduce_new: float32 [768, 192], P('batch')
- reduce_moment: float32 [768, 192], P('batch')
- reduce_square: float32 [768, 192], P('batch')
- reduce_half: bfloat16 [768, 192], P('batch')
- pooling_new: float32 [3, 9, 192], replicated
- pooling_moment: float32 [3, 9, 192], replicated
- pooling_square: float32 [3, 9, 192], replicated
- relheight_new: float32 [63, 96], replicated
- relheight_moment: float32 [63, 96], replicated
- relheight_square: float32 [63, 96], replicated
- relwidth_new: float32 [55, 96], replicated
- relwidth_moment: float32 [55, 96], replicated
- relwidth_square: float32 [55, 96], replicated
- gains_new: float32 [2, 192], replicated
- gains_moment: float32 [2, 192], replicated
- gains_square: float32 [2, 192], replicated
- biases_new: float32 [2112], replicated
- biases_moment: float32 [2112], replicated
- biases_square: float32 [2112], replicated
The draws below stay inside these ranges and needn't reach their ends.
Inputs may be any that keep to these rules, and one draw needn't show every extreme that they name: `extent`: column 0 is the image's valid height, at least 12, column 1 its valid width, at least 14; among the 3 images of each index of batch one has the full height 32.
All inputs are finite; a program needn't handle non-finite values.
Results may differ from the reference program's by a relative error of at most 0.012.
The reference program's roundings to bfloat16 on the way count: a program that leaves them out, or rounds other values in their place, can miss the bound.
Values may be sent and summed in bfloat16 or wider, within the bound.
A program may use at most 128 MiB of HBM per device.

```python
import math
import jax
import jax.numpy as jnp
from jax import lax

D = 192
HD = 96
HIDDEN_SIZE = 768
GRID_H = 32
GRID_W = 28
IMG_DEV = 3
STEP = 10
IMAGES = 24
TOKENS = 21504


def draw_extent(key, part):
    key = jax.random.fold_in(key, 7)
    key_one, key_two, key_three = jax.random.split(key, 3)
    heights = jax.random.randint(key_one, (IMAGES,), GRID_H * 3 // 8, GRID_H + 1)
    widths = jax.random.randint(key_two, (IMAGES,), GRID_W // 2, GRID_W + 1)
    full_rows = jax.random.randint(key_three, (IMAGES // IMG_DEV, 1), 0, IMG_DEV)
    slot_index = jnp.arange(IMG_DEV)[None, :]
    heights = jnp.where((slot_index == full_rows).reshape(-1), GRID_H, heights)
    return jnp.stack([heights, widths], axis=1).astype(jnp.int32)


def steps_of(rng, dims, cuts, least, high):
    factor_of, own = 1.0, jax.random.fold_in(rng, 6)
    for axis_at, blocks in cuts:
        draws = jnp.exp(jax.random.uniform(jax.random.fold_in(own, axis_at), (blocks,), jnp.float32, least / len(cuts), high / len(cuts)))
        factor_of = factor_of * jnp.repeat(draws, dims[axis_at] // blocks).reshape([-1 if axis == axis_at else 1 for axis in range(len(dims))])
    return factor_of


def centred(key, shape, deviation, reach, shards=(), dtype=jnp.bfloat16):
    level = steps_of(key, shape, shards, -0.22, 0.18) if shards else 1.0
    values = jax.random.normal(key, shape, jnp.float32) * deviation * level
    return jnp.minimum(jnp.maximum(values, -reach), reach).astype(dtype)


def setup_inputs(seed: int = 0) -> dict:
    key_list = jax.random.split(jax.random.key(seed), 31)
    activations = centred(key_list[0], (IMAGES, GRID_H, GRID_W, D), 1.0, 6.0, ((0, 8), (1, 4)))
    cotangent = centred(key_list[1], (IMAGES, GRID_H, GRID_W, D), 1.0, 6.0, ((0, 8), (1, 4)))
    extent = draw_extent(jax.random.fold_in(key_list[30], 71), 0)
    inproj_weight = centred(key_list[3], (D, 3 * D), D ** -0.5, 0.4375, ((0, 8),), jnp.float32)
    inproj_first = centred(key_list[4], (D, 3 * D), (0.055 * TOKENS ** 0.5), 48.0, ((0, 8),), jnp.float32)
    inproj_second = jnp.clip(jnp.exp(math.log(21.504) - 2.0794415 * jax.random.uniform(key_list[5], (D, 3 * D), jnp.float32) ** steps_of(key_list[5], (D, 3 * D), ((0, 8),), -0.2, 0.2)), 2.688, 21.504)
    outproj_weight = centred(key_list[6], (D, D), D ** -0.5, 0.4375, ((0, 8),), jnp.float32)
    outproj_first = centred(key_list[7], (D, D), (0.11 * TOKENS ** 0.5), 96.0, ((0, 8),), jnp.float32)
    outproj_second = jnp.clip(jnp.exp(math.log(86.016) - 2.0794415 * jax.random.uniform(key_list[8], (D, D), jnp.float32) ** steps_of(key_list[8], (D, D), ((0, 8),), -0.2, 0.2)), 10.752, 86.016)
    expand_weight = centred(key_list[9], (D, HIDDEN_SIZE), D ** -0.5, 0.4375, ((0, 8),), jnp.float32)
    expand_first = centred(key_list[10], (D, HIDDEN_SIZE), (0.0275 * TOKENS ** 0.5), 24.0, ((0, 8),), jnp.float32)
    expand_second = jnp.clip(jnp.exp(math.log(5.376) - 2.0794415 * jax.random.uniform(key_list[11], (D, HIDDEN_SIZE), jnp.float32) ** steps_of(key_list[11], (D, HIDDEN_SIZE), ((0, 8),), -0.2, 0.2)), 0.672, 5.376)
    reduce_weight = centred(key_list[12], (HIDDEN_SIZE, D), HIDDEN_SIZE ** -0.5, 0.21875, ((0, 8),), jnp.float32)
    reduce_first = centred(key_list[13], (HIDDEN_SIZE, D), (0.055 * TOKENS ** 0.5), 48.0, ((0, 8),), jnp.float32)
    reduce_second = jnp.clip(jnp.exp(math.log(21.504) - 2.0794415 * jax.random.uniform(key_list[14], (HIDDEN_SIZE, D), jnp.float32) ** steps_of(key_list[14], (HIDDEN_SIZE, D), ((0, 8),), -0.2, 0.2)), 2.688, 21.504)
    pooling_weight = centred(key_list[15], (3, 9, D), 9 ** -0.5, 2.0, (), jnp.float32)
    pooling_first = centred(key_list[16], (3, 9, D), (0.11 * TOKENS ** 0.5), 96.0, (), jnp.float32)
    pooling_second = jnp.clip(jnp.exp(jax.random.uniform(key_list[17], (3, 9, D), jnp.float32, math.log(10.752), math.log(86.016))), 10.752, 86.016)
    relheight_weight = centred(key_list[18], (2 * GRID_H - 1, HD), HD ** -0.5, 0.625, (), jnp.float32)
    relheight_first = centred(key_list[19], (2 * GRID_H - 1, HD), (0.044 * TOKENS ** 0.5), 40.0, (), jnp.float32)
    relheight_second = jnp.clip(jnp.exp(jax.random.uniform(key_list[20], (2 * GRID_H - 1, HD), jnp.float32, math.log(1.72032), math.log(13.76256))), 1.72032, 13.76256)
    relwidth_weight = centred(key_list[21], (2 * GRID_W - 1, HD), HD ** -0.5, 0.625, (), jnp.float32)
    relwidth_first = centred(key_list[22], (2 * GRID_W - 1, HD), (0.044 * TOKENS ** 0.5), 40.0, (), jnp.float32)
    relwidth_second = jnp.clip(jnp.exp(jax.random.uniform(key_list[23], (2 * GRID_W - 1, HD), jnp.float32, math.log(1.72032), math.log(13.76256))), 1.72032, 13.76256)
    gains_weight = jnp.clip(1.0 + 0.1 * jax.random.normal(key_list[24], (2, D), jnp.float32), 0.5, 1.5)
    gains_first = centred(key_list[25], (2, D), (0.11 * TOKENS ** 0.5), 96.0, (), jnp.float32)
    gains_second = jnp.clip(jnp.exp(jax.random.uniform(key_list[26], (2, D), jnp.float32, math.log(10.752), math.log(86.016))), 10.752, 86.016)
    biases_weight = centred(key_list[27], (7 * D + HIDDEN_SIZE,), 0.1, 0.6, (), jnp.float32)
    biases_first = centred(key_list[28], (7 * D + HIDDEN_SIZE,), (0.088 * TOKENS ** 0.5), 80.0, (), jnp.float32)
    biases_second = jnp.clip(jnp.exp(jax.random.uniform(key_list[29], (7 * D + HIDDEN_SIZE,), jnp.float32, math.log(6.88128), math.log(55.05024))), 6.88128, 55.05024)
    return {"activations": activations, "cotangent": cotangent, "extent": extent, "inproj_weight": inproj_weight, "inproj_first": inproj_first, "inproj_second": inproj_second, "outproj_weight": outproj_weight, "outproj_first": outproj_first, "outproj_second": outproj_second, "expand_weight": expand_weight, "expand_first": expand_first, "expand_second": expand_second, "reduce_weight": reduce_weight, "reduce_first": reduce_first, "reduce_second": reduce_second, "pooling_weight": pooling_weight, "pooling_first": pooling_first, "pooling_second": pooling_second, "relheight_weight": relheight_weight, "relheight_first": relheight_first, "relheight_second": relheight_second, "relwidth_weight": relwidth_weight, "relwidth_first": relwidth_first, "relwidth_second": relwidth_second, "gains_weight": gains_weight, "gains_first": gains_first, "gains_second": gains_second, "biases_weight": biases_weight, "biases_first": biases_first, "biases_second": biases_second}


@jax.custom_vjp
def low(v):
    return lax.optimization_barrier(v.astype(jnp.bfloat16)).astype(jnp.float32)

@jax.custom_vjp
def low_back(v):
    return v

def low_keep(v):
    return (low(v), None)

def low_pass(kept, grad):
    return (grad,)

def back_keep(v):
    return (v, None)

def back_low(kept, grad):
    return (low(grad),)
low.defvjp(low_keep, low_pass)
low_back.defvjp(back_keep, back_low)
highest = lax.Precision.HIGHEST
norm_eps = 1e-06
beta_one = 0.9
beta_two = 0.999
adam_eps = 1e-08
masked_value = -1000000000.0
step_rates = (0.04, 0.04, 0.04, 0.04, 0.2, 0.1, 0.1, 0.5, 0.1)
decay_rates = (0.05, 0.05, 0.05, 0.05, 0.05, 0.05, 0.05, 0.0, 0.0)

def layer_norm(values, gain_vec, shift_vec):
    centered = values - lax.optimization_barrier(jnp.mean(values, axis=-1, keepdims=True))
    variance = lax.optimization_barrier(jnp.mean(centered * centered, axis=-1, keepdims=True))
    return centered * lax.rsqrt(variance + norm_eps) * gain_vec + shift_vec

def matmul(left_side, right_side):
    return jnp.einsum('...i,ij->...j', left_side, right_side, precision=highest)

def full_pool(field, kernel, stride):
    row_total = field.shape[1]
    col_total = field.shape[2]
    padded = jnp.pad(field, ((0, 0), (1, 1), (1, 1), (0, 0)))
    result = 0.0
    for row_off in range(3):
        for col_off in range(3):
            result = result + kernel[3 * row_off + col_off] * padded[:, row_off:row_off + row_total:stride, col_off:col_off + col_total:stride]
    return result

def block_forward(inputs, params, token_mask, key_mask):
    inproj, outproj, expand, reduce_mat, pooling, relheight, relwidth, gains, biases = params
    images, row_total, col_total, channels = inputs.shape
    hidden_units = expand.shape[1]
    head_size = relheight.shape[1]
    head_count = channels // head_size
    key_rows = row_total // 2
    key_cols = col_total // 2
    first_shift = biases[:channels]
    second_shift = biases[channels:2 * channels]
    inproj_bias = biases[2 * channels:5 * channels]
    outproj_bias = biases[5 * channels:6 * channels]
    expand_bias = biases[6 * channels:6 * channels + hidden_units]
    reduce_bias = biases[6 * channels + hidden_units:]
    normed = layer_norm(inputs, gains[0], first_shift)
    projected = low_back(matmul(low(normed), low(inproj)) + inproj_bias) * token_mask[..., None]
    query_pool = full_pool(projected[..., :channels], pooling[0], 1)
    key_pool = full_pool(projected[..., channels:2 * channels], pooling[1], 2)
    value_pool = full_pool(projected[..., 2 * channels:], pooling[2], 2)
    query_heads = low(query_pool).reshape(images, row_total, col_total, head_count, head_size)
    key_heads = low(key_pool).reshape(images, key_rows, key_cols, head_count, head_size)
    value_keys = low(value_pool).reshape(images, key_rows * key_cols, head_count, head_size)
    row_dist = (jnp.arange(row_total)[:, None] - 2 * jnp.arange(key_rows)[None, :] + 2 * (key_rows - 1)).astype(jnp.int32)
    col_dist = (jnp.arange(col_total)[:, None] - 2 * jnp.arange(key_cols)[None, :] + 2 * (key_cols - 1)).astype(jnp.int32)
    height_table = low(relheight)[row_dist]
    width_table = low(relwidth)[col_dist]
    content = jnp.einsum('nyxhc,nuvhc->nhyxuv', query_heads, key_heads, precision=highest)
    along_rows = jnp.einsum('nyxhc,yuc->nhyxu', query_heads, height_table, precision=highest)
    along_cols = jnp.einsum('nyxhc,xvc->nhyxv', query_heads, width_table, precision=highest)
    scores = low_back(head_size ** (-0.5) * content + along_rows[..., None] + along_cols[..., None, :])
    scores = jnp.where(key_mask[:, None, None, None], scores, masked_value)
    flat_scores = scores.reshape(images, head_count, row_total, col_total, key_rows * key_cols)
    peak_score = lax.optimization_barrier(jnp.max(flat_scores, axis=-1, keepdims=True))
    raised = jnp.exp(flat_scores - peak_score)
    attn_probs = raised / lax.optimization_barrier(jnp.sum(raised, axis=-1, keepdims=True))
    mixed = jnp.einsum('nhyxk,nkhc->nyxhc', low(attn_probs), value_keys, precision=highest).reshape(images, row_total, col_total, channels) + query_pool
    attn_out = low_back(matmul(low(low_back(mixed)), low(outproj)) + outproj_bias)
    middle = inputs + attn_out
    second = layer_norm(middle, gains[1], second_shift)
    expanded = low_back(matmul(low(second), low(expand)) + expand_bias)
    reduced = low_back(matmul(low(jax.nn.gelu(expanded, approximate=False)), low(reduce_mat)) + reduce_bias)
    return token_mask[..., None] * (middle + reduced)

def adam_step(weight, first_state, second_state, gradient, step_rate, decay_rate):
    moment = beta_one * first_state + (1.0 - beta_one) * gradient
    square = beta_two * second_state + (1.0 - beta_two) * gradient * gradient
    unbiased = moment / (1.0 - beta_one ** STEP)
    scaled = square / (1.0 - beta_two ** STEP)
    updated = weight * (1.0 - step_rate * decay_rate) - step_rate * unbiased / (jnp.sqrt(scaled) + adam_eps)
    return (updated, moment, square)

def reference(activations, cotangent, extent, inproj_weight, inproj_first, inproj_second, outproj_weight, outproj_first, outproj_second, expand_weight, expand_first, expand_second, reduce_weight, reduce_first, reduce_second, pooling_weight, pooling_first, pooling_second, relheight_weight, relheight_first, relheight_second, relwidth_weight, relwidth_first, relwidth_second, gains_weight, gains_first, gains_second, biases_weight, biases_first, biases_second):
    weights = (inproj_weight, outproj_weight, expand_weight, reduce_weight, pooling_weight, relheight_weight, relwidth_weight, gains_weight, biases_weight)
    firsts = (inproj_first, outproj_first, expand_first, reduce_first, pooling_first, relheight_first, relwidth_first, gains_first, biases_first)
    seconds = (inproj_second, outproj_second, expand_second, reduce_second, pooling_second, relheight_second, relwidth_second, gains_second, biases_second)
    images, row_total, col_total, channels = activations.shape
    group_size = math.gcd(images, 4)
    group_count = images // group_size

    def scan_step(running, pieces):
        inputs, upstream, bounds = pieces
        token_mask = ((jnp.arange(row_total)[None, :, None] < bounds[:, 0, None, None]) & (jnp.arange(col_total)[None, None, :] < bounds[:, 1, None, None])).astype(jnp.float32)
        key_mask = (2 * jnp.arange(row_total // 2)[None, :, None] < bounds[:, 0, None, None]) & (2 * jnp.arange(col_total // 2)[None, None, :] < bounds[:, 1, None, None])
        result, pullback = jax.vjp(lambda values, params: block_forward(values, params, token_mask, key_mask), inputs.astype(jnp.float32), weights)
        input_part, weight_grads = pullback(upstream.astype(jnp.float32))
        running = tuple((total_grad + new_grad for total_grad, new_grad in zip(running, weight_grads)))
        return (running, (result.astype(jnp.bfloat16), input_part))
    grouped = (activations.reshape(group_count, group_size, row_total, col_total, channels), cotangent.reshape(group_count, group_size, row_total, col_total, channels), extent.reshape(group_count, group_size, 2))
    start = tuple((jnp.zeros(weight.shape, jnp.float32) for weight in weights))
    summed, (outputs, input_grads) = lax.scan(scan_step, start, grouped)
    output = outputs.reshape(images, row_total, col_total, channels)
    input_grad = input_grads.reshape(images, row_total, col_total, channels)
    fresh = [adam_step(weights[index], firsts[index], seconds[index], summed[index], step_rates[index], decay_rates[index]) for index in range(9)]
    return (output, input_grad, fresh[0][0], fresh[0][1], fresh[0][2], fresh[0][0].astype(jnp.bfloat16), fresh[1][0], fresh[1][1], fresh[1][2], fresh[1][0].astype(jnp.bfloat16), fresh[2][0], fresh[2][1], fresh[2][2], fresh[2][0].astype(jnp.bfloat16), fresh[3][0], fresh[3][1], fresh[3][2], fresh[3][0].astype(jnp.bfloat16), fresh[4][0], fresh[4][1], fresh[4][2], fresh[5][0], fresh[5][1], fresh[5][2], fresh[6][0], fresh[6][1], fresh[6][2], fresh[7][0], fresh[7][1], fresh[7][2], fresh[8][0], fresh[8][1], fresh[8][2])
```

```python
import functools
import types

import jax
import jax.numpy as jnp
from jax import lax
from jax.experimental import pallas as pl
from jax.experimental.pallas import tpu as pltpu
from jax.sharding import PartitionSpec as P

STEP = 10
MESH = pl.DeviceIdType.MESH
f32 = jnp.float32
bf16 = jnp.bfloat16

norm_eps = 1e-06
beta_one = 0.9
beta_two = 0.999
adam_eps = 1e-08
masked_value = -1000000000.0
step_rates = (0.04, 0.04, 0.04, 0.04, 0.2, 0.1, 0.1, 0.5, 0.1)
decay_rates = (0.05, 0.05, 0.05, 0.05, 0.05, 0.05, 0.05, 0.0, 0.0)

IMG, R, C, D, HD, HID = 3, 8, 28, 192, 96, 768
T = R * C
TX = T + 2 * R
HG = 4
KR, KC, KCP = R * HG // 2, C // 2, 16
KL = R // 2
KEYS = KR * KCP
SCALE = HD ** (-0.5)
KROWS = (KL + 1) * KCP
HX = 32
PE = HID + 4 * D + 2 * 128
PI = 3 * D


def nn(a, b):
    return lax.dot_general(a, b, (((1,), (0,)), ((), ())), preferred_element_type=f32)


def nt(a, b):
    return lax.dot_general(a, b, (((1,), (1,)), ((), ())), preferred_element_type=f32)


def tn(a, b):
    return lax.dot_general(a, b, (((0,), (0,)), ((), ())), preferred_element_type=f32)


def iota(shape, axis):
    return lax.broadcasted_iota(jnp.int32, shape, axis)


def rolled(x, by):
    return pltpu.roll(x, by % x.shape[0], 0)


def halves(x, axis):
    high = x.astype(bf16)
    return jnp.concatenate([high, (x - high.astype(f32)).astype(bf16)], axis=axis)


def normalise(x):
    mean = jnp.sum(x, axis=1, keepdims=True) * (1.0 / D)
    centered = x - mean
    inverse = lax.rsqrt(jnp.sum(centered * centered, axis=1, keepdims=True) * (1.0 / D) + norm_eps)
    return centered * inverse, inverse


def normalise_back(grad, gain, hat, inverse):
    scaled = grad * gain
    one = jnp.sum(scaled, axis=1, keepdims=True) * (1.0 / D)
    two = jnp.sum(scaled * hat, axis=1, keepdims=True) * (1.0 / D)
    return inverse * (scaled - one - hat * two)


def folded(x):
    return jnp.sum(x.reshape(x.shape[0] // 8, 8, x.shape[1]), axis=0)


def main_kernel(B, tree, *refs):
    r = types.SimpleNamespace(**jax.tree.unflatten(tree, refs))
    me = lax.axis_index("batch")
    hh = lax.axis_index("height")
    QB = B // HG
    rows = r.w_in.shape[0]

    def loop(first, last, body):
        def step(i, carry):
            body(i)
            return carry

        lax.fori_loop(first, last, step, 0)

    def next_batch(k):
        return lax.rem(me + k, B)

    def next_height(k):
        return lax.rem(hh + k, HG)

    local = [
        (r.act, r.v_act),
        (r.w_in, r.v_in),
        (r.w_out, r.v_out),
        (r.w_exp, r.v_exp),
        (r.w_red, r.v_red),
        (r.pool, r.v_pool),
        (r.relh, r.v_relh),
        (r.relw, r.v_relw),
        (r.gains, r.v_gains),
        (r.biases, r.v_biases.at[0]),
        (r.cot, r.v_cot),
    ]
    local = [pltpu.make_async_copy(a, b, r.s_local.at[k]) for k, (a, b) in enumerate(local)]
    for copy in local:
        copy.start()

    barrier = pltpu.get_barrier_semaphore()

    def greet_batch(k):
        pl.semaphore_signal(barrier, inc=1, device_id=(next_batch(k), hh), device_id_type=MESH)

    loop(1, B, greet_batch)
    for k in range(1, HG):
        pl.semaphore_signal(barrier, inc=1, device_id=(me, next_height(k)), device_id_type=MESH)

    def to_batch(src, dst, send, recv, b):
        return pltpu.make_async_remote_copy(
            src_ref=src, dst_ref=dst, send_sem=send, recv_sem=recv, device_id=(b, hh), device_id_type=MESH
        )

    def to_height(src, dst, send, recv, h):
        return pltpu.make_async_remote_copy(
            src_ref=src, dst_ref=dst, send_sem=send, recv_sem=recv, device_id=(me, h), device_id_type=MESH
        )

    def weight_copy(i, k):
        slot = r.g[i].at[me]
        return to_batch(slot, slot, r.s_wsend.at[i, k], r.s_wrecv.at[i, me], next_batch(k))

    def weight_arrival(i, k):
        b = next_batch(k)
        slot = r.g[i].at[b]
        return to_batch(slot, slot, r.s_wsend.at[i, k], r.s_wrecv.at[i, b], b)

    local[0].wait()
    local[1].wait()
    r.g[0][me] = r.v_in[...].astype(bf16)

    edge_rows = iota((2 * HX, T), 0)
    edge_cols = iota((2 * HX, T), 1)
    edges = (edge_cols == (edge_rows % HX) * R + (edge_rows // HX) * (R - 1)).astype(bf16)
    for n in range(IMG):
        outer = nn(edges, r.v_act[n]).astype(bf16)
        r.hs[0, n] = outer[:HX]
        r.hs[1, n] = outer[HX:]
    above, below = next_height(HG - 1), next_height(1)
    halo_up = to_height(r.hs.at[0], r.hr.at[1], r.s_hsend.at[0], r.s_hrecv.at[0], above)
    halo_down = to_height(r.hs.at[1], r.hr.at[0], r.s_hsend.at[1], r.s_hrecv.at[1], below)

    pl.semaphore_wait(barrier, B - 1 + HG - 1)
    loop(1, B, lambda k: weight_copy(0, k).start())
    halo_up.start()
    halo_down.start()
    for k in (2, 3, 4):
        local[k].wait()
    mine = r.g[1].at[me]
    mine[:, :HID] = r.v_exp[...].astype(bf16)
    for i in range(4):
        mine[:, HID + D * i : HID + D * (i + 1)] = r.v_red[rows * i : rows * (i + 1)].astype(bf16)
    mine[:, HID + 4 * D :] = jnp.concatenate(
        [r.v_out[...], jnp.zeros((rows, PE - HID - 5 * D), f32)], axis=1
    ).astype(bf16)
    loop(1, B, lambda k: weight_copy(1, k).start())

    for k in range(5, 11):
        local[k].wait()
    poolq, poolkv, table = r.poolq, r.poolkv, r.table
    poolq[...] = r.v_pool[:, 0, :]
    poolkv[:, :D] = r.v_pool[:, 1, :]
    poolkv[:, D:] = r.v_pool[:, 2, :]
    r.tablef[...] = jnp.zeros_like(r.tablef)
    relh_rows, relw_rows = r.v_relh.shape[0], r.v_relw.shape[0]
    for hd in range(2):
        r.tablef[128 * hd : 128 * hd + relh_rows, HD * hd : HD * (hd + 1)] = r.v_relh[...]
        r.tablef[128 * hd + 64 : 128 * hd + 64 + relw_rows, HD * hd : HD * (hd + 1)] = r.v_relw[...]
    table[...] = r.tablef[...].astype(bf16)
    shift_one = r.v_biases[0:1, 0:D]
    shift_two = r.v_biases[0:1, D : 2 * D]
    bias_q = r.v_biases[0:1, 2 * D : 3 * D]
    bias_kv = r.v_biases[0:1, 3 * D : 5 * D]
    bias_out = r.v_biases[0:1, 5 * D : 6 * D]
    bias_exp = r.v_biases[0:1, 6 * D : 6 * D + HID]
    bias_red = r.v_biases[0:1, 6 * D + HID : 7 * D + HID]
    gain_one = r.v_gains[0:1, :]
    gain_two = r.v_gains[1:2, :]
    acc, paccq, pacckv = r.acc, r.paccq, r.pacckv
    acc[...] = jnp.zeros_like(acc)
    paccq[...] = jnp.zeros_like(paccq)
    pacckv[...] = jnp.zeros_like(pacckv)
    kvx, qx, dqx = r.kvx, r.qx, r.dqx

    cell = iota((T, 1), 0)
    cell_y, cell_x = hh * R + cell % R, cell // R
    halo_at = iota((2 * IMG * HX, 1), 0)

    def cell_mask(n):
        return ((cell_y < r.extent[0, n]) & (cell_x < r.extent[1, n])).astype(f32)

    def first_norm(n):
        hat, inverse = normalise(r.v_act[n].astype(f32))
        r.ne[n] = (hat * gain_one + shift_one).astype(bf16)
        r.hat_one[n] = hat
        r.inv_one[n] = inverse
        kvx[n, 0:R, :] = jnp.zeros((R, 2 * D), f32)
        kvx[n, T + R :, :] = jnp.zeros((R, 2 * D), f32)
        for x in (qx, dqx):
            x[n, 0:R, :] = jnp.zeros((R, D), f32)
            x[n, T + R :, :] = jnp.zeros((R, D), f32)

    loop(0, IMG, first_norm)

    spread_rows = iota((T, 2 * HX), 0)
    spread_cols = iota((T, 2 * HX), 1)
    spread = (
        (spread_rows // R == spread_cols % HX) & (spread_rows % R == (spread_cols // HX) * (R - 1))
    ).astype(bf16)
    r.spread[...] = jnp.concatenate([spread, spread], axis=1)
    pick_rows = iota((KL * KCP, T // 2), 0)
    pick_cols = iota((KL * KCP, T // 2), 1)
    pick = (
        (pick_rows % KCP == pick_cols // R) & (pick_cols % R == 2 * (pick_rows // KCP))
    ).astype(bf16)
    r.pick[...] = jnp.concatenate([pick, pick], axis=1)
    back_rows = iota((3 * T // 2, KROWS), 0)
    back_cols = iota((3 * T // 2, KROWS), 1)
    back_tap, back_cell = back_rows // (T // 2), back_rows % (T // 2)
    unpick = (
        (back_cols % KCP == back_cell // R)
        & (back_cell % R == 2 * (back_cols // KCP) + back_tap - 1)
    ).astype(bf16)
    r.unpick[...] = jnp.concatenate([unpick, unpick], axis=1)
    key_rows = iota((KEYS, 64), 0)
    key_lane = iota((KEYS, 64), 1) % 32
    r.hot[...] = (
        (key_lane == key_rows // KCP) | (key_lane == KR + key_rows % KCP)
    ).astype(bf16)
    halo_up.wait_recv()
    halo_down.wait_recv()
    hat, _ = normalise(r.hr[...].reshape(2 * IMG * HX, D).astype(f32))
    r.nh[...] = (hat * gain_one + shift_one).astype(bf16)

    halo_y = jnp.where(halo_at < IMG * HX, hh * R - 1, hh * R + R)
    halo_image = halo_at // HX % IMG
    halo_ok = jnp.zeros((2 * IMG * HX, 1), jnp.bool_)
    for n in range(IMG):
        halo_ok = halo_ok | (
            (halo_image == n)
            & (halo_y >= 0)
            & (halo_y < r.extent[0, n])
            & (halo_at % HX < r.extent[1, n])
        )
    halo_ok = halo_ok.astype(f32)

    loop(1, B, lambda k: weight_arrival(0, k).wait_recv())
    wq, wkv, wout, wexp, wred = r.wq, r.wkv, r.wout, r.wexp, r.wred
    for b in range(B):
        shard = r.g[0][b].astype(f32)
        r.f_q[rows * b : rows * (b + 1), :] = shard[:, :D]
        r.f_kv[rows * b : rows * (b + 1), :] = shard[:, D:]
    wq[...] = r.f_q[...].astype(bf16)
    wkv[...] = r.f_kv[...].astype(bf16)

    kvg = r.kvg

    def kv_copy(n, k, source, target):
        slot = kvg.at[source, n]
        return to_height(slot, slot, r.s_ksend.at[n, k - 1], r.s_krecv.at[n, k - 1], target)

    half = IMG * HX
    r.halo_kv[...] = (nn(r.nh[:half], wkv[...]) + bias_kv) * halo_ok[:half]

    def columns(x, b):
        pairs = x.reshape(TX // (2 * R), 2 * R, x.shape[1])
        side = pairs[b // 2 : b // 2 + KC, R * (b % 2) : R * (b % 2) + R]
        return side.reshape(T // 2, x.shape[1])

    def keys_values(n):
        kvx[n, R : R + T, :] = (nn(r.ne[n], wkv[...]) + bias_kv) * cell_mask(n)
        field = kvx[n]
        sides = [columns(field, b) for b in range(3)]
        sums = [sum(poolkv[3 * a + b : 3 * a + b + 1, :] * sides[b] for b in range(3)) for a in range(3)]
        pooled = rolled(sums[0], 1) * (iota((T // 2, 1), 0) % R > 0).astype(f32) + sums[1] + rolled(sums[2], -1)
        edge = r.halo_kv[pl.ds(pl.multiple_of(n * HX, HX), HX), :]
        edge = (
            poolkv[0:1, :] * rolled(edge, 1) + poolkv[1:2, :] * edge + poolkv[2:3, :] * rolled(edge, -1)
        )
        edge_pick = (iota((KCP, HX), 1) == 2 * iota((KCP, HX), 0)).astype(bf16)
        edge = nn(jnp.concatenate([edge_pick, edge_pick], axis=1), halves(edge, 0))
        whole = nn(r.pick[...], halves(pooled, 0))
        kvg[hh, n] = jnp.concatenate([whole[:KCP] + edge, whole[KCP:]], axis=0).astype(bf16)
        for k in range(1, HG):
            kv_copy(n, k, hh, next_height(k)).start()

    loop(0, IMG, keys_values)

    qp, qa = r.qp, r.qa
    r.halo_q[...] = (nn(r.nh[...], wq[...]) + bias_q) * halo_ok
    lane = iota((T, 128), 1)
    y_at = hh * R + iota((T, 128), 0) % R
    x_at = iota((T, 128), 0) // R
    aux = lane % 32
    spot = jnp.where(aux < KR, y_at - 2 * aux + 2 * (KR - 1), 64 + x_at - 2 * (aux - KR) + 2 * (KC - 1))
    inner_top = (cell % R > 0).astype(f32)
    inner_low = (cell % R < R - 1).astype(f32)

    def beside(x):
        return [rolled(x, 1), x, rolled(x, -1)]

    def queries(n):
        qx[n, R : R + T, :] = (nn(r.ne[n], wq[...]) + bias_q) * cell_mask(n)
        field = qx[n]
        sums = [
            sum(poolq[3 * a + b : 3 * a + b + 1, :] * field[R * b : R * b + T] for b in range(3))
            for a in range(3)
        ]
        top = beside(r.halo_q[pl.ds(pl.multiple_of(n * HX, HX), HX), :])
        low = beside(r.halo_q[pl.ds(pl.multiple_of((IMG + n) * HX, HX), HX), :])
        top = sum(poolq[b : b + 1, :] * top[b] for b in range(3))
        low = sum(poolq[6 + b : 7 + b, :] * low[b] for b in range(3))
        edge = nn(r.spread[...], halves(jnp.concatenate([top, low], axis=0), 0))
        pooled = rolled(sums[0], 1) * inner_top + sums[1] + rolled(sums[2], -1) * inner_low + edge
        qp[n] = pooled
        query = pooled.astype(bf16)
        r.qh[n] = query
        along = nt(query, table[...])
        left, right = pooled[:, :128], pooled[:, 128:]
        right = jnp.concatenate([right, right], axis=1)
        for hd in range(2):
            near = along[:, 128 * hd : 128 * (hd + 1)]
            near = jnp.take_along_axis(near, spot, axis=1, mode="promise_in_bounds") * (HD**0.5)
            rest = near - near.astype(bf16).astype(f32)
            near = jnp.where(lane < 96, near, rest)
            if hd == 0:
                qa[n, hd, :, :128] = jnp.where(lane < HD, left, 0.0).astype(bf16)
                qa[n, hd, :, 128:] = jnp.where(lane < 64, 0.0, near).astype(bf16)
            else:
                qa[n, hd, :, :128] = jnp.where(lane < HD, 0.0, left).astype(bf16)
                qa[n, hd, :, 128:] = jnp.where(lane < 64, right, near).astype(bf16)

    loop(0, IMG, queries)

    key_at = iota((KEYS, 1), 0)
    probs, mxh = r.probs, r.mxh

    def attention(n):
        for k in range(1, HG):
            kv_copy(n, k, next_height(HG - k), hh).wait_recv()
        both = jnp.concatenate([kvg[s, n] for s in range(HG)], axis=0)
        r.ka[n, :, :D] = both[:, :D]
        r.ka[n, :, D:] = r.hot[...]
        r.va[n] = both[:, D:]
        valid = (2 * (key_at // KCP) < r.extent[0, n]) & (2 * (key_at % KCP) < r.extent[1, n])
        value = r.va[n].T
        mixed = []
        for hd in range(2):
            scores = nt(r.ka[n], qa[n, hd]) * SCALE
            scores = jnp.where(valid, scores, masked_value)
            raised = jnp.exp(scores - jnp.max(scores, axis=0, keepdims=True))
            prob = raised * (1.0 / jnp.sum(raised, axis=0, keepdims=True))
            probs[n, hd] = prob
            mixed.append(nn(value[HD * hd : HD * (hd + 1)], prob.astype(bf16)))
        mxh[n] = (jnp.concatenate(mixed, axis=0).T + qp[n]).astype(bf16)

    loop(0, IMG, attention)

    loop(1, B, lambda k: weight_arrival(1, k).wait_recv())
    for b in range(B):
        shard = r.g[1][b].astype(f32)
        r.f_exp[rows * b : rows * (b + 1), :] = shard[:, :HID]
        for i in range(4):
            at = 4 * rows * b + rows * i
            r.f_red[at : at + rows, :] = shard[:, HID + D * i : HID + D * (i + 1)]
        r.f_out[rows * b : rows * (b + 1), :] = shard[:, HID + 4 * D : HID + 5 * D]
    wout[...] = r.f_out[...].astype(bf16)
    wexp[...] = r.f_exp[...].astype(bf16)
    wred[...] = r.f_red[...].astype(bf16)

    def feed_forward(n):
        mask = cell_mask(n)
        middle = r.v_act[n].astype(f32) + nn(mxh[n], wout[...]) + bias_out
        hat, inverse = normalise(middle)
        second = (hat * gain_two + shift_two).astype(bf16)
        r.sh[n] = second
        expanded = nn(second, wexp[...]) + bias_exp
        half_erf = 0.5 + 0.5 * lax.erf(expanded * (0.5**0.5))
        activated = (expanded * half_erf).astype(bf16)
        slope = half_erf + expanded * jnp.exp(expanded * expanded * -0.5) * 0.3989422804014327
        r.ac[n] = activated
        r.v_res[n] = (mask * (middle + nn(activated, wred[...]) + bias_red)).astype(bf16)
        upstream = r.v_cot[n].astype(f32) * mask
        up_half = upstream.astype(bf16)
        r.uh[n] = up_half
        expanded_grad = (nt(up_half, wred[...]) * slope).astype(bf16)
        r.eg[n] = expanded_grad
        second_grad = nt(expanded_grad, wexp[...])
        acc[0:1, 2 * D : 3 * D] += jnp.sum(second_grad * hat, axis=0, keepdims=True)
        acc[0:1, 3 * D : 4 * D] += jnp.sum(second_grad, axis=0, keepdims=True)
        middle_grad = upstream + normalise_back(second_grad, gain_two, hat, inverse)
        r.mgd[n] = middle_grad
        attn_grad = middle_grad.astype(bf16)
        r.ag[n] = attn_grad
        r.mg[n] = nt(attn_grad, wout[...]).astype(bf16)

    loop(0, IMG, feed_forward)
    result_out = pltpu.make_async_copy(r.v_res, r.o_res, r.s_out.at[0])
    result_out.start()

    ones = jnp.ones((16, IMG * T), bf16)

    def flat(ref):
        return ref[...].reshape(IMG * T, ref.shape[-1])

    r.f_exp[...] = tn(flat(r.sh), flat(r.eg))
    acc[2:3, :] = nn(ones, flat(r.eg))[0:1]
    r.f_red[...] = tn(flat(r.uh), flat(r.ac)).T
    acc[1:2, D : 2 * D] = nn(ones, flat(r.uh))[0:1]
    r.f_out[...] = tn(flat(mxh), flat(r.ag))
    acc[1:2, 0:D] = nn(ones, flat(r.ag))[0:1]
    for b in range(B):
        r.d[1][b, :, :HID] = r.f_exp[rows * b : rows * (b + 1), :].astype(bf16)
        for i in range(4):
            at = 4 * rows * b + rows * i
            r.d[1][b, :, HID + D * i : HID + D * (i + 1)] = r.f_red[at : at + rows, :].astype(bf16)
        r.d[1][b, :, HID + 4 * D :] = jnp.concatenate(
            [r.f_out[rows * b : rows * (b + 1), :], jnp.zeros((rows, PE - HID - 5 * D), f32)], axis=1
        ).astype(bf16)

    def one_copy(i, k, target):
        return to_height(
            r.d[i].at[pl.ds(target * QB, QB)],
            r.p[i].at[k - 1],
            r.s_onesend.at[i, k - 1],
            r.s_onerecv.at[i, k - 1],
            target,
        )

    for k in range(1, HG):
        one_copy(1, k, next_height(k)).start()

    dkv = r.dkv
    y_lane = jnp.where(lane < 64, y_at + 2 * (KR - 1) - lane, x_at + 2 * (KC - 1) - (lane - 64))
    back_at = y_lane // 2
    back_ok = (y_lane >= 0) & (y_lane % 2 == 0) & (back_at < jnp.where(lane < 64, KR, KC))
    back_spot = jnp.where(back_ok, back_at + jnp.where(lane < 64, 64, 64 + KR), 0)
    back_ok = back_ok.astype(f32)

    def dkv_copy(n, k, target):
        return to_height(
            dkv.at[n, pl.ds(pl.multiple_of(target * (KL * KCP), KL * KCP), KROWS), :],
            r.dkvr.at[k - 1, n],
            r.s_dsend.at[n, k - 1],
            r.s_drecv.at[n, k - 1],
            target,
        )

    def attention_back(n):
        value = r.va[n]
        keys = r.ka[n].T
        mixed_grad = r.mg[n].astype(f32)
        query = r.qh[n].astype(f32)
        head = iota((T, D), 1) < HD
        probs_half, grads_half, dq, along = [], [], [], []
        mixed_heads = [jnp.where(head, mixed_grad, 0.0), jnp.where(head, 0.0, mixed_grad)]
        mixed_heads = [x.astype(bf16) for x in mixed_heads]
        query_heads = [jnp.where(head, query, 0.0), jnp.where(head, 0.0, query)]
        query_heads = [x.astype(bf16) for x in query_heads]
        key_grad, value_grad = 0.0, 0.0
        for hd in range(2):
            prob = probs[n, hd]
            prob_grad = nt(value, mixed_heads[hd])
            inner = jnp.sum(prob * prob_grad, axis=0, keepdims=True)
            score_grad = (prob * (prob_grad - inner)).astype(bf16)
            value_grad = value_grad + nn(prob.astype(bf16), mixed_heads[hd])
            key_grad = key_grad + nn(score_grad, query_heads[hd])
            back = nn(jnp.concatenate([keys[HD * hd : HD * (hd + 1)], keys[D : D + 32]], axis=0), score_grad)
            dq.append(back[:HD])
            along.append(back[HD:])
        dkv[n, 0:KEYS, :D] = (key_grad * SCALE).astype(bf16)
        dkv[n, 0:KEYS, D:] = value_grad.astype(bf16)
        dkv[n, KEYS:, :] = jnp.zeros((dkv.shape[1] - KEYS, 2 * D), bf16)
        for k in range(1, HG):
            dkv_copy(n, k, next_height(k)).start()
        back = jnp.concatenate(dq + along, axis=0).T
        right = back[:, 128:]
        apart = []
        for hd in range(2):
            apart.append(
                jnp.take_along_axis(right, back_spot + 32 * hd, axis=1, mode="promise_in_bounds") * back_ok
            )
        apart = halves(jnp.concatenate(apart, axis=1), 1)
        r.dr[n] = apart
        from_tables = nn(apart, jnp.concatenate([table[...], table[...]], axis=0))
        dqx[n, R : R + T, :] = back[:, :D] * SCALE + from_tables + mixed_grad
        outer = nn(edges, dqx[n, R : R + T, :].astype(bf16)).astype(bf16)
        r.dqs[0, n] = outer[:HX]
        r.dqs[1, n] = outer[HX:]

    loop(0, IMG, attention_back)
    back_up = to_height(r.dqs.at[0], r.dqr.at[1], r.s_qsend.at[0], r.s_qrecv.at[0], above)
    back_down = to_height(r.dqs.at[1], r.dqr.at[0], r.s_qsend.at[1], r.s_qrecv.at[1], below)
    back_up.start()
    back_down.start()

    def two_copy(i, j, b):
        return to_batch(r.t[i].at[j], r.u[i].at[me], r.s_twosend.at[i, j], r.s_tworecv.at[i, me], b)

    def two_arrival(i, b):
        return to_batch(r.t[i].at[0], r.u[i].at[b], r.s_twosend.at[i, 0], r.s_tworecv.at[i, b], b)

    def stage_one(i):
        for k in range(1, HG):
            one_copy(i, k, hh).wait_recv()

        def add(j):
            b = hh * QB + j
            total = r.d[i][b].astype(f32)
            for k in range(HG - 1):
                total = total + r.p[i][k, j].astype(f32)
            r.t[i][j] = total.astype(bf16)

            @pl.when(b != me)
            def _():
                two_copy(i, j, b).start()

        loop(0, QB, add)

    stage_one(1)

    both = tn(flat(r.qh), flat(r.dr))
    rel = (
        both[:HD, 0:128] + both[:HD, 256:384] + both[HD:, 128:256] + both[HD:, 384:512]
    )
    rel = jnp.concatenate([rel, jnp.zeros((128 - HD, 128), f32)], axis=0).T
    for q in range(HG):
        r.smallp[q, 24:, :] = rel[32 * q : 32 * (q + 1)]

    has_above = (hh > 0).astype(f32)
    has_below = (hh < HG - 1).astype(f32)
    back_up.wait_recv()
    back_down.wait_recv()

    def queries_back(n):
        edge = jnp.concatenate([r.dqr[0, n].astype(f32) * has_above, r.dqr[1, n].astype(f32) * has_below], axis=0)
        edge = nn(r.spread[:, : 2 * HX], edge.astype(bf16))
        nothing = jnp.zeros((R, D), f32)
        field = dqx[n]
        whole = field[R : R + T]
        later = jnp.concatenate([nothing, rolled(whole, -1) * inner_low + edge * (1.0 - inner_low), nothing], axis=0)
        sooner = jnp.concatenate([nothing, rolled(whole, 1) * inner_top + edge * (1.0 - inner_top), nothing], axis=0)
        own = qx[n, R : R + T, :]
        total = 0.0
        for a, moved in enumerate((later, field, sooner)):
            for b in range(3):
                here = moved[R * (2 - b) : R * (2 - b) + T]
                total = total + poolq[3 * a + b : 3 * a + b + 1, :] * here
                paccq[3 * a + b] += folded(here * own)
        r.pq[n] = (total * cell_mask(n)).astype(bf16)

    loop(0, IMG, queries_back)

    def keys_values_back(n):
        for k in range(1, HG):
            dkv_copy(n, k, hh).wait_recv()
        total = dkv[n, pl.ds(pl.multiple_of(hh * (KL * KCP), KL * KCP), KROWS), :].astype(f32)
        for k in range(HG - 1):
            total = total + r.dkvr[k, n].astype(f32)
        wide = nn(r.unpick[...], halves(total, 0))
        taps = [wide[T // 2 * a : T // 2 * (a + 1)] for a in range(3)]
        field = kvx[n]
        sides = [columns(field, b) for b in range(3)]
        even, odd, late = 0.0, 0.0, 0.0
        for a in range(3):
            even = even + poolkv[3 * a + 1 : 3 * a + 2, :] * taps[a]
            odd = odd + poolkv[3 * a + 2 : 3 * a + 3, :] * taps[a]
            late = late + poolkv[3 * a : 3 * a + 1, :] * taps[a]
            for b in range(3):
                pacckv[3 * a + b] += folded(sides[b] * taps[a])
        odd = odd + jnp.concatenate([late[R:], jnp.zeros((R, 2 * D), f32)], axis=0)
        pairs = [x.reshape(KC, R, 2 * D) for x in (even, odd)]
        result = jnp.concatenate(pairs, axis=1).reshape(T, 2 * D)
        r.pkv[n] = (result * cell_mask(n)).astype(bf16)

    loop(0, IMG, keys_values_back)

    r.f_q[...] = tn(flat(r.ne), flat(r.pq))
    r.f_kv[...] = tn(flat(r.ne), flat(r.pkv))
    for b in range(B):
        at = slice(rows * b, rows * (b + 1))
        r.d[0][b] = jnp.concatenate([r.f_q[at, :], r.f_kv[at, :]], axis=1).astype(bf16)
    for k in range(1, HG):
        one_copy(0, k, next_height(k)).start()

    def projection_back(n):
        grad = nt(r.pq[n], wq[...]) + nt(r.pkv[n], wkv[...])
        hat = r.hat_one[n]
        acc[0:1, 0:D] += jnp.sum(grad * hat, axis=0, keepdims=True)
        acc[0:1, D : 2 * D] += jnp.sum(grad, axis=0, keepdims=True)
        r.v_ig[n] = r.mgd[n] + normalise_back(grad, gain_one, hat, r.inv_one[n])

    loop(0, IMG, projection_back)
    input_out = pltpu.make_async_copy(r.v_ig, r.o_ig, r.s_out.at[1])
    input_out.start()

    small = r.small
    small[...] = jnp.zeros_like(small)
    for t in range(9):
        small[t : t + 1, 0:D] = jnp.sum(paccq[t], axis=0, keepdims=True)
        small[t : t + 1, D : 3 * D] = jnp.sum(pacckv[t], axis=0, keepdims=True)
    small[9:10, 0:D] = nn(ones, flat(r.pq))[0:1]
    small[9:10, D : 3 * D] = nn(ones, flat(r.pkv))[0:1]
    small[10:13, :] = acc[...]
    for q in range(HG):
        for i in range(6):
            r.smallp[q, 4 * i : 4 * (i + 1), :] = small[4 * q : 4 * (q + 1), 128 * i : 128 * (i + 1)]

    def small_one(k, target):
        return to_height(
            r.smallp.at[target], r.smallr.at[k - 1], r.s_smallsend.at[k - 1], r.s_smallrecv.at[k - 1], target
        )

    for k in range(1, HG):
        small_one(k, next_height(k)).start()

    def small_two(k):
        slot = r.smallu.at[me]
        return to_batch(slot, slot, r.s_smalltwo.at[k], r.s_smalltwor.at[me], next_batch(k))

    def small_two_arrival(k):
        b = next_batch(k)
        slot = r.smallu.at[b]
        return to_batch(slot, slot, r.s_smalltwo.at[k], r.s_smalltwor.at[b], b)

    stage_one(0)
    for k in range(1, HG):
        small_one(k, hh).wait_recv()
    total = r.smallp[hh]
    for k in range(HG - 1):
        total = total + r.smallr[k]
    r.smallu[me] = total
    loop(1, B, lambda k: small_two(k).start())

    owned = me // QB == hh
    spans = (slice(PE, PE + PI), slice(0, PE))

    def three_copy(i, k):
        return to_height(
            r.z[i], r.z[i], r.s_threesend.at[i, k - 1], r.s_threerecv.at[i], next_height(k)
        )

    @pl.when(owned)
    def _():
        for i in (1, 0):
            loop(1, B, lambda k, i=i: two_arrival(i, next_batch(k)).wait_recv())
            r.u[i][me] = r.t[i][me - hh * QB]
            total = r.u[i][0].astype(f32)
            for b in range(1, B):
                total = total + r.u[i][b].astype(f32)
            r.z[i][...] = total
            for k in range(1, HG):
                three_copy(i, k).start()

    def small_three(k):
        slot = r.smallz.at[hh]
        return to_height(slot, slot, r.s_smallthree.at[k - 1], r.s_smallthreer.at[k - 1], next_height(k))

    def small_three_arrival(k):
        slot = r.smallz.at[next_height(HG - k)]
        return to_height(slot, slot, r.s_smallthree.at[k - 1], r.s_smallthreer.at[k - 1], next_height(k))

    loop(1, B, lambda k: small_two_arrival(k).wait_recv())
    total = r.smallu[0]
    for b in range(1, B):
        total = total + r.smallu[b]
    r.smallz[hh] = total
    for k in range(1, HG):
        small_three(k).start()

    @pl.when(jnp.logical_not(owned))
    def _():
        for i in range(2):
            three_copy(i, 1).wait_recv()

    for k in range(1, HG):
        small_three_arrival(k).wait_recv()
    outs = [(r.z[0], r.o_z[0]), (r.z[1], r.o_z[1]), (r.smallz, r.o_small)]
    outs = [pltpu.make_async_copy(a, b, r.s_out.at[2 + k]) for k, (a, b) in enumerate(outs)]
    for out in outs:
        out.start()

    for copy in (halo_up, halo_down, back_up, back_down):
        copy.wait_send()
    for i in range(2):
        loop(1, B, lambda k, i=i: weight_copy(i, k).wait_send())
    for k in range(1, HG):
        for n in range(IMG):
            kv_copy(n, k, hh, next_height(k)).wait_send()
            dkv_copy(n, k, next_height(k)).wait_send()
        for i in range(2):
            one_copy(i, k, next_height(k)).wait_send()
        small_one(k, next_height(k)).wait_send()
        small_three(k).wait_send()

    def sent_two(j):
        @pl.when(hh * QB + j != me)
        def _():
            for i in range(2):
                two_copy(i, j, hh * QB + j).wait_send()

    loop(0, QB, sent_two)
    loop(1, B, lambda k: small_two(k).wait_send())

    @pl.when(owned)
    def _():
        for i in range(2):
            for k in range(1, HG):
                three_copy(i, k).wait_send()

    result_out.wait()
    input_out.wait()
    for out in outs:
        out.wait()


def adam_step(weight, first_state, second_state, gradient, step_rate, decay_rate):
    moment = beta_one * first_state + (1.0 - beta_one) * gradient
    square = beta_two * second_state + (1.0 - beta_two) * gradient * gradient
    unbiased = moment * (1.0 / (1.0 - beta_one**STEP))
    scaled = square * (1.0 / (1.0 - beta_two**STEP))
    updated = weight * (1.0 - step_rate * decay_rate) - step_rate * unbiased / (jnp.sqrt(scaled) + adam_eps)
    return (updated, moment, square)


def adam_kernel(tree, *refs):
    r = types.SimpleNamespace(**jax.tree.unflatten(tree, refs))

    def row(ref):
        return ref.at[0] if ref.shape[0] == 1 and len(ref.shape) == 2 else ref

    arrivals = []
    for index, (source, target) in enumerate(zip(r.given, r.v_given)):
        arrivals.append(pltpu.make_async_copy(source, row(target), r.s_in.at[index]))
        arrivals[-1].start()
    rows = r.v_given[0].shape[0]
    small = r.small
    for i in range(4):
        arrivals[i].wait()
    for q in range(HG):
        for i in range(6):
            small[4 * q : 4 * (q + 1), 128 * i : 128 * (i + 1)] = r.v_given[2][q, 4 * i : 4 * (i + 1), :]
    rel = jnp.concatenate([r.v_given[2][q, 24:, :] for q in range(HG)], axis=0)
    for t in range(9):
        for i in range(3):
            r.pgrad[t, i : i + 1, :] = small[t : t + 1, D * i : D * (i + 1)]
    bgrad = r.bgrad
    bgrad[0:1, 0:D] = small[10:11, D : 2 * D]
    bgrad[0:1, D : 2 * D] = small[10:11, 3 * D :]
    bgrad[0:1, 2 * D : 5 * D] = small[9:10, : 3 * D]
    bgrad[0:1, 5 * D : 6 * D] = small[11:12, 0:D]
    bgrad[0:1, 6 * D : 6 * D + HID] = small[12:13, :]
    bgrad[0:1, 6 * D + HID :] = small[11:12, D : 2 * D]
    pack = r.v_given[1]
    given = [r.v_given[3 + 3 * index : 6 + 3 * index] for index in range(9)]
    gradients = [
        lambda: r.v_given[0][...],
        lambda: pack[:, HID + 4 * D : HID + 5 * D],
        lambda: pack[:, :HID],
        lambda: jnp.concatenate([pack[:, HID + D * i : HID + D * (i + 1)] for i in range(4)], axis=0),
        lambda: r.pgrad[...],
        lambda: rel[0 : given[5][0].shape[0], 0:HD],
        lambda: rel[64 : 64 + given[6][0].shape[0], 0:HD],
        lambda: jnp.concatenate([small[10:11, 0:D], small[10:11, 2 * D : 3 * D]], axis=0),
        lambda: bgrad[...],
    ]
    leaving = []

    def leave(index):
        copy = pltpu.make_async_copy(row(r.v_fresh[index]), r.fresh[index], r.s_out.at[index])
        copy.start()
        leaving.append(copy)

    for index in range(9):
        for k in range(3):
            if index or k:
                arrivals[3 + 3 * index + k].wait()
        weight, first, second = [x[...] for x in given[index]]
        fresh = adam_step(
            weight, first, second, gradients[index](), step_rates[index], decay_rates[index]
        )
        if index < 4:
            fresh += (fresh[0].astype(bf16),)
        at = 4 * min(index, 4) + 3 * max(index - 4, 0)
        for k, value in enumerate(fresh):
            r.v_fresh[at + k][...] = value
            leave(at + k)
    for copy in leaving:
        copy.wait()


def shards(activations, cotangent, extent, *params):
    B = lax.axis_size("batch")
    assert lax.axis_size("height") == HG and activations.shape == (IMG, R, C, D)
    params = list(params)
    for k in range(12, 15):
        params[k] = params[k].transpose(1, 0, 2)
    weights = params[0::3]
    rows = weights[0].shape[0]
    QB = B // HG
    assert weights[3].shape[0] == 4 * rows

    def by_column(x):
        return x.transpose(0, 2, 1, 3).reshape(IMG, T, D)

    def like(x):
        return jax.ShapeDtypeStruct(x.shape, x.dtype)

    anywhere = pl.BlockSpec(memory_space=pl.ANY)
    vm, dma = pltpu.VMEM, pltpu.SemaphoreType.DMA

    def call(kernel, operands, results, scratch, specs, **kwargs):
        flat_operands, operand_tree = jax.tree.flatten(operands)
        flat_results, result_tree = jax.tree.flatten(results)
        whole, tree = jax.tree.flatten({**operands, **results, **scratch})
        order = {id(x): k for k, x in enumerate(flat_operands + flat_results + jax.tree.leaves(scratch))}
        places = [order[id(x)] for x in whole]

        def ordered(*refs):
            return kernel(tree, *[refs[k] for k in places])

        out = pl.pallas_call(
            ordered,
            out_shape=flat_results,
            in_specs=[specs.get(id(x), anywhere) for x in flat_operands],
            out_specs=[anywhere] * len(flat_results),
            scratch_shapes=jax.tree.leaves(scratch),
            **kwargs,
        )(*flat_operands)
        return jax.tree.unflatten(result_tree, out)

    operands = dict(
        act=by_column(activations),
        cot=by_column(cotangent),
        extent=extent.T,
        w_in=weights[0],
        w_out=weights[1],
        w_exp=weights[2],
        w_red=weights[3],
        pool=weights[4],
        relh=weights[5],
        relw=weights[6],
        gains=weights[7],
        biases=weights[8],
    )
    results = dict(
        o_res=jax.ShapeDtypeStruct((IMG, T, D), bf16),
        o_ig=jax.ShapeDtypeStruct((IMG, T, D), f32),
        o_z=[jax.ShapeDtypeStruct((rows, PI), f32), jax.ShapeDtypeStruct((rows, PE), f32)],
        o_small=jax.ShapeDtypeStruct((HG, 56, 128), f32),
    )
    lanes = (PI, PE)
    scratch = dict(
        v_act=vm((IMG, T, D), bf16),
        v_cot=vm((IMG, T, D), bf16),
        v_in=vm(weights[0].shape, f32),
        v_out=vm(weights[1].shape, f32),
        v_exp=vm(weights[2].shape, f32),
        v_red=vm(weights[3].shape, f32),
        v_pool=vm(weights[4].shape, f32),
        v_relh=vm(weights[5].shape, f32),
        v_relw=vm(weights[6].shape, f32),
        v_gains=vm(weights[7].shape, f32),
        v_biases=vm((1,) + weights[8].shape, f32),
        g=[vm((B, rows, x), bf16) for x in lanes],
        d=[vm((B, rows, x), bf16) for x in lanes],
        p=[vm((HG - 1, QB, rows, x), bf16) for x in lanes],
        t=[vm((QB, rows, x), bf16) for x in lanes],
        u=[vm((B, rows, x), bf16) for x in lanes],
        z=[vm((rows, x), f32) for x in lanes],
        f_q=vm((D, D), f32),
        f_kv=vm((D, 2 * D), f32),
        f_exp=vm((D, HID), f32),
        f_red=vm((HID, D), f32),
        f_out=vm((D, D), f32),
        wq=vm((D, D), bf16),
        wkv=vm((D, 2 * D), bf16),
        wout=vm((D, D), bf16),
        wexp=vm((D, HID), bf16),
        wred=vm((HID, D), bf16),
        poolq=vm((9, D), f32),
        poolkv=vm((9, 2 * D), f32),
        tablef=vm((256, D), f32),
        table=vm((256, D), bf16),
        hs=vm((2, IMG, HX, D), bf16),
        hr=vm((2, IMG, HX, D), bf16),
        nh=vm((2 * IMG * HX, D), bf16),
        halo_q=vm((2 * IMG * HX, D), f32),
        halo_kv=vm((IMG * HX, 2 * D), f32),
        spread=vm((T, 4 * HX), bf16),
        pick=vm((KL * KCP, T), bf16),
        unpick=vm((3 * T // 2, 2 * KROWS), bf16),
        hot=vm((KEYS, 64), bf16),
        acc=vm((3, HID), f32),
        paccq=vm((9, 8, D), f32),
        pacckv=vm((9, 8, 2 * D), f32),
        ne=vm((IMG, T, D), bf16),
        hat_one=vm((IMG, T, D), f32),
        inv_one=vm((IMG, T, 1), f32),
        kvx=vm((IMG, TX, 2 * D), f32),
        qx=vm((IMG, TX, D), f32),
        dqx=vm((IMG, TX, D), f32),
        kvg=vm((HG, IMG, KL * KCP, 2 * D), bf16),
        ka=vm((IMG, KEYS, 256), bf16),
        va=vm((IMG, KEYS, D), bf16),
        qp=vm((IMG, T, D), f32),
        qh=vm((IMG, T, D), bf16),
        qa=vm((IMG, 2, T, 256), bf16),
        probs=vm((IMG, 2, KEYS, T), f32),
        mxh=vm((IMG, T, D), bf16),
        sh=vm((IMG, T, D), bf16),
        ac=vm((IMG, T, HID), bf16),
        uh=vm((IMG, T, D), bf16),
        eg=vm((IMG, T, HID), bf16),
        mgd=vm((IMG, T, D), f32),
        ag=vm((IMG, T, D), bf16),
        mg=vm((IMG, T, D), bf16),
        v_res=vm((IMG, T, D), bf16),
        v_ig=vm((IMG, T, D), f32),
        dkv=vm((IMG, KEYS + KL * KCP, 2 * D), bf16),
        dkvr=vm((HG - 1, IMG, KROWS, 2 * D), bf16),
        dqs=vm((2, IMG, HX, D), bf16),
        dqr=vm((2, IMG, HX, D), bf16),
        dr=vm((IMG, T, 512), bf16),
        pq=vm((IMG, T, D), bf16),
        pkv=vm((IMG, T, 2 * D), bf16),
        small=vm((16, HID), f32),
        smallp=vm((HG, 56, 128), f32),
        smallr=vm((HG - 1, 56, 128), f32),
        smallu=vm((B, 56, 128), f32),
        smallz=vm((HG, 56, 128), f32),
        s_local=dma((11,)),
        s_out=dma((5,)),
        s_wsend=dma((2, B)),
        s_wrecv=dma((2, B)),
        s_hsend=dma((2,)),
        s_hrecv=dma((2,)),
        s_ksend=dma((IMG, HG - 1)),
        s_krecv=dma((IMG, HG - 1)),
        s_dsend=dma((IMG, HG - 1)),
        s_drecv=dma((IMG, HG - 1)),
        s_qsend=dma((2,)),
        s_qrecv=dma((2,)),
        s_onesend=dma((2, HG - 1)),
        s_onerecv=dma((2, HG - 1)),
        s_smallsend=dma((HG - 1,)),
        s_smallrecv=dma((HG - 1,)),
        s_twosend=dma((2, QB)),
        s_tworecv=dma((2, B)),
        s_smalltwo=dma((B,)),
        s_smalltwor=dma((B,)),
        s_threesend=dma((2, HG - 1)),
        s_threerecv=dma((2,)),
        s_smallthree=dma((HG - 1,)),
        s_smallthreer=dma((HG - 1,)),
    )
    main = call(
        functools.partial(main_kernel, B),
        operands,
        results,
        scratch,
        {id(operands["extent"]): pl.BlockSpec(memory_space=pltpu.SMEM)},
        compiler_params=pltpu.CompilerParams(
            collective_id=0, has_side_effects=True, vmem_limit_bytes=52 * 1024 * 1024
        ),
        name="block",
    )
    given = main["o_z"] + [main["o_small"]] + params
    fresh = []
    for index in range(9):
        fresh += [like(weights[index]) for _ in range(3)]
        if index < 4:
            fresh += [jax.ShapeDtypeStruct(weights[index].shape, bf16)]

    def room(x):
        return vm((1,) + x.shape if len(x.shape) == 1 else x.shape, x.dtype)

    fresh = call(
        adam_kernel,
        dict(given=given),
        dict(fresh=fresh),
        dict(
            v_given=[room(x) for x in given],
            v_fresh=[room(x) for x in fresh],
            small=vm((16, HID), f32),
            pgrad=vm(weights[4].shape, f32),
            bgrad=vm((1,) + weights[8].shape, f32),
            s_in=dma((len(given),)),
            s_out=dma((len(fresh),)),
        ),
        {},
        name="adam",
    )["fresh"]
    for k in range(16, 19):
        fresh[k] = fresh[k].transpose(1, 0, 2)

    def by_row(x):
        return x.reshape(IMG, C, R, D).transpose(0, 2, 1, 3)

    return (by_row(main["o_res"]), by_row(main["o_ig"])) + tuple(fresh)


def solution(mesh):
    grid = P("batch", "height", None, None)
    rows = P("batch", None)
    in_specs = (grid, grid, rows) + (rows,) * 12 + (P(),) * 15
    out_specs = (grid, grid) + (rows,) * 16 + (P(),) * 15
    return jax.shard_map(shards, mesh=mesh, in_specs=in_specs, out_specs=out_specs, check_vma=False)
```

```python
import functools
import types

import jax
import jax.numpy as jnp
from jax import lax
from jax.experimental import pallas as pl
from jax.experimental.pallas import tpu as pltpu
from jax.sharding import PartitionSpec as P

STEP = 10
MESH = pl.DeviceIdType.MESH
f32 = jnp.float32
bf16 = jnp.bfloat16

norm_eps = 1e-06
beta_one = 0.9
beta_two = 0.999
adam_eps = 1e-08
masked_value = -1000000000.0
step_rates = (0.04, 0.04, 0.04, 0.04, 0.2, 0.1, 0.1, 0.5, 0.1)
decay_rates = (0.05, 0.05, 0.05, 0.05, 0.05, 0.05, 0.05, 0.0, 0.0)

IMG, R, C, D, HD, HID = 3, 8, 28, 192, 96, 768
T = R * C
TX = T + 2 * R
HG = 4
KR, KC, KCP = R * HG // 2, C // 2, 16
KL = R // 2
KEYS = KR * KCP
SCALE = HD ** (-0.5)
KROWS = (KL + 1) * KCP
HX = 32
PH = HID + 128
PE = 2 * PH


def nn(a, b):
    return lax.dot_general(a, b, (((1,), (0,)), ((), ())), preferred_element_type=f32)


def nt(a, b):
    return lax.dot_general(a, b, (((1,), (1,)), ((), ())), preferred_element_type=f32)


def tn(a, b):
    return lax.dot_general(a, b, (((0,), (0,)), ((), ())), preferred_element_type=f32)


def iota(shape, axis):
    return lax.broadcasted_iota(jnp.int32, shape, axis)


def rolled(x, by):
    return pltpu.roll(x, by % x.shape[0], 0)


def halves(x, axis):
    high = x.astype(bf16)
    return jnp.concatenate([high, (x - high.astype(f32)).astype(bf16)], axis=axis)


def normalise(x):
    mean = jnp.sum(x, axis=1, keepdims=True) * (1.0 / D)
    centered = x - mean
    inverse = lax.rsqrt(jnp.sum(centered * centered, axis=1, keepdims=True) * (1.0 / D) + norm_eps)
    return centered * inverse, inverse


def normalise_back(grad, gain, hat, inverse):
    scaled = grad * gain
    one = jnp.sum(scaled, axis=1, keepdims=True) * (1.0 / D)
    two = jnp.sum(scaled * hat, axis=1, keepdims=True) * (1.0 / D)
    return inverse * (scaled - one - hat * two)


def folded(x):
    return jnp.sum(x.reshape(x.shape[0] // 8, 8, x.shape[1]), axis=0)


def main_kernel(B, tree, *refs):
    r = types.SimpleNamespace(**jax.tree.unflatten(tree, refs))
    me = lax.axis_index("batch")
    hh = lax.axis_index("height")
    HB = B // 2
    rows = r.w_in.shape[0]
    side = lax.rem(hh, 2)
    pair = lax.div(hh, 2)
    twin = hh + 1 - 2 * side
    across = lax.rem(hh + 2, HG)
    corner = lax.rem(twin + 2, HG)

    def loop(first, last, body):
        def step(i, carry):
            body(i)
            return carry

        lax.fori_loop(first, last, step, 0)

    def next_batch(k):
        return lax.rem(me + k, B)

    def next_height(k):
        return lax.rem(hh + k, HG)

    local = [
        (r.act, r.v_act),
        (r.w_in, r.v_in),
        (r.w_out, r.v_out),
        (r.w_exp, r.v_exp),
        (r.w_red, r.v_red),
        (r.pool, r.v_pool),
        (r.relh, r.v_relh),
        (r.relw, r.v_relw),
        (r.gains, r.v_gains),
        (r.biases, r.v_biases.at[0]),
        (r.cot, r.v_cot),
    ]
    local = [pltpu.make_async_copy(a, b, r.s_local.at[k]) for k, (a, b) in enumerate(local)]
    for copy in local:
        copy.start()

    barrier = pltpu.get_barrier_semaphore()

    def greet_batch(k):
        pl.semaphore_signal(barrier, inc=1, device_id=(next_batch(k), hh), device_id_type=MESH)

    loop(1, B, greet_batch)
    for k in range(1, HG):
        pl.semaphore_signal(barrier, inc=1, device_id=(me, next_height(k)), device_id_type=MESH)

    def to_batch(src, dst, send, recv, b):
        return pltpu.make_async_remote_copy(
            src_ref=src, dst_ref=dst, send_sem=send, recv_sem=recv, device_id=(b, hh), device_id_type=MESH
        )

    def to_height(src, dst, send, recv, h):
        return pltpu.make_async_remote_copy(
            src_ref=src, dst_ref=dst, send_sem=send, recv_sem=recv, device_id=(me, h), device_id_type=MESH
        )

    def in_copy(k):
        slot = r.gin.at[me]
        return to_batch(slot, slot, r.s_wsend.at[0, k], r.s_wrecv.at[0, me], next_batch(k))

    def in_arrival(k):
        b = next_batch(k)
        slot = r.gin.at[b]
        return to_batch(slot, slot, r.s_wsend.at[0, k], r.s_wrecv.at[0, b], b)

    def rest_copy(k):
        slot = r.grest.at[side, me]
        return to_batch(slot, slot, r.s_wsend.at[1, k], r.s_wrecv.at[1, me], next_batch(k))

    def rest_arrival(k):
        b = next_batch(k)
        slot = r.grest.at[side, b]
        return to_batch(slot, slot, r.s_wsend.at[1, k], r.s_wrecv.at[1, b], b)

    def rest_handed(half, target):
        slot = r.grest.at[half]
        return to_height(slot, slot, r.s_wsend.at[0, 0], r.s_wrecv.at[2, 0], target)

    local[0].wait()
    local[1].wait()
    r.gin[me] = r.v_in[...].astype(bf16)

    edge_rows = iota((2 * HX, T), 0)
    edge_cols = iota((2 * HX, T), 1)
    edges = (edge_cols == (edge_rows % HX) * R + (edge_rows // HX) * (R - 1)).astype(bf16)
    for n in range(IMG):
        outer = nn(edges, r.v_act[n]).astype(bf16)
        r.hs[0, n] = outer[:HX]
        r.hs[1, n] = outer[HX:]
    above, below = next_height(HG - 1), next_height(1)
    halo_up = to_height(r.hs.at[0], r.hr.at[1], r.s_hsend.at[0], r.s_hrecv.at[0], above)
    halo_down = to_height(r.hs.at[1], r.hr.at[0], r.s_hsend.at[1], r.s_hrecv.at[1], below)

    pl.semaphore_wait(barrier, B - 1 + HG - 1)
    loop(1, B, lambda k: in_copy(k).start())
    halo_up.start()
    halo_down.start()
    for k in (2, 3, 4):
        local[k].wait()
    spare = jnp.zeros((rows, PE - HID - 5 * D), f32)
    left = jnp.concatenate([r.v_exp[...], r.v_out[:, :128]], axis=1)
    blocks = [r.v_red[rows * i : rows * (i + 1)] for i in range(4)]
    right = jnp.concatenate(blocks + [r.v_out[:, 128:], spare], axis=1)
    r.grest[side, me] = jnp.where(side == 0, left, right).astype(bf16)
    loop(1, B, lambda k: rest_copy(k).start())

    for k in range(5, 11):
        local[k].wait()
    poolq, poolkv, table = r.poolq, r.poolkv, r.table
    poolq[...] = r.v_pool[:, 0, :]
    poolkv[:, :D] = r.v_pool[:, 1, :]
    poolkv[:, D:] = r.v_pool[:, 2, :]
    r.tablef[...] = jnp.zeros_like(r.tablef)
    relh_rows, relw_rows = r.v_relh.shape[0], r.v_relw.shape[0]
    for hd in range(2):
        r.tablef[128 * hd : 128 * hd + relh_rows, HD * hd : HD * (hd + 1)] = r.v_relh[...]
        r.tablef[128 * hd + 64 : 128 * hd + 64 + relw_rows, HD * hd : HD * (hd + 1)] = r.v_relw[...]
    table[...] = r.tablef[...].astype(bf16)
    shift_one = r.v_biases[0:1, 0:D]
    shift_two = r.v_biases[0:1, D : 2 * D]
    bias_q = r.v_biases[0:1, 2 * D : 3 * D]
    bias_kv = r.v_biases[0:1, 3 * D : 5 * D]
    bias_out = r.v_biases[0:1, 5 * D : 6 * D]
    bias_exp = r.v_biases[0:1, 6 * D : 6 * D + HID]
    bias_red = r.v_biases[0:1, 6 * D + HID : 7 * D + HID]
    gain_one = r.v_gains[0:1, :]
    gain_two = r.v_gains[1:2, :]
    acc, paccq, pacckv = r.acc, r.paccq, r.pacckv
    acc[...] = jnp.zeros_like(acc)
    paccq[...] = jnp.zeros_like(paccq)
    pacckv[...] = jnp.zeros_like(pacckv)
    kvx, qx, dqx = r.kvx, r.qx, r.dqx

    cell = iota((T, 1), 0)
    cell_y, cell_x = hh * R + cell % R, cell // R
    halo_at = iota((2 * IMG * HX, 1), 0)

    def cell_mask(n):
        return ((cell_y < r.extent[0, n]) & (cell_x < r.extent[1, n])).astype(f32)

    def first_norm(n):
        hat, inverse = normalise(r.v_act[n].astype(f32))
        r.ne[n] = (hat * gain_one + shift_one).astype(bf16)
        r.hat_one[n] = hat
        r.inv_one[n] = inverse
        kvx[n, 0:R, :] = jnp.zeros((R, 2 * D), f32)
        kvx[n, T + R :, :] = jnp.zeros((R, 2 * D), f32)
        for x in (qx, dqx):
            x[n, 0:R, :] = jnp.zeros((R, D), f32)
            x[n, T + R :, :] = jnp.zeros((R, D), f32)

    loop(0, IMG, first_norm)

    spread_rows = iota((T, 2 * HX), 0)
    spread_cols = iota((T, 2 * HX), 1)
    spread = (
        (spread_rows // R == spread_cols % HX) & (spread_rows % R == (spread_cols // HX) * (R - 1))
    ).astype(bf16)
    r.spread[...] = jnp.concatenate([spread, spread], axis=1)
    pick_rows = iota((KL * KCP, T // 2), 0)
    pick_cols = iota((KL * KCP, T // 2), 1)
    pick = (
        (pick_rows % KCP == pick_cols // R) & (pick_cols % R == 2 * (pick_rows // KCP))
    ).astype(bf16)
    r.pick[...] = jnp.concatenate([pick, pick], axis=1)
    back_rows = iota((3 * T // 2, KROWS), 0)
    back_cols = iota((3 * T // 2, KROWS), 1)
    back_tap, back_cell = back_rows // (T // 2), back_rows % (T // 2)
    unpick = (
        (back_cols % KCP == back_cell // R)
        & (back_cell % R == 2 * (back_cols // KCP) + back_tap - 1)
    ).astype(bf16)
    r.unpick[...] = jnp.concatenate([unpick, unpick], axis=1)
    key_rows = iota((KEYS, 64), 0)
    key_lane = iota((KEYS, 64), 1) % 32
    r.hot[...] = (
        (key_lane == key_rows // KCP) | (key_lane == KR + key_rows % KCP)
    ).astype(bf16)
    halo_up.wait_recv()
    halo_down.wait_recv()
    hat, _ = normalise(r.hr[...].reshape(2 * IMG * HX, D).astype(f32))
    r.nh[...] = (hat * gain_one + shift_one).astype(bf16)

    halo_y = jnp.where(halo_at < IMG * HX, hh * R - 1, hh * R + R)
    halo_image = halo_at // HX % IMG
    halo_ok = jnp.zeros((2 * IMG * HX, 1), jnp.bool_)
    for n in range(IMG):
        halo_ok = halo_ok | (
            (halo_image == n)
            & (halo_y >= 0)
            & (halo_y < r.extent[0, n])
            & (halo_at % HX < r.extent[1, n])
        )
    halo_ok = halo_ok.astype(f32)

    loop(1, B, lambda k: in_arrival(k).wait_recv())
    wq, wkv, wout, wexp, wred = r.wq, r.wkv, r.wout, r.wexp, r.wred
    for b in range(B):
        shard = r.gin[b].astype(f32)
        r.f_q[rows * b : rows * (b + 1), :] = shard[:, :D]
        r.f_kv[rows * b : rows * (b + 1), :] = shard[:, D:]
    wq[...] = r.f_q[...].astype(bf16)
    wkv[...] = r.f_kv[...].astype(bf16)

    kvg = r.kvg

    def kv_copy(n, k, source, target):
        slot = kvg.at[source, n]
        return to_height(slot, slot, r.s_ksend.at[n, k], r.s_krecv.at[n, k], target)

    half = IMG * HX
    r.halo_kv[...] = (nn(r.nh[:half], wkv[...]) + bias_kv) * halo_ok[:half]

    def columns(x, b):
        pairs = x.reshape(TX // (2 * R), 2 * R, x.shape[1])
        side = pairs[b // 2 : b // 2 + KC, R * (b % 2) : R * (b % 2) + R]
        return side.reshape(T // 2, x.shape[1])

    def keys_values(n):
        kvx[n, R : R + T, :] = (nn(r.ne[n], wkv[...]) + bias_kv) * cell_mask(n)
        field = kvx[n]
        sides = [columns(field, b) for b in range(3)]
        sums = [sum(poolkv[3 * a + b : 3 * a + b + 1, :] * sides[b] for b in range(3)) for a in range(3)]
        pooled = rolled(sums[0], 1) * (iota((T // 2, 1), 0) % R > 0).astype(f32) + sums[1] + rolled(sums[2], -1)
        edge = r.halo_kv[pl.ds(pl.multiple_of(n * HX, HX), HX), :]
        edge = (
            poolkv[0:1, :] * rolled(edge, 1) + poolkv[1:2, :] * edge + poolkv[2:3, :] * rolled(edge, -1)
        )
        edge_pick = (iota((KCP, HX), 1) == 2 * iota((KCP, HX), 0)).astype(bf16)
        edge = nn(jnp.concatenate([edge_pick, edge_pick], axis=1), halves(edge, 0))
        whole = nn(r.pick[...], halves(pooled, 0))
        kvg[hh, n] = jnp.concatenate([whole[:KCP] + edge, whole[KCP:]], axis=0).astype(bf16)
        kv_copy(n, 1, hh, across).start()
        kv_copy(n, 0, hh, twin).start()

    loop(0, IMG, keys_values)

    qp, qa = r.qp, r.qa
    r.halo_q[...] = (nn(r.nh[...], wq[...]) + bias_q) * halo_ok
    lane = iota((T, 128), 1)
    y_at = hh * R + iota((T, 128), 0) % R
    x_at = iota((T, 128), 0) // R
    aux = lane % 32
    spot = jnp.where(aux < KR, y_at - 2 * aux + 2 * (KR - 1), 64 + x_at - 2 * (aux - KR) + 2 * (KC - 1))
    inner_top = (cell % R > 0).astype(f32)
    inner_low = (cell % R < R - 1).astype(f32)

    def beside(x):
        return [rolled(x, 1), x, rolled(x, -1)]

    def queries(n):
        qx[n, R : R + T, :] = (nn(r.ne[n], wq[...]) + bias_q) * cell_mask(n)
        field = qx[n]
        sums = [
            sum(poolq[3 * a + b : 3 * a + b + 1, :] * field[R * b : R * b + T] for b in range(3))
            for a in range(3)
        ]
        top = beside(r.halo_q[pl.ds(pl.multiple_of(n * HX, HX), HX), :])
        low = beside(r.halo_q[pl.ds(pl.multiple_of((IMG + n) * HX, HX), HX), :])
        top = sum(poolq[b : b + 1, :] * top[b] for b in range(3))
        low = sum(poolq[6 + b : 7 + b, :] * low[b] for b in range(3))
        edge = nn(r.spread[...], halves(jnp.concatenate([top, low], axis=0), 0))
        pooled = rolled(sums[0], 1) * inner_top + sums[1] + rolled(sums[2], -1) * inner_low + edge
        qp[n] = pooled
        query = pooled.astype(bf16)
        r.qh[n] = query
        along = nt(query, table[...])
        left, right = pooled[:, :128], pooled[:, 128:]
        right = jnp.concatenate([right, right], axis=1)
        for hd in range(2):
            near = along[:, 128 * hd : 128 * (hd + 1)]
            near = jnp.take_along_axis(near, spot, axis=1, mode="promise_in_bounds") * (HD**0.5)
            rest = near - near.astype(bf16).astype(f32)
            near = jnp.where(lane < 96, near, rest)
            if hd == 0:
                qa[n, hd, :, :128] = jnp.where(lane < HD, left, 0.0).astype(bf16)
                qa[n, hd, :, 128:] = jnp.where(lane < 64, 0.0, near).astype(bf16)
            else:
                qa[n, hd, :, :128] = jnp.where(lane < HD, 0.0, left).astype(bf16)
                qa[n, hd, :, 128:] = jnp.where(lane < 64, right, near).astype(bf16)

    loop(0, IMG, queries)

    def kv_on(n):
        kv_copy(n, 1, across, hh).wait_recv()
        kv_copy(n, 2, across, twin).start()

    loop(0, IMG, kv_on)
    loop(1, B, lambda k: rest_arrival(k).wait_recv())
    rest_handed(side, twin).start()

    key_at = iota((KEYS, 1), 0)
    probs, mxh = r.probs, r.mxh

    def attention(n):
        kv_copy(n, 0, twin, hh).wait_recv()
        kv_copy(n, 2, corner, hh).wait_recv()
        both = jnp.concatenate([kvg[s, n] for s in range(HG)], axis=0)
        r.ka[n, :, :D] = both[:, :D]
        r.ka[n, :, D:] = r.hot[...]
        r.va[n] = both[:, D:]
        valid = (2 * (key_at // KCP) < r.extent[0, n]) & (2 * (key_at % KCP) < r.extent[1, n])
        value = r.va[n].T
        mixed = []
        for hd in range(2):
            scores = nt(r.ka[n], qa[n, hd]) * SCALE
            scores = jnp.where(valid, scores, masked_value)
            raised = jnp.exp(scores - jnp.max(scores, axis=0, keepdims=True))
            prob = raised * (1.0 / jnp.sum(raised, axis=0, keepdims=True))
            probs[n, hd] = prob
            mixed.append(nn(value[HD * hd : HD * (hd + 1)], prob.astype(bf16)))
        mxh[n] = (jnp.concatenate(mixed, axis=0).T + qp[n]).astype(bf16)

    loop(0, IMG, attention)

    rest_handed(1 - side, hh).wait_recv()
    for b in range(B):
        one, two = r.grest[0, b].astype(f32), r.grest[1, b].astype(f32)
        r.f_exp[rows * b : rows * (b + 1), :] = one[:, :HID]
        for i in range(4):
            at = 4 * rows * b + rows * i
            r.f_red[at : at + rows, :] = two[:, D * i : D * (i + 1)]
        r.f_out[rows * b : rows * (b + 1), :128] = one[:, HID:]
        r.f_out[rows * b : rows * (b + 1), 128:] = two[:, 4 * D : 5 * D - 128]
    wout[...] = r.f_out[...].astype(bf16)
    wexp[...] = r.f_exp[...].astype(bf16)
    wred[...] = r.f_red[...].astype(bf16)

    def feed_forward(n):
        mask = cell_mask(n)
        middle = r.v_act[n].astype(f32) + nn(mxh[n], wout[...]) + bias_out
        hat, inverse = normalise(middle)
        second = (hat * gain_two + shift_two).astype(bf16)
        r.sh[n] = second
        expanded = nn(second, wexp[...]) + bias_exp
        half_erf = 0.5 + 0.5 * lax.erf(expanded * (0.5**0.5))
        activated = (expanded * half_erf).astype(bf16)
        slope = half_erf + expanded * jnp.exp(expanded * expanded * -0.5) * 0.3989422804014327
        r.ac[n] = activated
        r.v_res[n] = (mask * (middle + nn(activated, wred[...]) + bias_red)).astype(bf16)
        upstream = r.v_cot[n].astype(f32) * mask
        up_half = upstream.astype(bf16)
        r.uh[n] = up_half
        expanded_grad = (nt(up_half, wred[...]) * slope).astype(bf16)
        r.eg[n] = expanded_grad
        second_grad = nt(expanded_grad, wexp[...])
        acc[0:1, 2 * D : 3 * D] += jnp.sum(second_grad * hat, axis=0, keepdims=True)
        acc[0:1, 3 * D : 4 * D] += jnp.sum(second_grad, axis=0, keepdims=True)
        middle_grad = upstream + normalise_back(second_grad, gain_two, hat, inverse)
        r.mgd[n] = middle_grad
        attn_grad = middle_grad.astype(bf16)
        r.ag[n] = attn_grad
        r.mg[n] = nt(attn_grad, wout[...]).astype(bf16)

    loop(0, IMG, feed_forward)
    result_out = pltpu.make_async_copy(r.v_res, r.o_res, r.s_out.at[0])
    result_out.start()

    ones = jnp.ones((16, IMG * T), bf16)

    def flat(ref):
        return ref[...].reshape(IMG * T, ref.shape[-1])

    r.f_exp[...] = tn(flat(r.sh), flat(r.eg))
    acc[2:3, :] = nn(ones, flat(r.eg))[0:1]
    r.f_red[...] = tn(flat(r.uh), flat(r.ac)).T
    acc[1:2, D : 2 * D] = nn(ones, flat(r.uh))[0:1]
    r.f_out[...] = tn(flat(mxh), flat(r.ag))
    acc[1:2, 0:D] = nn(ones, flat(r.ag))[0:1]
    spare = jnp.zeros((rows, PE - HID - 5 * D), f32)
    for b in range(B):
        r.d[1][b, :, :HID] = r.f_exp[rows * b : rows * (b + 1), :].astype(bf16)
        out_rows = r.f_out[rows * b : rows * (b + 1), :]
        r.d[1][b, :, HID:PH] = out_rows[:, :128].astype(bf16)
        blocks = [r.f_red[rows * (4 * b + i) : rows * (4 * b + i + 1), :] for i in range(4)]
        r.d[1][b, :, PH:] = jnp.concatenate(blocks + [out_rows[:, 128:], spare], axis=1).astype(bf16)

    def one_copy(i, half, target):
        return to_height(
            r.d[i].at[pl.ds(half * HB, HB)], r.p[i], r.s_onesend.at[i], r.s_onerecv.at[i], target
        )

    def two_copy(i, j, b):
        return to_batch(r.t[i].at[j], r.u[i].at[me], r.s_twosend.at[i, j], r.s_tworecv.at[i, me], b)

    def two_arrival(i, b):
        return to_batch(r.t[i].at[0], r.u[i].at[b], r.s_twosend.at[i, 0], r.s_tworecv.at[i, b], b)

    def three_copy(i, k, which, target):
        slot = r.z[i].at[which]
        return to_height(slot, slot, r.s_threesend.at[i, k], r.s_threerecv.at[i, which], target)

    others = (twin, across, corner)
    owned = lax.div(me, HB) == side

    def stage_one(i):
        one_copy(i, 1 - side, twin).start()

    def stage_two(i):
        one_copy(i, side, hh).wait_recv()

        def add(j):
            b = side * HB + j
            r.t[i][j] = (r.d[i][b].astype(f32) + r.p[i][j].astype(f32)).astype(bf16)

            @pl.when(b != me)
            def _():
                two_copy(i, j, b).start()

        loop(0, HB, add)

    def stage_three(i):
        @pl.when(owned)
        def _():
            loop(1, B, lambda k: two_arrival(i, next_batch(k)).wait_recv())
            r.u[i][me] = r.t[i][me - side * HB]
            total = r.u[i][0].astype(f32)
            for b in range(1, B):
                total = total + r.u[i][b].astype(f32)
            r.z[i][pair] = total.astype(r.z[i].dtype)
            for k, target in enumerate(others):
                three_copy(i, k, pair, target).start()

    def stage_four(i):
        @pl.when(jnp.logical_not(owned))
        def _():
            three_copy(i, 0, pair, hh).wait_recv()

        three_copy(i, 0, 1 - pair, hh).wait_recv()

    def small_one(j, half, target):
        return to_height(r.sp[j].at[half], r.sr[j], r.s_smallsend.at[j], r.s_smallrecv.at[j], target)

    def small_two(j, k):
        slot = r.su[j].at[me]
        return to_batch(slot, slot, r.s_smalltwo.at[j, k], r.s_smalltwor.at[j, me], next_batch(k))

    def small_two_arrival(j, k):
        b = next_batch(k)
        slot = r.su[j].at[b]
        return to_batch(slot, slot, r.s_smalltwo.at[j, k], r.s_smalltwor.at[j, b], b)

    def small_three(j, k, which, target):
        slot = r.sz[j].at[which]
        return to_height(slot, slot, r.s_smallthree.at[j, k], r.s_smallthreer.at[j, which], target)

    def small_stage_one(j):
        small_one(j, 1 - side, twin).start()

    def small_stage_two(j):
        small_one(j, side, hh).wait_recv()
        r.su[j][me] = (r.sp[j][side] + r.sr[j][...]).astype(r.su[j].dtype)
        loop(1, B, lambda k: small_two(j, k).start())

    def small_stage_three(j):
        loop(1, B, lambda k: small_two_arrival(j, k).wait_recv())
        total = r.su[j][0].astype(f32)
        for b in range(1, B):
            total = total + r.su[j][b].astype(f32)
        r.sz[j][hh] = total
        for k, target in enumerate(others):
            small_three(j, k, hh, target).start()

    def small_stage_four(j):
        for other in others:
            small_three(j, 0, other, hh).wait_recv()

    stage_one(1)

    dkv = r.dkv
    y_lane = jnp.where(lane < 64, y_at + 2 * (KR - 1) - lane, x_at + 2 * (KC - 1) - (lane - 64))
    back_at = y_lane // 2
    back_ok = (y_lane >= 0) & (y_lane % 2 == 0) & (back_at < jnp.where(lane < 64, KR, KC))
    back_spot = jnp.where(back_ok, back_at + jnp.where(lane < 64, 64, 64 + KR), 0)
    back_ok = back_ok.astype(f32)

    def key_rows_of(ref, n, h):
        return ref.at[n, pl.ds(pl.multiple_of(h * (KL * KCP), KL * KCP), KROWS), :]

    def dkv_one(n, k, h, target):
        return to_height(key_rows_of(dkv, n, h), r.dkvr.at[k, n], r.s_dsend.at[n, k], r.s_drecv.at[n, k], target)

    def dkv_two(n, target):
        return to_height(r.dkvs.at[n], r.dkvr.at[2, n], r.s_dsend.at[n, 2], r.s_drecv.at[n, 2], target)

    def dkv_on(n):
        dkv_one(n, 0, across, hh).wait_recv()
        r.dkvs[n] = (key_rows_of(dkv, n, across)[...].astype(f32) + r.dkvr[0, n].astype(f32)).astype(bf16)
        dkv_two(n, across).start()

    def attention_back(n):
        value = r.va[n]
        keys = r.ka[n].T
        mixed_grad = r.mg[n].astype(f32)
        query = r.qh[n].astype(f32)
        head = iota((T, D), 1) < HD
        probs_half, grads_half, dq, along = [], [], [], []
        mixed_heads = [jnp.where(head, mixed_grad, 0.0), jnp.where(head, 0.0, mixed_grad)]
        mixed_heads = [x.astype(bf16) for x in mixed_heads]
        query_heads = [jnp.where(head, query, 0.0), jnp.where(head, 0.0, query)]
        query_heads = [x.astype(bf16) for x in query_heads]
        key_grad, value_grad = 0.0, 0.0
        for hd in range(2):
            prob = probs[n, hd]
            prob_grad = nt(value, mixed_heads[hd])
            inner = jnp.sum(prob * prob_grad, axis=0, keepdims=True)
            score_grad = (prob * (prob_grad - inner)).astype(bf16)
            value_grad = value_grad + nn(prob.astype(bf16), mixed_heads[hd])
            key_grad = key_grad + nn(score_grad, query_heads[hd])
            back = nn(jnp.concatenate([keys[HD * hd : HD * (hd + 1)], keys[D : D + 32]], axis=0), score_grad)
            dq.append(back[:HD])
            along.append(back[HD:])
        dkv[n, 0:KEYS, :D] = (key_grad * SCALE).astype(bf16)
        dkv[n, 0:KEYS, D:] = value_grad.astype(bf16)
        dkv[n, KEYS:, :] = jnp.zeros((dkv.shape[1] - KEYS, 2 * D), bf16)
        dkv_one(n, 0, corner, twin).start()
        dkv_one(n, 1, twin, twin).start()
        back = jnp.concatenate(dq + along, axis=0).T
        right = back[:, 128:]
        apart = []
        for hd in range(2):
            apart.append(
                jnp.take_along_axis(right, back_spot + 32 * hd, axis=1, mode="promise_in_bounds") * back_ok
            )
        apart = halves(jnp.concatenate(apart, axis=1), 1)
        r.dr[n] = apart
        from_tables = nn(apart, jnp.concatenate([table[...], table[...]], axis=0))
        dqx[n, R : R + T, :] = back[:, :D] * SCALE + from_tables + mixed_grad
        outer = nn(edges, dqx[n, R : R + T, :].astype(bf16)).astype(bf16)
        r.dqs[0, n] = outer[:HX]
        r.dqs[1, n] = outer[HX:]

        @pl.when(n == 0)
        def _():
            stage_two(1)

        @pl.when(n > 0)
        def _():
            dkv_on(n - 1)

    loop(0, IMG, attention_back)
    back_up = to_height(r.dqs.at[0], r.dqr.at[1], r.s_qsend.at[0], r.s_qrecv.at[0], above)
    back_down = to_height(r.dqs.at[1], r.dqr.at[0], r.s_qsend.at[1], r.s_qrecv.at[1], below)
    back_up.start()
    back_down.start()

    both = tn(flat(r.qh), flat(r.dr))
    rel = (
        both[:HD, 0:128] + both[:HD, 256:384] + both[HD:, 128:256] + both[HD:, 384:512]
    )
    rel = jnp.concatenate([rel, jnp.zeros((128 - HD, 128), f32)], axis=0).T
    dkv_on(IMG - 1)
    early = r.early
    early[...] = jnp.zeros_like(early)
    early[0:48, 0:128] = rel[0:48]
    early[0:48, 128:256] = rel[48:96]
    early[0:32, 256:384] = rel[96:128]
    for i, piece in enumerate((acc[0:1, 2 * D : 3 * D], acc[0:1, 3 * D :], acc[1:2, 0:D], acc[1:2, D : 2 * D])):
        early[48 + i : 49 + i, D:] = piece
    early[58:59, :] = acc[2:3, : 2 * D]
    early[59:60, :] = acc[2:3, 2 * D :]

    has_above = (hh > 0).astype(f32)
    has_below = (hh < HG - 1).astype(f32)
    back_up.wait_recv()
    back_down.wait_recv()

    def queries_back(n):
        edge = jnp.concatenate([r.dqr[0, n].astype(f32) * has_above, r.dqr[1, n].astype(f32) * has_below], axis=0)
        edge = nn(r.spread[:, : 2 * HX], edge.astype(bf16))
        nothing = jnp.zeros((R, D), f32)
        field = dqx[n]
        whole = field[R : R + T]
        later = jnp.concatenate([nothing, rolled(whole, -1) * inner_low + edge * (1.0 - inner_low), nothing], axis=0)
        sooner = jnp.concatenate([nothing, rolled(whole, 1) * inner_top + edge * (1.0 - inner_top), nothing], axis=0)
        own = qx[n, R : R + T, :]
        total = 0.0
        for a, moved in enumerate((later, field, sooner)):
            for b in range(3):
                here = moved[R * (2 - b) : R * (2 - b) + T]
                total = total + poolq[3 * a + b : 3 * a + b + 1, :] * here
                paccq[3 * a + b] += folded(here * own)
        r.pq[n] = (total * cell_mask(n)).astype(bf16)

    loop(0, IMG, queries_back)
    r.f_q[...] = tn(flat(r.ne), flat(r.pq))
    for b in range(B):
        r.d[2][b] = r.f_q[rows * b : rows * (b + 1), :].astype(bf16)
    stage_one(2)
    for t in range(9):
        early[48 + t : 49 + t, 0:D] = jnp.sum(paccq[t], axis=0, keepdims=True)
    early[57:58, 0:D] = nn(ones, flat(r.pq))[0:1]
    for k in range(2):
        r.sp[0][k] = early[32 * k : 32 * (k + 1), :]
    small_stage_one(0)

    def keys_values_back(n):
        dkv_one(n, 1, hh, hh).wait_recv()
        dkv_two(n, hh).wait_recv()
        total = key_rows_of(dkv, n, hh)[...].astype(f32) + r.dkvr[1, n].astype(f32) + r.dkvr[2, n].astype(f32)
        wide = nn(r.unpick[...], halves(total, 0))
        taps = [wide[T // 2 * a : T // 2 * (a + 1)] for a in range(3)]
        field = kvx[n]
        sides = [columns(field, b) for b in range(3)]
        even, odd, late = 0.0, 0.0, 0.0
        for a in range(3):
            even = even + poolkv[3 * a + 1 : 3 * a + 2, :] * taps[a]
            odd = odd + poolkv[3 * a + 2 : 3 * a + 3, :] * taps[a]
            late = late + poolkv[3 * a : 3 * a + 1, :] * taps[a]
            for b in range(3):
                pacckv[3 * a + b] += folded(sides[b] * taps[a])
        odd = odd + jnp.concatenate([late[R:], jnp.zeros((R, 2 * D), f32)], axis=0)
        pairs = [x.reshape(KC, R, 2 * D) for x in (even, odd)]
        result = jnp.concatenate(pairs, axis=1).reshape(T, 2 * D)
        r.pkv[n] = (result * cell_mask(n)).astype(bf16)

    loop(0, IMG, keys_values_back)

    r.f_kv[...] = tn(flat(r.ne), flat(r.pkv))
    for b in range(B):
        r.d[0][b] = r.f_kv[rows * b : rows * (b + 1), :].astype(bf16)
    stage_one(0)
    stage_two(2)
    small_stage_two(0)

    def projection_back(n):
        grad = nt(r.pq[n], wq[...]) + nt(r.pkv[n], wkv[...])
        hat = r.hat_one[n]
        acc[0:1, 0:D] += jnp.sum(grad * hat, axis=0, keepdims=True)
        acc[0:1, D : 2 * D] += jnp.sum(grad, axis=0, keepdims=True)
        r.v_ig[n] = r.mgd[n] + normalise_back(grad, gain_one, hat, r.inv_one[n])

        @pl.when(n == 0)
        def _():
            stage_two(0)

    loop(0, IMG, projection_back)
    input_out = pltpu.make_async_copy(r.v_ig, r.o_ig, r.s_out.at[1])
    input_out.start()

    late = r.late
    late[...] = jnp.zeros_like(late)
    for t in range(9):
        late[t : t + 1, :] = jnp.sum(pacckv[t], axis=0, keepdims=True)
    late[9:10, :] = nn(ones, flat(r.pkv))[0:1]
    late[10:11, :] = acc[0:1, 0 : 2 * D]
    for k in range(2):
        r.sp[1][k] = late[8 * k : 8 * (k + 1), :]
    small_stage_one(1)
    stage_three(1)
    small_stage_two(1)
    stage_three(2)
    small_stage_three(0)
    stage_three(0)
    small_stage_three(1)
    for i in (1, 2, 0):
        stage_four(i)
    for j in range(2):
        small_stage_four(j)
    outs = list(zip(r.z, r.o_z)) + list(zip(r.sz, r.o_sz))
    outs = [pltpu.make_async_copy(a, b, r.s_out.at[2 + k]) for k, (a, b) in enumerate(outs)]
    for out in outs:
        out.start()

    for copy in (halo_up, halo_down, back_up, back_down, rest_handed(side, twin)):
        copy.wait_send()

    def sent_weights(k):
        in_copy(k).wait_send()
        rest_copy(k).wait_send()
        for j in range(2):
            small_two(j, k).wait_send()

    loop(1, B, sent_weights)

    def sent_images(n):
        kv_copy(n, 0, hh, twin).wait_send()
        kv_copy(n, 1, hh, across).wait_send()
        kv_copy(n, 2, across, twin).wait_send()
        dkv_one(n, 0, corner, twin).wait_send()
        dkv_one(n, 1, twin, twin).wait_send()
        dkv_two(n, across).wait_send()

    loop(0, IMG, sent_images)
    for i in range(3):
        one_copy(i, 1 - side, twin).wait_send()
    for j in range(2):
        small_one(j, 1 - side, twin).wait_send()
        for k, target in enumerate(others):
            small_three(j, k, hh, target).wait_send()

    def sent_two(j):
        @pl.when(side * HB + j != me)
        def _():
            for i in range(3):
                two_copy(i, j, side * HB + j).wait_send()

    loop(0, HB, sent_two)

    @pl.when(owned)
    def _():
        for i in range(3):
            for k, target in enumerate(others):
                three_copy(i, k, pair, target).wait_send()

    result_out.wait()
    input_out.wait()
    for out in outs:
        out.wait()


def adam_step(weight, first_state, second_state, gradient, step_rate, decay_rate):
    moment = beta_one * first_state + (1.0 - beta_one) * gradient
    square = beta_two * second_state + (1.0 - beta_two) * gradient * gradient
    unbiased = moment * (1.0 / (1.0 - beta_one**STEP))
    scaled = square * (1.0 / (1.0 - beta_two**STEP))
    updated = weight * (1.0 - step_rate * decay_rate) - step_rate * unbiased / (jnp.sqrt(scaled) + adam_eps)
    return (updated, moment, square)


def adam_kernel(tree, *refs):
    r = types.SimpleNamespace(**jax.tree.unflatten(tree, refs))

    def row(ref):
        return ref.at[0] if ref.shape[0] == 1 and len(ref.shape) == 2 else ref

    arrivals = []
    for index, (source, target) in enumerate(zip(r.given, r.v_given)):
        arrivals.append(pltpu.make_async_copy(source, row(target), r.s_in.at[index]))
        arrivals[-1].start()
    through = [(r.ig, r.v_ig, r.o_ig), (r.res, r.v_res, r.o_res)]
    through = [
        (pltpu.make_async_copy(a, b, r.s_through.at[k]), pltpu.make_async_copy(b, c, r.s_through.at[2 + k]))
        for k, (a, b, c) in enumerate(through)
    ]
    for enter, _ in through:
        enter.start()
    for i in range(5):
        arrivals[i].wait()
    planes = [x[0].astype(f32) + x[1].astype(f32) for x in r.v_given[0:3]]
    early, late = [
        jnp.concatenate([x[0] + x[2], x[1] + x[3]], axis=0) for x in r.v_given[3:5]
    ]
    pack = planes[1]
    rel = jnp.concatenate([early[0:48, 0:128], early[0:48, 128:256], early[0:32, 256:384]], axis=0)
    for t in range(9):
        r.pgrad[t, 0:1, :] = early[48 + t : 49 + t, 0:D]
        r.pgrad[t, 1:2, :] = late[t : t + 1, 0:D]
        r.pgrad[t, 2:3, :] = late[t : t + 1, D:]
    bgrad = r.bgrad
    bgrad[0:1, 0:D] = late[10:11, D:]
    bgrad[0:1, D : 2 * D] = early[49:50, D:]
    bgrad[0:1, 2 * D : 3 * D] = early[57:58, 0:D]
    bgrad[0:1, 3 * D : 5 * D] = late[9:10, :]
    bgrad[0:1, 5 * D : 6 * D] = early[50:51, D:]
    bgrad[0:1, 6 * D : 8 * D] = early[58:59, :]
    bgrad[0:1, 8 * D : 10 * D] = early[59:60, :]
    bgrad[0:1, 10 * D :] = early[51:52, D:]
    given = [r.v_given[5 + 3 * index : 8 + 3 * index] for index in range(9)]
    gradients = [
        lambda: jnp.concatenate([planes[2], planes[0]], axis=1),
        lambda: jnp.concatenate([pack[:, HID:PH], pack[:, PH + 4 * D : PH + 5 * D - 128]], axis=1),
        lambda: pack[:, :HID],
        lambda: jnp.concatenate([pack[:, PH + D * i : PH + D * (i + 1)] for i in range(4)], axis=0),
        lambda: r.pgrad[...],
        lambda: rel[0 : given[5][0].shape[0], 0:HD],
        lambda: rel[64 : 64 + given[6][0].shape[0], 0:HD],
        lambda: jnp.concatenate([late[10:11, 0:D], early[48:49, D:]], axis=0),
        lambda: bgrad[...],
    ]
    leaving = []

    def leave(index):
        copy = pltpu.make_async_copy(row(r.v_fresh[index]), r.fresh[index], r.s_out.at[index])
        copy.start()
        leaving.append(copy)

    for index in range(9):
        for k in range(3):
            arrivals[5 + 3 * index + k].wait()
        weight, first, second = [x[...] for x in given[index]]
        fresh = adam_step(
            weight, first, second, gradients[index](), step_rates[index], decay_rates[index]
        )
        if index < 4:
            fresh += (fresh[0].astype(bf16),)
        at = 4 * min(index, 4) + 3 * max(index - 4, 0)
        for k, value in enumerate(fresh):
            r.v_fresh[at + k][...] = value
            leave(at + k)
        if index == 0:
            for enter, leave_again in through:
                enter.wait()
                leave_again.start()
                leaving.append(leave_again)
    for copy in leaving:
        copy.wait()


def shards(activations, cotangent, extent, *params):
    B = lax.axis_size("batch")
    assert lax.axis_size("height") == HG and activations.shape == (IMG, R, C, D)
    params = list(params)
    for k in range(12, 15):
        params[k] = params[k].transpose(1, 0, 2)
    weights = params[0::3]
    rows = weights[0].shape[0]
    HB = B // 2
    assert weights[3].shape[0] == 4 * rows

    def by_column(x):
        return x.transpose(0, 2, 1, 3).reshape(IMG, T, D)

    def like(x):
        return jax.ShapeDtypeStruct(x.shape, x.dtype)

    anywhere = pl.BlockSpec(memory_space=pl.ANY)
    vm, dma = pltpu.VMEM, pltpu.SemaphoreType.DMA

    def call(kernel, operands, results, scratch, specs, **kwargs):
        flat_operands, operand_tree = jax.tree.flatten(operands)
        flat_results, result_tree = jax.tree.flatten(results)
        whole, tree = jax.tree.flatten({**operands, **results, **scratch})
        order = {id(x): k for k, x in enumerate(flat_operands + flat_results + jax.tree.leaves(scratch))}
        places = [order[id(x)] for x in whole]

        def ordered(*refs):
            return kernel(tree, *[refs[k] for k in places])

        out = pl.pallas_call(
            ordered,
            out_shape=flat_results,
            in_specs=[specs.get(id(x), anywhere) for x in flat_operands],
            out_specs=[anywhere] * len(flat_results),
            scratch_shapes=jax.tree.leaves(scratch),
            **kwargs,
        )(*flat_operands)
        return jax.tree.unflatten(result_tree, out)

    operands = dict(
        act=by_column(activations),
        cot=by_column(cotangent),
        extent=extent.T,
        w_in=weights[0],
        w_out=weights[1],
        w_exp=weights[2],
        w_red=weights[3],
        pool=weights[4],
        relh=weights[5],
        relw=weights[6],
        gains=weights[7],
        biases=weights[8],
    )
    results = dict(
        o_res=jax.ShapeDtypeStruct((IMG, T, D), bf16),
        o_ig=jax.ShapeDtypeStruct((IMG, T, D), f32),
        o_z=[jax.ShapeDtypeStruct((2, rows, x), y) for x, y in ((2 * D, f32), (PE, bf16), (D, f32))],
        o_sz=[jax.ShapeDtypeStruct((HG, x, 2 * D), f32) for x in (32, 8)],
    )
    lanes = (2 * D, PE, D)
    scratch = dict(
        v_act=vm((IMG, T, D), bf16),
        v_cot=vm((IMG, T, D), bf16),
        v_in=vm(weights[0].shape, f32),
        v_out=vm(weights[1].shape, f32),
        v_exp=vm(weights[2].shape, f32),
        v_red=vm(weights[3].shape, f32),
        v_pool=vm(weights[4].shape, f32),
        v_relh=vm(weights[5].shape, f32),
        v_relw=vm(weights[6].shape, f32),
        v_gains=vm(weights[7].shape, f32),
        v_biases=vm((1,) + weights[8].shape, f32),
        gin=vm((B, rows, 3 * D), bf16),
        grest=vm((2, B, rows, PH), bf16),
        d=[vm((B, rows, x), bf16) for x in lanes],
        p=[vm((HB, rows, x), bf16) for x in lanes],
        t=[vm((HB, rows, x), bf16) for x in lanes],
        u=[vm((B, rows, x), bf16) for x in lanes],
        z=[vm(x.shape, x.dtype) for x in results["o_z"]],
        sp=[vm((2, x, 2 * D), f32) for x in (32, 8)],
        sr=[vm((x, 2 * D), f32) for x in (32, 8)],
        su=[vm((B, 32, 2 * D), bf16), vm((B, 8, 2 * D), f32)],
        sz=[vm(x.shape, x.dtype) for x in results["o_sz"]],
        early=vm((64, 2 * D), f32),
        late=vm((16, 2 * D), f32),
        f_q=vm((D, D), f32),
        f_kv=vm((D, 2 * D), f32),
        f_exp=vm((D, HID), f32),
        f_red=vm((HID, D), f32),
        f_out=vm((D, D), f32),
        wq=vm((D, D), bf16),
        wkv=vm((D, 2 * D), bf16),
        wout=vm((D, D), bf16),
        wexp=vm((D, HID), bf16),
        wred=vm((HID, D), bf16),
        poolq=vm((9, D), f32),
        poolkv=vm((9, 2 * D), f32),
        tablef=vm((256, D), f32),
        table=vm((256, D), bf16),
        hs=vm((2, IMG, HX, D), bf16),
        hr=vm((2, IMG, HX, D), bf16),
        nh=vm((2 * IMG * HX, D), bf16),
        halo_q=vm((2 * IMG * HX, D), f32),
        halo_kv=vm((IMG * HX, 2 * D), f32),
        spread=vm((T, 4 * HX), bf16),
        pick=vm((KL * KCP, T), bf16),
        unpick=vm((3 * T // 2, 2 * KROWS), bf16),
        hot=vm((KEYS, 64), bf16),
        acc=vm((3, HID), f32),
        paccq=vm((9, 8, D), f32),
        pacckv=vm((9, 8, 2 * D), f32),
        ne=vm((IMG, T, D), bf16),
        hat_one=vm((IMG, T, D), f32),
        inv_one=vm((IMG, T, 1), f32),
        kvx=vm((IMG, TX, 2 * D), f32),
        qx=vm((IMG, TX, D), f32),
        dqx=vm((IMG, TX, D), f32),
        kvg=vm((HG, IMG, KL * KCP, 2 * D), bf16),
        ka=vm((IMG, KEYS, 256), bf16),
        va=vm((IMG, KEYS, D), bf16),
        qp=vm((IMG, T, D), f32),
        qh=vm((IMG, T, D), bf16),
        qa=vm((IMG, 2, T, 256), bf16),
        probs=vm((IMG, 2, KEYS, T), f32),
        mxh=vm((IMG, T, D), bf16),
        sh=vm((IMG, T, D), bf16),
        ac=vm((IMG, T, HID), bf16),
        uh=vm((IMG, T, D), bf16),
        eg=vm((IMG, T, HID), bf16),
        mgd=vm((IMG, T, D), f32),
        ag=vm((IMG, T, D), bf16),
        mg=vm((IMG, T, D), bf16),
        v_res=vm((IMG, T, D), bf16),
        v_ig=vm((IMG, T, D), f32),
        dkv=vm((IMG, KEYS + KL * KCP, 2 * D), bf16),
        dkvr=vm((3, IMG, KROWS, 2 * D), bf16),
        dkvs=vm((IMG, KROWS, 2 * D), bf16),
        dqs=vm((2, IMG, HX, D), bf16),
        dqr=vm((2, IMG, HX, D), bf16),
        dr=vm((IMG, T, 512), bf16),
        pq=vm((IMG, T, D), bf16),
        pkv=vm((IMG, T, 2 * D), bf16),
        s_local=dma((11,)),
        s_out=dma((7,)),
        s_wsend=dma((2, B)),
        s_wrecv=dma((3, B)),
        s_hsend=dma((2,)),
        s_hrecv=dma((2,)),
        s_ksend=dma((IMG, 3)),
        s_krecv=dma((IMG, 3)),
        s_dsend=dma((IMG, 3)),
        s_drecv=dma((IMG, 3)),
        s_qsend=dma((2,)),
        s_qrecv=dma((2,)),
        s_onesend=dma((3,)),
        s_onerecv=dma((3,)),
        s_twosend=dma((3, HB)),
        s_tworecv=dma((3, B)),
        s_threesend=dma((3, 3)),
        s_threerecv=dma((3, 2)),
        s_smallsend=dma((2,)),
        s_smallrecv=dma((2,)),
        s_smalltwo=dma((2, B)),
        s_smalltwor=dma((2, B)),
        s_smallthree=dma((2, 3)),
        s_smallthreer=dma((2, HG)),
    )
    main = call(
        functools.partial(main_kernel, B),
        operands,
        results,
        scratch,
        {id(operands["extent"]): pl.BlockSpec(memory_space=pltpu.SMEM)},
        compiler_params=pltpu.CompilerParams(
            collective_id=0, has_side_effects=True, vmem_limit_bytes=60 * 1024 * 1024
        ),
        name="block",
    )
    given = main["o_z"] + main["o_sz"] + params
    fresh = []
    for index in range(9):
        fresh += [like(weights[index]) for _ in range(3)]
        if index < 4:
            fresh += [jax.ShapeDtypeStruct(weights[index].shape, bf16)]

    def room(x):
        return vm((1,) + x.shape if len(x.shape) == 1 else x.shape, x.dtype)

    fresh = call(
        adam_kernel,
        dict(given=given, res=main["o_res"], ig=main["o_ig"]),
        dict(fresh=fresh, o_res=like(main["o_res"]), o_ig=like(main["o_ig"])),
        dict(
            v_given=[room(x) for x in given],
            v_fresh=[room(x) for x in fresh],
            pgrad=vm(weights[4].shape, f32),
            bgrad=vm((1,) + weights[8].shape, f32),
            s_in=dma((len(given),)),
            s_out=dma((len(fresh),)),
            s_through=dma((4,)),
            v_res=vm((IMG, T, D), bf16),
            v_ig=vm((IMG, T, D), f32),
        ),
        {},
        name="adam",
    )
    res, ig, fresh = fresh["o_res"], fresh["o_ig"], fresh["fresh"]
    for k in range(16, 19):
        fresh[k] = fresh[k].transpose(1, 0, 2)

    def by_row(x):
        return x.reshape(IMG, C, R, D).transpose(0, 2, 1, 3)

    return (by_row(res), by_row(ig)) + tuple(fresh)


def solution(mesh):
    grid = P("batch", "height", None, None)
    rows = P("batch", None)
    in_specs = (grid, grid, rows) + (rows,) * 12 + (P(),) * 15
    out_specs = (grid, grid) + (rows,) * 16 + (P(),) * 15
    return jax.shard_map(shards, mesh=mesh, in_specs=in_specs, out_specs=out_specs, check_vma=False)
```

```python
import functools
import types

import jax
import jax.numpy as jnp
from jax import lax
from jax.experimental import pallas as pl
from jax.experimental.pallas import tpu as pltpu
from jax.sharding import PartitionSpec as P

STEP = 10
MESH = pl.DeviceIdType.MESH
f32 = jnp.float32
bf16 = jnp.bfloat16

norm_eps = 1e-06
beta_one = 0.9
beta_two = 0.999
adam_eps = 1e-08
masked_value = -1000000000.0
step_rates = (0.04, 0.04, 0.04, 0.04, 0.2, 0.1, 0.1, 0.5, 0.1)
decay_rates = (0.05, 0.05, 0.05, 0.05, 0.05, 0.05, 0.05, 0.0, 0.0)

IMG, R, C, D, HD, HID = 3, 8, 28, 192, 96, 768
T = R * C
TX = T + 2 * R
HG = 4
KR, KC, KCP = R * HG // 2, C // 2, 16
KL = R // 2
KEYS = KR * KCP
SCALE = HD ** (-0.5)
KROWS = (KL + 1) * KCP
HX = 32
PH = HID + 128
PE = 2 * PH


def nn(a, b):
    return lax.dot_general(a, b, (((1,), (0,)), ((), ())), preferred_element_type=f32)


def nt(a, b):
    return lax.dot_general(a, b, (((1,), (1,)), ((), ())), preferred_element_type=f32)


def tn(a, b):
    return lax.dot_general(a, b, (((0,), (0,)), ((), ())), preferred_element_type=f32)


def iota(shape, axis):
    return lax.broadcasted_iota(jnp.int32, shape, axis)


def rolled(x, by):
    return pltpu.roll(x, by % x.shape[0], 0)


def halves(x, axis):
    high = x.astype(bf16)
    return jnp.concatenate([high, (x - high.astype(f32)).astype(bf16)], axis=axis)


def normalise(x):
    mean = jnp.sum(x, axis=1, keepdims=True) * (1.0 / D)
    centered = x - mean
    inverse = lax.rsqrt(jnp.sum(centered * centered, axis=1, keepdims=True) * (1.0 / D) + norm_eps)
    return centered * inverse, inverse


def normalise_back(grad, gain, hat, inverse):
    scaled = grad * gain
    one = jnp.sum(scaled, axis=1, keepdims=True) * (1.0 / D)
    two = jnp.sum(scaled * hat, axis=1, keepdims=True) * (1.0 / D)
    return inverse * (scaled - one - hat * two)


def folded(x):
    return jnp.sum(x.reshape(x.shape[0] // 8, 8, x.shape[1]), axis=0)


def main_kernel(B, tree, *refs):
    r = types.SimpleNamespace(**jax.tree.unflatten(tree, refs))
    me = lax.axis_index("batch")
    hh = lax.axis_index("height")
    HB = B // 2
    rows = r.w_in.shape[0]
    side = lax.rem(hh, 2)
    pair = lax.div(hh, 2)
    twin = hh + 1 - 2 * side
    across = lax.rem(hh + 2, HG)
    corner = lax.rem(twin + 2, HG)

    def loop(first, last, body):
        def step(i, carry):
            body(i)
            return carry

        lax.fori_loop(first, last, step, 0)

    def next_batch(k):
        return lax.rem(me + k, B)

    def next_height(k):
        return lax.rem(hh + k, HG)

    local = [
        (r.act, r.v_act),
        (r.w_in, r.v_in),
        (r.w_out, r.v_out),
        (r.w_exp, r.v_exp),
        (r.w_red, r.v_red),
        (r.pool, r.v_pool),
        (r.relh, r.v_relh),
        (r.relw, r.v_relw),
        (r.gains, r.v_gains),
        (r.biases, r.v_biases.at[0]),
        (r.cot, r.v_cot),
    ]
    local = [pltpu.make_async_copy(a, b, r.s_local.at[k]) for k, (a, b) in enumerate(local)]
    for copy in local:
        copy.start()

    barrier = pltpu.get_barrier_semaphore()

    def greet_batch(k):
        pl.semaphore_signal(barrier, inc=1, device_id=(next_batch(k), hh), device_id_type=MESH)

    loop(1, B, greet_batch)
    for k in range(1, HG):
        pl.semaphore_signal(barrier, inc=1, device_id=(me, next_height(k)), device_id_type=MESH)

    def to_batch(src, dst, send, recv, b):
        return pltpu.make_async_remote_copy(
            src_ref=src, dst_ref=dst, send_sem=send, recv_sem=recv, device_id=(b, hh), device_id_type=MESH
        )

    def to_height(src, dst, send, recv, h):
        return pltpu.make_async_remote_copy(
            src_ref=src, dst_ref=dst, send_sem=send, recv_sem=recv, device_id=(me, h), device_id_type=MESH
        )

    def in_slot(i, b):
        return r.gkv.at[side, b] if i == 0 else r.gq_in.at[b]

    def in_copy(i, k):
        slot = in_slot(i, me)
        return to_batch(slot, slot, r.s_isend.at[i, k], r.s_irecv.at[i, me], next_batch(k))

    def in_arrival(i, k):
        b = next_batch(k)
        slot = in_slot(i, b)
        return to_batch(slot, slot, r.s_isend.at[i, k], r.s_irecv.at[i, b], b)

    def in_handed(half, target):
        slot = r.gkv.at[half]
        return to_height(slot, slot, r.s_hand.at[2], r.s_hand.at[3], target)

    def rest_copy(k):
        slot = r.grest.at[side, me]
        return to_batch(slot, slot, r.s_wsend.at[k], r.s_wrecv.at[me], next_batch(k))

    def rest_arrival(k):
        b = next_batch(k)
        slot = r.grest.at[side, b]
        return to_batch(slot, slot, r.s_wsend.at[k], r.s_wrecv.at[b], b)

    def rest_handed(half, target):
        slot = r.grest.at[half]
        return to_height(slot, slot, r.s_hand.at[0], r.s_hand.at[1], target)

    local[1].wait()
    r.gkv[side, me] = jnp.where(side == 0, r.v_in[:, D : 2 * D], r.v_in[:, 2 * D :]).astype(bf16)
    r.gq_in[me] = r.v_in[:, :D].astype(bf16)
    pl.semaphore_wait(barrier, B - 1 + HG - 1)
    loop(1, B, lambda k: in_copy(0, k).start())
    loop(1, B, lambda k: in_copy(1, k).start())

    edge_rows = iota((2 * HX, T), 0)
    edge_cols = iota((2 * HX, T), 1)
    edges = (edge_cols == (edge_rows % HX) * R + (edge_rows // HX) * (R - 1)).astype(bf16)
    local[0].wait()
    for n in range(IMG):
        outer = nn(edges, r.v_act[n]).astype(bf16)
        r.hs[0, n] = outer[:HX]
        r.hs[1, n] = outer[HX:]
    above, below = next_height(HG - 1), next_height(1)
    halo_up = to_height(r.hs.at[0], r.hr.at[1], r.s_hsend.at[0], r.s_hrecv.at[0], above)
    halo_down = to_height(r.hs.at[1], r.hr.at[0], r.s_hsend.at[1], r.s_hrecv.at[1], below)

    halo_up.start()
    halo_down.start()
    for k in (2, 3, 4):
        local[k].wait()
    spare = jnp.zeros((rows, PE - HID - 5 * D), f32)
    left = jnp.concatenate([r.v_exp[...], r.v_out[:, :128]], axis=1)
    blocks = [r.v_red[rows * i : rows * (i + 1)] for i in range(4)]
    right = jnp.concatenate(blocks + [r.v_out[:, 128:], spare], axis=1)
    r.grest[side, me] = jnp.where(side == 0, left, right).astype(bf16)
    loop(1, B, lambda k: rest_copy(k).start())

    for k in range(5, 11):
        local[k].wait()
    poolq, poolkv, table = r.poolq, r.poolkv, r.table
    poolq[...] = r.v_pool[:, 0, :]
    poolkv[:, :D] = r.v_pool[:, 1, :]
    poolkv[:, D:] = r.v_pool[:, 2, :]
    r.tablef[...] = jnp.zeros_like(r.tablef)
    relh_rows, relw_rows = r.v_relh.shape[0], r.v_relw.shape[0]
    for hd in range(2):
        r.tablef[128 * hd : 128 * hd + relh_rows, HD * hd : HD * (hd + 1)] = r.v_relh[...]
        r.tablef[128 * hd + 64 : 128 * hd + 64 + relw_rows, HD * hd : HD * (hd + 1)] = r.v_relw[...]
    table[...] = r.tablef[...].astype(bf16)
    shift_one = r.v_biases[0:1, 0:D]
    shift_two = r.v_biases[0:1, D : 2 * D]
    bias_q = r.v_biases[0:1, 2 * D : 3 * D]
    bias_kv = r.v_biases[0:1, 3 * D : 5 * D]
    bias_out = r.v_biases[0:1, 5 * D : 6 * D]
    bias_exp = r.v_biases[0:1, 6 * D : 6 * D + HID]
    bias_red = r.v_biases[0:1, 6 * D + HID : 7 * D + HID]
    gain_one = r.v_gains[0:1, :]
    gain_two = r.v_gains[1:2, :]
    acc, paccq, pacckv = r.acc, r.paccq, r.pacckv
    acc[...] = jnp.zeros_like(acc)
    paccq[...] = jnp.zeros_like(paccq)
    pacckv[...] = jnp.zeros_like(pacckv)
    kvx, qx, dqx = r.kvx, r.qx, r.dqx

    cell = iota((T, 1), 0)
    cell_y, cell_x = hh * R + cell % R, cell // R
    halo_at = iota((2 * IMG * HX, 1), 0)

    def cell_mask(n):
        return ((cell_y < r.extent[0, n]) & (cell_x < r.extent[1, n])).astype(f32)

    def first_norm(n):
        hat, inverse = normalise(r.v_act[n].astype(f32))
        r.ne[n] = (hat * gain_one + shift_one).astype(bf16)
        r.hat_one[n] = hat
        r.inv_one[n] = inverse
        kvx[n, 0:R, :] = jnp.zeros((R, 2 * D), f32)
        kvx[n, T + R :, :] = jnp.zeros((R, 2 * D), f32)
        for x in (qx, dqx):
            x[n, 0:R, :] = jnp.zeros((R, D), f32)
            x[n, T + R :, :] = jnp.zeros((R, D), f32)

    for n in range(IMG):
        first_norm(n)

    spread_rows = iota((T, 2 * HX), 0)
    spread_cols = iota((T, 2 * HX), 1)
    spread = (
        (spread_rows // R == spread_cols % HX) & (spread_rows % R == (spread_cols // HX) * (R - 1))
    ).astype(bf16)
    r.spread[...] = jnp.concatenate([spread, spread], axis=1)
    pick_rows = iota((KL * KCP, T // 2), 0)
    pick_cols = iota((KL * KCP, T // 2), 1)
    pick = (
        (pick_rows % KCP == pick_cols // R) & (pick_cols % R == 2 * (pick_rows // KCP))
    ).astype(bf16)
    r.pick[...] = jnp.concatenate([pick, pick], axis=1)
    back_rows = iota((3 * T // 2, KROWS), 0)
    back_cols = iota((3 * T // 2, KROWS), 1)
    back_tap, back_cell = back_rows // (T // 2), back_rows % (T // 2)
    unpick = (
        (back_cols % KCP == back_cell // R)
        & (back_cell % R == 2 * (back_cols // KCP) + back_tap - 1)
    ).astype(bf16)
    r.unpick[...] = jnp.concatenate([unpick, unpick], axis=1)
    key_rows = iota((KEYS, 64), 0)
    key_lane = iota((KEYS, 64), 1) % 32
    r.hot[...] = (
        (key_lane == key_rows // KCP) | (key_lane == KR + key_rows % KCP)
    ).astype(bf16)
    halo_up.wait_recv()
    halo_down.wait_recv()
    hat, _ = normalise(r.hr[...].reshape(2 * IMG * HX, D).astype(f32))
    r.nh[...] = (hat * gain_one + shift_one).astype(bf16)

    halo_y = jnp.where(halo_at < IMG * HX, hh * R - 1, hh * R + R)
    halo_image = halo_at // HX % IMG
    halo_ok = jnp.zeros((2 * IMG * HX, 1), jnp.bool_)
    for n in range(IMG):
        halo_ok = halo_ok | (
            (halo_image == n)
            & (halo_y >= 0)
            & (halo_y < r.extent[0, n])
            & (halo_at % HX < r.extent[1, n])
        )
    halo_ok = halo_ok.astype(f32)

    wq, wkv, wout, wexp, wred = r.wq, r.wkv, r.wout, r.wexp, r.wred

    loop(1, B, lambda k: in_arrival(0, k).wait_recv())
    in_handed(side, twin).start()
    in_handed(1 - side, hh).wait_recv()
    for b in range(B):
        for i in range(2):
            r.f_kv[rows * b : rows * (b + 1), D * i : D * (i + 1)] = r.gkv[i, b].astype(f32)
    wkv[...] = r.f_kv[...].astype(bf16)

    kvg = r.kvg

    def kv_copy(n, k, source, target):
        slot = kvg.at[source, n]
        return to_height(slot, slot, r.s_ksend.at[n, k], r.s_krecv.at[n, k], target)

    half = IMG * HX
    r.halo_kv[...] = (nn(r.nh[:half], wkv[...]) + bias_kv) * halo_ok[:half]

    def columns(x, b):
        pairs = x.reshape(TX // (2 * R), 2 * R, x.shape[1])
        side = pairs[b // 2 : b // 2 + KC, R * (b % 2) : R * (b % 2) + R]
        return side.reshape(T // 2, x.shape[1])

    def keys_values(n):
        kvx[n, R : R + T, :] = (nn(r.ne[n], wkv[...]) + bias_kv) * cell_mask(n)
        field = kvx[n]
        sides = [columns(field, b) for b in range(3)]
        sums = [sum(poolkv[3 * a + b : 3 * a + b + 1, :] * sides[b] for b in range(3)) for a in range(3)]
        pooled = rolled(sums[0], 1) * (iota((T // 2, 1), 0) % R > 0).astype(f32) + sums[1] + rolled(sums[2], -1)
        edge = r.halo_kv[pl.ds(pl.multiple_of(n * HX, HX), HX), :]
        edge = (
            poolkv[0:1, :] * rolled(edge, 1) + poolkv[1:2, :] * edge + poolkv[2:3, :] * rolled(edge, -1)
        )
        edge_pick = (iota((KCP, HX), 1) == 2 * iota((KCP, HX), 0)).astype(bf16)
        edge = nn(jnp.concatenate([edge_pick, edge_pick], axis=1), halves(edge, 0))
        whole = nn(r.pick[...], halves(pooled, 0))
        kvg[hh, n] = jnp.concatenate([whole[:KCP] + edge, whole[KCP:]], axis=0).astype(bf16)
        kv_copy(n, 1, hh, across).start()
        kv_copy(n, 0, hh, twin).start()

    for n in range(IMG):
        keys_values(n)

    loop(1, B, lambda k: in_arrival(1, k).wait_recv())
    for b in range(B):
        r.f_q[rows * b : rows * (b + 1), :] = r.gq_in[b].astype(f32)
    wq[...] = r.f_q[...].astype(bf16)
    qp, qa = r.qp, r.qa
    r.halo_q[...] = (nn(r.nh[...], wq[...]) + bias_q) * halo_ok
    lane = iota((T, 128), 1)
    y_at = hh * R + iota((T, 128), 0) % R
    x_at = iota((T, 128), 0) // R
    aux = lane % 32
    spot = jnp.where(aux < KR, y_at - 2 * aux + 2 * (KR - 1), 64 + x_at - 2 * (aux - KR) + 2 * (KC - 1))
    inner_top = (cell % R > 0).astype(f32)
    inner_low = (cell % R < R - 1).astype(f32)

    def beside(x):
        return [rolled(x, 1), x, rolled(x, -1)]

    def queries(n):
        qx[n, R : R + T, :] = (nn(r.ne[n], wq[...]) + bias_q) * cell_mask(n)
        field = qx[n]
        sums = [
            sum(poolq[3 * a + b : 3 * a + b + 1, :] * field[R * b : R * b + T] for b in range(3))
            for a in range(3)
        ]
        top = beside(r.halo_q[pl.ds(pl.multiple_of(n * HX, HX), HX), :])
        low = beside(r.halo_q[pl.ds(pl.multiple_of((IMG + n) * HX, HX), HX), :])
        top = sum(poolq[b : b + 1, :] * top[b] for b in range(3))
        low = sum(poolq[6 + b : 7 + b, :] * low[b] for b in range(3))
        edge = nn(r.spread[...], halves(jnp.concatenate([top, low], axis=0), 0))
        pooled = rolled(sums[0], 1) * inner_top + sums[1] + rolled(sums[2], -1) * inner_low + edge
        qp[n] = pooled
        query = pooled.astype(bf16)
        r.qh[n] = query
        along = nt(query, table[...])
        left, right = pooled[:, :128], pooled[:, 128:]
        right = jnp.concatenate([right, right], axis=1)
        for hd in range(2):
            near = along[:, 128 * hd : 128 * (hd + 1)]
            near = jnp.take_along_axis(near, spot, axis=1, mode="promise_in_bounds") * (HD**0.5)
            rest = near - near.astype(bf16).astype(f32)
            near = jnp.where(lane < 96, near, rest)
            if hd == 0:
                qa[n, hd, :, :128] = jnp.where(lane < HD, left, 0.0).astype(bf16)
                qa[n, hd, :, 128:] = jnp.where(lane < 64, 0.0, near).astype(bf16)
            else:
                qa[n, hd, :, :128] = jnp.where(lane < HD, 0.0, left).astype(bf16)
                qa[n, hd, :, 128:] = jnp.where(lane < 64, right, near).astype(bf16)

    for n in range(IMG):
        queries(n)

    def kv_on(n):
        kv_copy(n, 1, across, hh).wait_recv()
        kv_copy(n, 2, across, twin).start()

    for n in range(IMG):
        kv_on(n)

    key_at = iota((KEYS, 1), 0)
    probs, mxh = r.probs, r.mxh

    def attention(n):
        kv_copy(n, 0, twin, hh).wait_recv()
        kv_copy(n, 2, corner, hh).wait_recv()
        both = jnp.concatenate([kvg[s, n] for s in range(HG)], axis=0)
        r.ka[n, :, :D] = both[:, :D]
        r.ka[n, :, D:] = r.hot[...]
        r.va[n] = both[:, D:]
        valid = (2 * (key_at // KCP) < r.extent[0, n]) & (2 * (key_at % KCP) < r.extent[1, n])
        value = r.va[n].T
        mixed = []
        for hd in range(2):
            scores = nt(r.ka[n], qa[n, hd]) * SCALE
            scores = jnp.where(valid, scores, masked_value)
            raised = jnp.exp(scores - jnp.max(scores, axis=0, keepdims=True))
            prob = raised * (1.0 / jnp.sum(raised, axis=0, keepdims=True))
            probs[n, hd] = prob
            mixed.append(nn(value[HD * hd : HD * (hd + 1)], prob.astype(bf16)))
        mxh[n] = (jnp.concatenate(mixed, axis=0).T + qp[n]).astype(bf16)

    for n in range(IMG):
        attention(n)
        if n == 1:
            loop(1, B, lambda k: rest_arrival(k).wait_recv())
            rest_handed(side, twin).start()

    rest_handed(1 - side, hh).wait_recv()
    for b in range(B):
        one, two = r.grest[0, b].astype(f32), r.grest[1, b].astype(f32)
        r.f_exp[rows * b : rows * (b + 1), :] = one[:, :HID]
        for i in range(4):
            at = 4 * rows * b + rows * i
            r.f_red[at : at + rows, :] = two[:, D * i : D * (i + 1)]
        r.f_out[rows * b : rows * (b + 1), :128] = one[:, HID:]
        r.f_out[rows * b : rows * (b + 1), 128:] = two[:, 4 * D : 5 * D - 128]
    wout[...] = r.f_out[...].astype(bf16)
    wexp[...] = r.f_exp[...].astype(bf16)
    wred[...] = r.f_red[...].astype(bf16)

    def feed_forward(n):
        mask = cell_mask(n)
        middle = r.v_act[n].astype(f32) + nn(mxh[n], wout[...]) + bias_out
        hat, inverse = normalise(middle)
        second = (hat * gain_two + shift_two).astype(bf16)
        r.sh[n] = second
        expanded = nn(second, wexp[...]) + bias_exp
        half_erf = 0.5 + 0.5 * lax.erf(expanded * (0.5**0.5))
        activated = (expanded * half_erf).astype(bf16)
        slope = half_erf + expanded * jnp.exp(expanded * expanded * -0.5) * 0.3989422804014327
        r.ac[n] = activated
        r.v_res[n] = (mask * (middle + nn(activated, wred[...]) + bias_red)).astype(bf16)
        upstream = r.v_cot[n].astype(f32) * mask
        up_half = upstream.astype(bf16)
        r.uh[n] = up_half
        expanded_grad = (nt(up_half, wred[...]) * slope).astype(bf16)
        r.eg[n] = expanded_grad
        second_grad = nt(expanded_grad, wexp[...])
        acc[0:1, 2 * D : 3 * D] += jnp.sum(second_grad * hat, axis=0, keepdims=True)
        acc[0:1, 3 * D : 4 * D] += jnp.sum(second_grad, axis=0, keepdims=True)
        middle_grad = upstream + normalise_back(second_grad, gain_two, hat, inverse)
        r.mgd[n] = middle_grad
        attn_grad = middle_grad.astype(bf16)
        r.ag[n] = attn_grad
        r.mg[n] = nt(attn_grad, wout[...]).astype(bf16)

    for n in range(IMG):
        feed_forward(n)
    result_out = pltpu.make_async_copy(r.v_res, r.o_res, r.s_out.at[0])
    result_out.start()

    ones = jnp.ones((16, IMG * T), bf16)

    def flat(ref):
        return ref[...].reshape(IMG * T, ref.shape[-1])

    r.f_exp[...] = tn(flat(r.sh), flat(r.eg))
    acc[2:3, :] = nn(ones, flat(r.eg))[0:1]
    r.f_red[...] = tn(flat(r.uh), flat(r.ac)).T
    acc[1:2, D : 2 * D] = nn(ones, flat(r.uh))[0:1]
    r.f_out[...] = tn(flat(mxh), flat(r.ag))
    acc[1:2, 0:D] = nn(ones, flat(r.ag))[0:1]
    spare = jnp.zeros((rows, PE - HID - 5 * D), f32)
    for b in range(B):
        r.d[1][b, :, :HID] = r.f_exp[rows * b : rows * (b + 1), :].astype(bf16)
        out_rows = r.f_out[rows * b : rows * (b + 1), :]
        r.d[1][b, :, HID:PH] = out_rows[:, :128].astype(bf16)
        blocks = [r.f_red[rows * (4 * b + i) : rows * (4 * b + i + 1), :] for i in range(4)]
        r.d[1][b, :, PH:] = jnp.concatenate(blocks + [out_rows[:, 128:], spare], axis=1).astype(bf16)

    def one_copy(i, half, target):
        return to_height(
            r.d[i].at[pl.ds(half * HB, HB)], r.p[i], r.s_onesend.at[i], r.s_onerecv.at[i], target
        )

    def two_copy(i, j, b):
        return to_batch(r.t[i].at[j], r.u[i].at[me], r.s_twosend.at[i, j], r.s_tworecv.at[i, me], b)

    def two_arrival(i, b):
        return to_batch(r.t[i].at[0], r.u[i].at[b], r.s_twosend.at[i, 0], r.s_tworecv.at[i, b], b)

    def three_own(i):
        return pltpu.make_async_copy(r.z[i].at[pair], r.o_z[i].at[pair], r.s_three.at[i])

    def three_copy(i, k, which, target):
        return to_height(r.z[i].at[which], r.o_z[i].at[which], r.s_threesend.at[i, k], r.s_threerecv.at[i, which], target)

    others = (twin, across, corner)
    owned = lax.div(me, HB) == side

    def stage_one(i):
        one_copy(i, 1 - side, twin).start()

    def stage_two(i):
        one_copy(i, side, hh).wait_recv()

        def add(j):
            b = side * HB + j
            r.t[i][j] = (r.d[i][b].astype(f32) + r.p[i][j].astype(f32)).astype(bf16)

            @pl.when(b != me)
            def _():
                two_copy(i, j, b).start()

        loop(0, HB, add)

    def stage_three(i):
        @pl.when(owned)
        def _():
            loop(1, B, lambda k: two_arrival(i, next_batch(k)).wait_recv())
            r.u[i][me] = r.t[i][me - side * HB]
            total = r.u[i][0].astype(f32)
            for b in range(1, B):
                total = total + r.u[i][b].astype(f32)
            r.z[i][pair] = total.astype(r.z[i].dtype)
            for k, target in enumerate(others):
                three_copy(i, k, pair, target).start()
            three_own(i).start()

    def stage_four(i):
        @pl.when(jnp.logical_not(owned))
        def _():
            three_copy(i, 0, pair, hh).wait_recv()

        three_copy(i, 0, 1 - pair, hh).wait_recv()

    def early_one(k, part, target):
        return to_height(r.sp[0].at[part], r.sr[0].at[k - 1], r.s_earlysend.at[k - 1], r.s_earlyrecv.at[k - 1], target)

    def late_one(half, target):
        return to_height(r.sp[1].at[half], r.sr[1].at[0], r.s_late.at[0], r.s_late.at[1], target)

    def small_two(j, k):
        slot = r.su[j].at[me]
        return to_batch(slot, slot, r.s_smalltwo.at[j, k], r.s_smalltwor.at[j, me], next_batch(k))

    def small_two_arrival(j, k):
        b = next_batch(k)
        slot = r.su[j].at[b]
        return to_batch(slot, slot, r.s_smalltwo.at[j, k], r.s_smalltwor.at[j, b], b)

    def small_own(j):
        return pltpu.make_async_copy(r.sz[j].at[hh], r.o_sz[j].at[hh], r.s_smallown.at[j])

    def small_three(j, k, which, target):
        return to_height(r.sz[j].at[which], r.o_sz[j].at[which], r.s_smallthree.at[j, k], r.s_smallthreer.at[j, which], target)

    def small_stage_one(j):
        if j == 0:
            for k in range(1, HG):
                early_one(k, next_height(k), next_height(k)).start()
        else:
            late_one(1 - side, twin).start()

    def small_stage_one_sent(j):
        if j == 0:
            for k in range(1, HG):
                early_one(k, next_height(k), next_height(k)).wait_send()
        else:
            late_one(1 - side, twin).wait_send()

    def small_stage_two(j):
        if j == 0:
            total = r.sp[0][hh]
            for k in range(1, HG):
                early_one(k, hh, hh).wait_recv()
                total = total + r.sr[0][k - 1]
        else:
            late_one(side, hh).wait_recv()
            total = r.sp[1][side] + r.sr[1][0]
        r.su[j][me] = total.astype(bf16)
        loop(1, B, lambda k: small_two(j, k).start())

    def small_stage_three(j):
        loop(1, B, lambda k: small_two_arrival(j, k).wait_recv())
        total = r.su[j][0].astype(f32)
        for b in range(1, B):
            total = total + r.su[j][b].astype(f32)
        r.sz[j][hh] = total
        for k, target in enumerate(others):
            small_three(j, k, hh, target).start()
        small_own(j).start()

    def small_stage_four(j):
        for other in others:
            small_three(j, 0, other, hh).wait_recv()

    stage_one(1)

    dkv = r.dkv
    y_lane = jnp.where(lane < 64, y_at + 2 * (KR - 1) - lane, x_at + 2 * (KC - 1) - (lane - 64))
    back_at = y_lane // 2
    back_ok = (y_lane >= 0) & (y_lane % 2 == 0) & (back_at < jnp.where(lane < 64, KR, KC))
    back_spot = jnp.where(back_ok, back_at + jnp.where(lane < 64, 64, 64 + KR), 0)
    back_ok = back_ok.astype(f32)

    def key_rows_of(ref, n, h):
        return ref.at[n, pl.ds(pl.multiple_of(h * (KL * KCP), KL * KCP), KROWS), :]

    def dkv_one(n, k, h, target):
        return to_height(key_rows_of(dkv, n, h), r.dkvr.at[k, n], r.s_dsend.at[n, k], r.s_drecv.at[n, k], target)

    def dkv_two(n, target):
        return to_height(r.dkvs.at[n], r.dkvr.at[2, n], r.s_dsend.at[n, 2], r.s_drecv.at[n, 2], target)

    def dkv_on(n):
        dkv_one(n, 0, across, hh).wait_recv()
        r.dkvs[n] = (key_rows_of(dkv, n, across)[...].astype(f32) + r.dkvr[0, n].astype(f32)).astype(bf16)
        dkv_two(n, across).start()

    def halo_back(n, k, target):
        return to_height(
            r.dqs.at[k, n], r.dqr.at[1 - k, n], r.s_qsend.at[n, k], r.s_qrecv.at[n, 1 - k], target
        )

    head = iota((T, D), 1) < HD

    def heads(x):
        x = x.astype(f32)
        return [jnp.where(head, x, 0.0).astype(bf16), jnp.where(head, 0.0, x).astype(bf16)]

    def scores_back(n):
        value = r.va[n]
        mixed_heads, query_heads = heads(r.mg[n]), heads(r.qh[n])
        key_grad, value_grad = 0.0, 0.0
        for hd in range(2):
            prob = probs[n, hd]
            prob_grad = nt(value, mixed_heads[hd])
            inner = jnp.sum(prob * prob_grad, axis=0, keepdims=True)
            score_grad = (prob * (prob_grad - inner)).astype(bf16)
            r.sg[n, hd] = score_grad
            value_grad = value_grad + nn(prob.astype(bf16), mixed_heads[hd])
            key_grad = key_grad + nn(score_grad, query_heads[hd])
        dkv[n, 0:KEYS, :D] = (key_grad * SCALE).astype(bf16)
        dkv[n, 0:KEYS, D:] = value_grad.astype(bf16)
        dkv[n, KEYS:, :] = jnp.zeros((dkv.shape[1] - KEYS, 2 * D), bf16)
        dkv_one(n, 0, corner, twin).start()
        dkv_one(n, 1, twin, twin).start()

    def rows_back(n):
        keys = r.ka[n].T
        dq, along = [], []
        for hd in range(2):
            here = jnp.concatenate([keys[HD * hd : HD * (hd + 1)], keys[D : D + 32]], axis=0)
            back = nn(here, r.sg[n, hd])
            dq.append(back[:HD])
            along.append(back[HD:])
        back = jnp.concatenate(dq + along, axis=0).T
        right = back[:, 128:]
        apart = []
        for hd in range(2):
            apart.append(
                jnp.take_along_axis(right, back_spot + 32 * hd, axis=1, mode="promise_in_bounds") * back_ok
            )
        apart = halves(jnp.concatenate(apart, axis=1), 1)
        r.dr[n] = apart
        from_tables = nn(apart, jnp.concatenate([table[...], table[...]], axis=0))
        dqx[n, R : R + T, :] = back[:, :D] * SCALE + from_tables + r.mg[n].astype(f32)
        outer = nn(edges, dqx[n, R : R + T, :].astype(bf16)).astype(bf16)
        r.dqs[0, n] = outer[:HX]
        r.dqs[1, n] = outer[HX:]
        halo_back(n, 0, above).start()
        halo_back(n, 1, below).start()

    scores_back(0)
    scores_back(1)
    dkv_on(0)
    scores_back(2)
    dkv_on(1)
    stage_two(1)
    rows_back(0)
    rows_back(1)
    dkv_on(2)
    rows_back(2)

    both = tn(flat(r.qh), flat(r.dr))
    rel = (
        both[:HD, 0:128] + both[:HD, 256:384] + both[HD:, 128:256] + both[HD:, 384:512]
    )
    rel = jnp.concatenate([rel, jnp.zeros((128 - HD, 128), f32)], axis=0).T
    early = r.early
    early[...] = jnp.zeros_like(early)
    early[0:48, 0:128] = rel[0:48]
    early[0:48, 128:256] = rel[48:96]
    early[0:32, 256:384] = rel[96:128]
    early[48:49, :] = acc[0:1, 2 * D :]
    early[49:50, :] = acc[1:2, 0 : 2 * D]
    early[50:51, :] = acc[2:3, : 2 * D]
    early[51:52, :] = acc[2:3, 2 * D :]
    for k in range(HG):
        r.sp[0][k] = early[16 * k : 16 * (k + 1), :]
    small_stage_one(0)

    has_above = (hh > 0).astype(f32)
    has_below = (hh < HG - 1).astype(f32)

    def queries_back(n):
        halo_back(n, 0, below).wait_recv()
        halo_back(n, 1, above).wait_recv()
        edge = jnp.concatenate([r.dqr[0, n].astype(f32) * has_above, r.dqr[1, n].astype(f32) * has_below], axis=0)
        edge = nn(r.spread[:, : 2 * HX], edge.astype(bf16))
        nothing = jnp.zeros((R, D), f32)
        field = dqx[n]
        whole = field[R : R + T]
        later = jnp.concatenate([nothing, rolled(whole, -1) * inner_low + edge * (1.0 - inner_low), nothing], axis=0)
        sooner = jnp.concatenate([nothing, rolled(whole, 1) * inner_top + edge * (1.0 - inner_top), nothing], axis=0)
        own = qx[n, R : R + T, :]
        total = 0.0
        for a, moved in enumerate((later, field, sooner)):
            for b in range(3):
                here = moved[R * (2 - b) : R * (2 - b) + T]
                total = total + poolq[3 * a + b : 3 * a + b + 1, :] * here
                paccq[3 * a + b] += folded(here * own)
        r.pq[n] = (total * cell_mask(n)).astype(bf16)

    def keys_values_back(n):
        dkv_one(n, 1, hh, hh).wait_recv()
        dkv_two(n, hh).wait_recv()
        total = key_rows_of(dkv, n, hh)[...].astype(f32) + r.dkvr[1, n].astype(f32) + r.dkvr[2, n].astype(f32)
        wide = nn(r.unpick[...], halves(total, 0))
        taps = [wide[T // 2 * a : T // 2 * (a + 1)] for a in range(3)]
        field = kvx[n]
        sides = [columns(field, b) for b in range(3)]
        even, odd, late = 0.0, 0.0, 0.0
        for a in range(3):
            even = even + poolkv[3 * a + 1 : 3 * a + 2, :] * taps[a]
            odd = odd + poolkv[3 * a + 2 : 3 * a + 3, :] * taps[a]
            late = late + poolkv[3 * a : 3 * a + 1, :] * taps[a]
            for b in range(3):
                pacckv[3 * a + b] += folded(sides[b] * taps[a])
        odd = odd + jnp.concatenate([late[R:], jnp.zeros((R, 2 * D), f32)], axis=0)
        pairs = [x.reshape(KC, R, 2 * D) for x in (even, odd)]
        result = jnp.concatenate(pairs, axis=1).reshape(T, 2 * D)
        r.pkv[n] = (result * cell_mask(n)).astype(bf16)

    keys_values_back(0)
    for n in range(IMG):
        queries_back(n)
    r.f_q[...] = tn(flat(r.ne), flat(r.pq))
    for b in range(B):
        r.d[2][b] = r.f_q[rows * b : rows * (b + 1), :].astype(bf16)
    stage_one(2)
    keys_values_back(1)
    small_stage_two(0)
    for n in range(IMG):
        r.gq[n] = nt(r.pq[n], wq[...])
    stage_two(2)
    keys_values_back(2)

    r.f_kv[...] = tn(flat(r.ne), flat(r.pkv))
    for b in range(B):
        r.d[0][b] = r.f_kv[rows * b : rows * (b + 1), :].astype(bf16)
    stage_one(0)

    def projection_back(n):
        grad = r.gq[n] + nt(r.pkv[n], wkv[...])
        hat = r.hat_one[n]
        acc[0:1, 0:D] += jnp.sum(grad * hat, axis=0, keepdims=True)
        acc[0:1, D : 2 * D] += jnp.sum(grad, axis=0, keepdims=True)
        r.v_ig[n] = r.mgd[n] + normalise_back(grad, gain_one, hat, r.inv_one[n])

    projection_back(0)
    projection_back(1)
    stage_two(0)
    projection_back(2)
    input_out = pltpu.make_async_copy(r.v_ig, r.o_ig, r.s_out.at[1])
    input_out.start()

    late = r.late
    for t in range(9):
        late[t : t + 1, :] = jnp.sum(pacckv[t], axis=0, keepdims=True)
        late[11 + t // 2 : 12 + t // 2, D * (t % 2) : D * (t % 2 + 1)] = jnp.sum(paccq[t], axis=0, keepdims=True)
    late[9:10, :] = nn(ones, flat(r.pkv))[0:1]
    late[10:11, :] = acc[0:1, 0 : 2 * D]
    late[15:16, D:] = nn(ones, flat(r.pq))[0:1]
    for k in range(2):
        r.sp[1][k] = late[8 * k : 8 * (k + 1), :]
    small_stage_one(1)
    stage_three(1)
    small_stage_two(1)
    stage_three(2)
    small_stage_three(0)
    stage_three(0)
    small_stage_three(1)
    for i in (1, 2, 0):
        stage_four(i)
    for j in range(2):
        small_stage_four(j)

    for copy in (halo_up, halo_down, in_handed(side, twin), rest_handed(side, twin)):
        copy.wait_send()

    def sent_weights(k):
        in_copy(0, k).wait_send()
        in_copy(1, k).wait_send()
        rest_copy(k).wait_send()
        for j in range(2):
            small_two(j, k).wait_send()

    loop(1, B, sent_weights)

    def sent_images(n):
        kv_copy(n, 0, hh, twin).wait_send()
        kv_copy(n, 1, hh, across).wait_send()
        kv_copy(n, 2, across, twin).wait_send()
        dkv_one(n, 0, corner, twin).wait_send()
        dkv_one(n, 1, twin, twin).wait_send()
        dkv_two(n, across).wait_send()
        halo_back(n, 0, above).wait_send()
        halo_back(n, 1, below).wait_send()

    loop(0, IMG, sent_images)
    for i in range(3):
        one_copy(i, 1 - side, twin).wait_send()
    for j in range(2):
        small_stage_one_sent(j)
        small_own(j).wait()
        for k, target in enumerate(others):
            small_three(j, k, hh, target).wait_send()

    def sent_two(j):
        @pl.when(side * HB + j != me)
        def _():
            for i in range(3):
                two_copy(i, j, side * HB + j).wait_send()

    loop(0, HB, sent_two)

    @pl.when(owned)
    def _():
        for i in range(3):
            three_own(i).wait()
            for k, target in enumerate(others):
                three_copy(i, k, pair, target).wait_send()

    result_out.wait()
    input_out.wait()


def adam_step(weight, first_state, second_state, gradient, step_rate, decay_rate):
    moment = beta_one * first_state + (1.0 - beta_one) * gradient
    square = beta_two * second_state + (1.0 - beta_two) * gradient * gradient
    unbiased = moment * (1.0 / (1.0 - beta_one**STEP))
    scaled = square * (1.0 / (1.0 - beta_two**STEP))
    updated = weight * (1.0 - step_rate * decay_rate) - step_rate * unbiased / (jnp.sqrt(scaled) + adam_eps)
    return (updated, moment, square)


def adam_kernel(tree, *refs):
    r = types.SimpleNamespace(**jax.tree.unflatten(tree, refs))

    def row(ref):
        return ref.at[0] if ref.shape[0] == 1 and len(ref.shape) == 2 else ref

    arrivals = []
    for index, (source, target) in enumerate(zip(r.given, r.v_given)):
        arrivals.append(pltpu.make_async_copy(source, row(target), r.s_in.at[index]))
        arrivals[-1].start()
    through = [(r.ig, r.v_ig, r.o_ig), (r.res, r.v_res, r.o_res)]
    through = [
        (pltpu.make_async_copy(a, b, r.s_through.at[k]), pltpu.make_async_copy(b, c, r.s_through.at[2 + k]))
        for k, (a, b, c) in enumerate(through)
    ]
    for enter, _ in through:
        enter.start()
    for i in range(5):
        arrivals[i].wait()
    planes = [x[0].astype(f32) + x[1].astype(f32) for x in r.v_given[0:3]]
    early, late = r.v_given[3:5]
    early = jnp.concatenate([early[k] for k in range(HG)], axis=0)
    late = jnp.concatenate([late[0] + late[2], late[1] + late[3]], axis=0)
    pack = planes[1]
    rel = jnp.concatenate([early[0:48, 0:128], early[0:48, 128:256], early[0:32, 256:384]], axis=0)
    for t in range(9):
        r.pgrad[t, 0:1, :] = late[11 + t // 2 : 12 + t // 2, D * (t % 2) : D * (t % 2 + 1)]
        r.pgrad[t, 1:2, :] = late[t : t + 1, 0:D]
        r.pgrad[t, 2:3, :] = late[t : t + 1, D:]
    bgrad = r.bgrad
    bgrad[0:1, 0:D] = late[10:11, D:]
    bgrad[0:1, D : 2 * D] = early[48:49, D:]
    bgrad[0:1, 2 * D : 3 * D] = late[15:16, D:]
    bgrad[0:1, 3 * D : 5 * D] = late[9:10, :]
    bgrad[0:1, 5 * D : 6 * D] = early[49:50, 0:D]
    bgrad[0:1, 6 * D : 8 * D] = early[50:51, :]
    bgrad[0:1, 8 * D : 10 * D] = early[51:52, :]
    bgrad[0:1, 10 * D :] = early[49:50, D:]
    given = [r.v_given[5 + 3 * index : 8 + 3 * index] for index in range(9)]
    gradients = [
        lambda: jnp.concatenate([planes[2], planes[0]], axis=1),
        lambda: jnp.concatenate([pack[:, HID:PH], pack[:, PH + 4 * D : PH + 5 * D - 128]], axis=1),
        lambda: pack[:, :HID],
        lambda: jnp.concatenate([pack[:, PH + D * i : PH + D * (i + 1)] for i in range(4)], axis=0),
        lambda: r.pgrad[...],
        lambda: rel[0 : given[5][0].shape[0], 0:HD],
        lambda: rel[64 : 64 + given[6][0].shape[0], 0:HD],
        lambda: jnp.concatenate([late[10:11, 0:D], early[48:49, 0:D]], axis=0),
        lambda: bgrad[...],
    ]
    leaving = []

    def leave(index):
        copy = pltpu.make_async_copy(row(r.v_fresh[index]), r.fresh[index], r.s_out.at[index])
        copy.start()
        leaving.append(copy)

    for index in range(9):
        for k in range(3):
            arrivals[5 + 3 * index + k].wait()
        weight, first, second = [x[...] for x in given[index]]
        fresh = adam_step(
            weight, first, second, gradients[index](), step_rates[index], decay_rates[index]
        )
        if index < 4:
            fresh += (fresh[0].astype(bf16),)
        at = 4 * min(index, 4) + 3 * max(index - 4, 0)
        for k, value in enumerate(fresh):
            r.v_fresh[at + k][...] = value
            leave(at + k)
        if index == 0:
            for enter, leave_again in through:
                enter.wait()
                leave_again.start()
                leaving.append(leave_again)
    for copy in leaving:
        copy.wait()


def shards(activations, cotangent, extent, *params):
    B = lax.axis_size("batch")
    assert lax.axis_size("height") == HG and activations.shape == (IMG, R, C, D)
    params = list(params)
    for k in range(12, 15):
        params[k] = params[k].transpose(1, 0, 2)
    weights = params[0::3]
    rows = weights[0].shape[0]
    HB = B // 2
    assert weights[3].shape[0] == 4 * rows

    def by_column(x):
        return x.transpose(0, 2, 1, 3).reshape(IMG, T, D)

    def like(x):
        return jax.ShapeDtypeStruct(x.shape, x.dtype)

    anywhere = pl.BlockSpec(memory_space=pl.ANY)
    vm, dma = pltpu.VMEM, pltpu.SemaphoreType.DMA

    def call(kernel, operands, results, scratch, specs, **kwargs):
        flat_operands, operand_tree = jax.tree.flatten(operands)
        flat_results, result_tree = jax.tree.flatten(results)
        whole, tree = jax.tree.flatten({**operands, **results, **scratch})
        order = {id(x): k for k, x in enumerate(flat_operands + flat_results + jax.tree.leaves(scratch))}
        places = [order[id(x)] for x in whole]

        def ordered(*refs):
            return kernel(tree, *[refs[k] for k in places])

        out = pl.pallas_call(
            ordered,
            out_shape=flat_results,
            in_specs=[specs.get(id(x), anywhere) for x in flat_operands],
            out_specs=[anywhere] * len(flat_results),
            scratch_shapes=jax.tree.leaves(scratch),
            **kwargs,
        )(*flat_operands)
        return jax.tree.unflatten(result_tree, out)

    operands = dict(
        act=by_column(activations),
        cot=by_column(cotangent),
        extent=extent.T,
        w_in=weights[0],
        w_out=weights[1],
        w_exp=weights[2],
        w_red=weights[3],
        pool=weights[4],
        relh=weights[5],
        relw=weights[6],
        gains=weights[7],
        biases=weights[8],
    )
    results = dict(
        o_res=jax.ShapeDtypeStruct((IMG, T, D), bf16),
        o_ig=jax.ShapeDtypeStruct((IMG, T, D), f32),
        o_z=[jax.ShapeDtypeStruct((2, rows, x), y) for x, y in ((2 * D, f32), (PE, bf16), (D, f32))],
        o_sz=[jax.ShapeDtypeStruct((HG, x, 2 * D), f32) for x in (16, 8)],
    )
    lanes = (2 * D, PE, D)
    scratch = dict(
        v_act=vm((IMG, T, D), bf16),
        v_cot=vm((IMG, T, D), bf16),
        v_in=vm(weights[0].shape, f32),
        v_out=vm(weights[1].shape, f32),
        v_exp=vm(weights[2].shape, f32),
        v_red=vm(weights[3].shape, f32),
        v_pool=vm(weights[4].shape, f32),
        v_relh=vm(weights[5].shape, f32),
        v_relw=vm(weights[6].shape, f32),
        v_gains=vm(weights[7].shape, f32),
        v_biases=vm((1,) + weights[8].shape, f32),
        gkv=vm((2, B, rows, D), bf16),
        gq_in=vm((B, rows, D), bf16),
        grest=vm((2, B, rows, PH), bf16),
        d=[vm((B, rows, x), bf16) for x in lanes],
        p=[vm((HB, rows, x), bf16) for x in lanes],
        t=[vm((HB, rows, x), bf16) for x in lanes],
        u=[vm((B, rows, x), bf16) for x in lanes],
        z=[vm(x.shape, x.dtype) for x in results["o_z"]],
        sp=[vm((HG, 16, 2 * D), f32), vm((2, 8, 2 * D), f32)],
        sr=[vm((HG - 1, 16, 2 * D), f32), vm((1, 8, 2 * D), f32)],
        su=[vm((B, x, 2 * D), bf16) for x in (16, 8)],
        sz=[vm(x.shape, x.dtype) for x in results["o_sz"]],
        early=vm((64, 2 * D), f32),
        late=vm((16, 2 * D), f32),
        f_q=vm((D, D), f32),
        f_kv=vm((D, 2 * D), f32),
        f_exp=vm((D, HID), f32),
        f_red=vm((HID, D), f32),
        f_out=vm((D, D), f32),
        wq=vm((D, D), bf16),
        wkv=vm((D, 2 * D), bf16),
        wout=vm((D, D), bf16),
        wexp=vm((D, HID), bf16),
        wred=vm((HID, D), bf16),
        poolq=vm((9, D), f32),
        poolkv=vm((9, 2 * D), f32),
        tablef=vm((256, D), f32),
        table=vm((256, D), bf16),
        hs=vm((2, IMG, HX, D), bf16),
        hr=vm((2, IMG, HX, D), bf16),
        nh=vm((2 * IMG * HX, D), bf16),
        halo_q=vm((2 * IMG * HX, D), f32),
        halo_kv=vm((IMG * HX, 2 * D), f32),
        spread=vm((T, 4 * HX), bf16),
        pick=vm((KL * KCP, T), bf16),
        unpick=vm((3 * T // 2, 2 * KROWS), bf16),
        hot=vm((KEYS, 64), bf16),
        acc=vm((3, HID), f32),
        paccq=vm((9, 8, D), f32),
        pacckv=vm((9, 8, 2 * D), f32),
        ne=vm((IMG, T, D), bf16),
        hat_one=vm((IMG, T, D), f32),
        inv_one=vm((IMG, T, 1), f32),
        kvx=vm((IMG, TX, 2 * D), f32),
        qx=vm((IMG, TX, D), f32),
        dqx=vm((IMG, TX, D), f32),
        kvg=vm((HG, IMG, KL * KCP, 2 * D), bf16),
        ka=vm((IMG, KEYS, 256), bf16),
        va=vm((IMG, KEYS, D), bf16),
        qp=vm((IMG, T, D), f32),
        qh=vm((IMG, T, D), bf16),
        qa=vm((IMG, 2, T, 256), bf16),
        probs=vm((IMG, 2, KEYS, T), f32),
        sg=vm((IMG, 2, KEYS, T), bf16),
        mxh=vm((IMG, T, D), bf16),
        sh=vm((IMG, T, D), bf16),
        ac=vm((IMG, T, HID), bf16),
        uh=vm((IMG, T, D), bf16),
        eg=vm((IMG, T, HID), bf16),
        mgd=vm((IMG, T, D), f32),
        ag=vm((IMG, T, D), bf16),
        mg=vm((IMG, T, D), bf16),
        v_res=vm((IMG, T, D), bf16),
        v_ig=vm((IMG, T, D), f32),
        dkv=vm((IMG, KEYS + KL * KCP, 2 * D), bf16),
        dkvr=vm((3, IMG, KROWS, 2 * D), bf16),
        dkvs=vm((IMG, KROWS, 2 * D), bf16),
        dqs=vm((2, IMG, HX, D), bf16),
        dqr=vm((2, IMG, HX, D), bf16),
        dr=vm((IMG, T, 512), bf16),
        pq=vm((IMG, T, D), bf16),
        gq=vm((IMG, T, D), f32),
        pkv=vm((IMG, T, 2 * D), bf16),
        s_local=dma((11,)),
        s_out=dma((2,)),
        s_isend=dma((2, B)),
        s_irecv=dma((2, B)),
        s_wsend=dma((B,)),
        s_wrecv=dma((B,)),
        s_hand=dma((4,)),
        s_hsend=dma((2,)),
        s_hrecv=dma((2,)),
        s_ksend=dma((IMG, 3)),
        s_krecv=dma((IMG, 3)),
        s_dsend=dma((IMG, 3)),
        s_drecv=dma((IMG, 3)),
        s_qsend=dma((IMG, 2)),
        s_qrecv=dma((IMG, 2)),
        s_onesend=dma((3,)),
        s_onerecv=dma((3,)),
        s_twosend=dma((3, HB)),
        s_tworecv=dma((3, B)),
        s_three=dma((3,)),
        s_smallown=dma((2,)),
        s_threesend=dma((3, 3)),
        s_threerecv=dma((3, 2)),
        s_earlysend=dma((HG - 1,)),
        s_earlyrecv=dma((HG - 1,)),
        s_late=dma((2,)),
        s_smalltwo=dma((2, B)),
        s_smalltwor=dma((2, B)),
        s_smallthree=dma((2, 3)),
        s_smallthreer=dma((2, HG)),
    )
    main = call(
        functools.partial(main_kernel, B),
        operands,
        results,
        scratch,
        {id(operands["extent"]): pl.BlockSpec(memory_space=pltpu.SMEM)},
        compiler_params=pltpu.CompilerParams(
            collective_id=0, has_side_effects=True, vmem_limit_bytes=60 * 1024 * 1024
        ),
        name="block",
    )
    given = main["o_z"] + main["o_sz"] + params
    fresh = []
    for index in range(9):
        fresh += [like(weights[index]) for _ in range(3)]
        if index < 4:
            fresh += [jax.ShapeDtypeStruct(weights[index].shape, bf16)]

    def room(x):
        return vm((1,) + x.shape if len(x.shape) == 1 else x.shape, x.dtype)

    fresh = call(
        adam_kernel,
        dict(given=given, res=main["o_res"], ig=main["o_ig"]),
        dict(fresh=fresh, o_res=like(main["o_res"]), o_ig=like(main["o_ig"])),
        dict(
            v_given=[room(x) for x in given],
            v_fresh=[room(x) for x in fresh],
            pgrad=vm(weights[4].shape, f32),
            bgrad=vm((1,) + weights[8].shape, f32),
            s_in=dma((len(given),)),
            s_out=dma((len(fresh),)),
            s_through=dma((4,)),
            v_res=vm((IMG, T, D), bf16),
            v_ig=vm((IMG, T, D), f32),
        ),
        {},
        name="adam",
    )
    res, ig, fresh = fresh["o_res"], fresh["o_ig"], fresh["fresh"]
    for k in range(16, 19):
        fresh[k] = fresh[k].transpose(1, 0, 2)

    def by_row(x):
        return x.reshape(IMG, C, R, D).transpose(0, 2, 1, 3)

    return (by_row(res), by_row(ig)) + tuple(fresh)


def solution(mesh):
    grid = P("batch", "height", None, None)
    rows = P("batch", None)
    in_specs = (grid, grid, rows) + (rows,) * 12 + (P(),) * 15
    out_specs = (grid, grid) + (rows,) * 16 + (P(),) * 15
    return jax.shard_map(shards, mesh=mesh, in_specs=in_specs, out_specs=out_specs, check_vma=False)
```

```python
import functools
import types

import jax
import jax.numpy as jnp
from jax import lax
from jax.experimental import pallas as pl
from jax.experimental.pallas import tpu as pltpu
from jax.sharding import PartitionSpec as P

STEP = 10
MESH = pl.DeviceIdType.MESH
f32 = jnp.float32
bf16 = jnp.bfloat16

norm_eps = 1e-06
beta_one = 0.9
beta_two = 0.999
adam_eps = 1e-08
masked_value = -1000000000.0
step_rates = (0.04, 0.04, 0.04, 0.04, 0.2, 0.1, 0.1, 0.5, 0.1)
decay_rates = (0.05, 0.05, 0.05, 0.05, 0.05, 0.05, 0.05, 0.0, 0.0)

IMG, R, C, D, HD, HID = 3, 8, 28, 192, 96, 768
T = R * C
TX = T + 2 * R
HG = 4
KR, KC, KCP = R * HG // 2, C // 2, 16
KL = R // 2
KEYS = KR * KCP
SCALE = HD ** (-0.5)
KROWS = (KL + 1) * KCP
HX = 32
PH = HID + 128
PE = 2 * PH


def nn(a, b):
    return lax.dot_general(a, b, (((1,), (0,)), ((), ())), preferred_element_type=f32)


def nt(a, b):
    return lax.dot_general(a, b, (((1,), (1,)), ((), ())), preferred_element_type=f32)


def tn(a, b):
    return lax.dot_general(a, b, (((0,), (0,)), ((), ())), preferred_element_type=f32)


def iota(shape, axis):
    return lax.broadcasted_iota(jnp.int32, shape, axis)


def rolled(x, by):
    return pltpu.roll(x, by % x.shape[0], 0)


def halves(x, axis):
    high = x.astype(bf16)
    return jnp.concatenate([high, (x - high.astype(f32)).astype(bf16)], axis=axis)


def normalise(x):
    mean = jnp.sum(x, axis=1, keepdims=True) * (1.0 / D)
    centered = x - mean
    inverse = lax.rsqrt(jnp.sum(centered * centered, axis=1, keepdims=True) * (1.0 / D) + norm_eps)
    return centered * inverse, inverse


def normalise_back(grad, gain, hat, inverse):
    scaled = grad * gain
    one = jnp.sum(scaled, axis=1, keepdims=True) * (1.0 / D)
    two = jnp.sum(scaled * hat, axis=1, keepdims=True) * (1.0 / D)
    return inverse * (scaled - one - hat * two)


def folded(x):
    return jnp.sum(x.reshape(x.shape[0] // 8, 8, x.shape[1]), axis=0)


def main_kernel(B, tree, *refs):
    r = types.SimpleNamespace(**jax.tree.unflatten(tree, refs))
    me = lax.axis_index("batch")
    hh = lax.axis_index("height")
    HB = B // 2
    rows = r.w_in.shape[0]
    side = lax.rem(hh, 2)
    pair = lax.div(hh, 2)
    twin = hh + 1 - 2 * side
    across = lax.rem(hh + 2, HG)
    corner = lax.rem(twin + 2, HG)

    def loop(first, last, body):
        if last - first < 8:
            for i in range(first, last):
                body(i)
            return

        def step(i, carry):
            body(i)
            return carry

        lax.fori_loop(first, last, step, 0)

    def next_batch(k):
        return lax.rem(me + k, B)

    def next_height(k):
        return lax.rem(hh + k, HG)

    local = [
        (r.act, r.v_act),
        (r.w_in, r.v_in),
        (r.w_out, r.v_out),
        (r.w_exp, r.v_exp),
        (r.w_red, r.v_red),
        (r.pool, r.v_pool),
        (r.relh, r.v_relh),
        (r.relw, r.v_relw),
        (r.gains, r.v_gains),
        (r.biases, r.v_biases.at[0]),
        (r.cot, r.v_cot),
    ]
    local = [pltpu.make_async_copy(a, b, r.s_local.at[k]) for k, (a, b) in enumerate(local)]
    for copy in local:
        copy.start()

    barrier = pltpu.get_barrier_semaphore()

    def greet_batch(k):
        pl.semaphore_signal(barrier, inc=1, device_id=(next_batch(k), hh), device_id_type=MESH)

    loop(1, B, greet_batch)
    for k in range(1, HG):
        pl.semaphore_signal(barrier, inc=1, device_id=(me, next_height(k)), device_id_type=MESH)

    def to_batch(src, dst, send, recv, b):
        return pltpu.make_async_remote_copy(
            src_ref=src, dst_ref=dst, send_sem=send, recv_sem=recv, device_id=(b, hh), device_id_type=MESH
        )

    def to_height(src, dst, send, recv, h):
        return pltpu.make_async_remote_copy(
            src_ref=src, dst_ref=dst, send_sem=send, recv_sem=recv, device_id=(me, h), device_id_type=MESH
        )

    def in_slot(i, b):
        return r.gkv.at[side, b] if i == 0 else r.gq_in.at[b]

    def in_copy(i, k):
        slot = in_slot(i, me)
        return to_batch(slot, slot, r.s_isend.at[i, k], r.s_irecv.at[i, me], next_batch(k))

    def in_arrival(i, k):
        b = next_batch(k)
        slot = in_slot(i, b)
        return to_batch(slot, slot, r.s_isend.at[i, k], r.s_irecv.at[i, b], b)

    def in_handed(half, target):
        slot = r.gkv.at[half]
        return to_height(slot, slot, r.s_hand.at[2], r.s_hand.at[3], target)

    def rest_copy(k):
        slot = r.grest.at[side, me]
        return to_batch(slot, slot, r.s_wsend.at[k], r.s_wrecv.at[me], next_batch(k))

    def rest_arrival(k):
        b = next_batch(k)
        slot = r.grest.at[side, b]
        return to_batch(slot, slot, r.s_wsend.at[k], r.s_wrecv.at[b], b)

    def rest_handed(half, target):
        slot = r.grest.at[half]
        return to_height(slot, slot, r.s_hand.at[0], r.s_hand.at[1], target)

    local[1].wait()
    r.gkv[side, me] = jnp.where(side == 0, r.v_in[:, D : 2 * D], r.v_in[:, 2 * D :]).astype(bf16)
    r.gq_in[me] = r.v_in[:, :D].astype(bf16)
    pl.semaphore_wait(barrier, B - 1 + HG - 1)
    loop(1, B, lambda k: in_copy(0, k).start())
    loop(1, B, lambda k: in_copy(1, k).start())

    edge_rows = iota((2 * HX, T), 0)
    edge_cols = iota((2 * HX, T), 1)
    edges = (edge_cols == (edge_rows % HX) * R + (edge_rows // HX) * (R - 1)).astype(bf16)
    local[0].wait()
    for n in range(IMG):
        outer = nn(edges, r.v_act[n]).astype(bf16)
        r.hs[0, n] = outer[:HX]
        r.hs[1, n] = outer[HX:]
    above, below = next_height(HG - 1), next_height(1)
    halo_up = to_height(r.hs.at[0], r.hr.at[1], r.s_hsend.at[0], r.s_hrecv.at[0], above)
    halo_down = to_height(r.hs.at[1], r.hr.at[0], r.s_hsend.at[1], r.s_hrecv.at[1], below)

    halo_up.start()
    halo_down.start()
    for k in (2, 3, 4):
        local[k].wait()
    spare = jnp.zeros((rows, PE - HID - 5 * D), f32)
    left = jnp.concatenate([r.v_exp[...], r.v_out[:, :128]], axis=1)
    blocks = [r.v_red[rows * i : rows * (i + 1)] for i in range(4)]
    right = jnp.concatenate(blocks + [r.v_out[:, 128:], spare], axis=1)
    r.grest[side, me] = jnp.where(side == 0, left, right).astype(bf16)
    loop(1, B, lambda k: rest_copy(k).start())

    for k in range(5, 11):
        local[k].wait()
    poolq, poolkv, table = r.poolq, r.poolkv, r.table
    poolq[...] = r.v_pool[:, 0, :]
    poolkv[:, :D] = r.v_pool[:, 1, :]
    poolkv[:, D:] = r.v_pool[:, 2, :]
    r.tablef[...] = jnp.zeros_like(r.tablef)
    relh_rows, relw_rows = r.v_relh.shape[0], r.v_relw.shape[0]
    for hd in range(2):
        r.tablef[128 * hd : 128 * hd + relh_rows, HD * hd : HD * (hd + 1)] = r.v_relh[...]
        r.tablef[128 * hd + 64 : 128 * hd + 64 + relw_rows, HD * hd : HD * (hd + 1)] = r.v_relw[...]
    table[...] = r.tablef[...].astype(bf16)
    shift_one = r.v_biases[0:1, 0:D]
    shift_two = r.v_biases[0:1, D : 2 * D]
    bias_q = r.v_biases[0:1, 2 * D : 3 * D]
    bias_kv = r.v_biases[0:1, 3 * D : 5 * D]
    bias_out = r.v_biases[0:1, 5 * D : 6 * D]
    bias_exp = r.v_biases[0:1, 6 * D : 6 * D + HID]
    bias_red = r.v_biases[0:1, 6 * D + HID : 7 * D + HID]
    gain_one = r.v_gains[0:1, :]
    gain_two = r.v_gains[1:2, :]
    acc, paccq, pacckv = r.acc, r.paccq, r.pacckv
    acc[...] = jnp.zeros_like(acc)
    paccq[...] = jnp.zeros_like(paccq)
    pacckv[...] = jnp.zeros_like(pacckv)
    kvx, qx, dqx = r.kvx, r.qx, r.dqx

    cell = iota((T, 1), 0)
    cell_y, cell_x = hh * R + cell % R, cell // R
    halo_at = iota((2 * IMG * HX, 1), 0)

    def cell_mask(n):
        return ((cell_y < r.extent[0, n]) & (cell_x < r.extent[1, n])).astype(f32)

    def first_norm(n):
        hat, inverse = normalise(r.v_act[n].astype(f32))
        r.ne[n] = (hat * gain_one + shift_one).astype(bf16)
        r.hat_one[n] = hat
        r.inv_one[n] = inverse
        kvx[n, 0:R, :] = jnp.zeros((R, 2 * D), f32)
        kvx[n, T + R :, :] = jnp.zeros((R, 2 * D), f32)
        for x in (qx, dqx):
            x[n, 0:R, :] = jnp.zeros((R, D), f32)
            x[n, T + R :, :] = jnp.zeros((R, D), f32)

    for n in range(IMG):
        first_norm(n)

    spread_rows = iota((T, 2 * HX), 0)
    spread_cols = iota((T, 2 * HX), 1)
    spread = (
        (spread_rows // R == spread_cols % HX) & (spread_rows % R == (spread_cols // HX) * (R - 1))
    ).astype(bf16)
    r.spread[...] = jnp.concatenate([spread, spread], axis=1)
    pick_rows = iota((KL * KCP, T // 2), 0)
    pick_cols = iota((KL * KCP, T // 2), 1)
    pick = (
        (pick_rows % KCP == pick_cols // R) & (pick_cols % R == 2 * (pick_rows // KCP))
    ).astype(bf16)
    r.pick[...] = jnp.concatenate([pick, pick], axis=1)
    back_rows = iota((3 * T // 2, KROWS), 0)
    back_cols = iota((3 * T // 2, KROWS), 1)
    back_tap, back_cell = back_rows // (T // 2), back_rows % (T // 2)
    unpick = (
        (back_cols % KCP == back_cell // R)
        & (back_cell % R == 2 * (back_cols // KCP) + back_tap - 1)
    ).astype(bf16)
    r.unpick[...] = jnp.concatenate([unpick, unpick], axis=1)
    key_rows = iota((KEYS, 64), 0)
    key_lane = iota((KEYS, 64), 1) % 32
    r.hot[...] = (
        (key_lane == key_rows // KCP) | (key_lane == KR + key_rows % KCP)
    ).astype(bf16)
    halo_up.wait_recv()
    halo_down.wait_recv()
    hat, _ = normalise(r.hr[...].reshape(2 * IMG * HX, D).astype(f32))
    r.nh[...] = (hat * gain_one + shift_one).astype(bf16)

    halo_y = jnp.where(halo_at < IMG * HX, hh * R - 1, hh * R + R)
    halo_image = halo_at // HX % IMG
    halo_ok = jnp.zeros((2 * IMG * HX, 1), jnp.bool_)
    for n in range(IMG):
        halo_ok = halo_ok | (
            (halo_image == n)
            & (halo_y >= 0)
            & (halo_y < r.extent[0, n])
            & (halo_at % HX < r.extent[1, n])
        )
    halo_ok = halo_ok.astype(f32)

    wq, wkv, wout, wexp, wred = r.wq, r.wkv, r.wout, r.wexp, r.wred

    loop(1, B, lambda k: in_arrival(0, k).wait_recv())
    in_handed(side, twin).start()
    in_handed(1 - side, hh).wait_recv()
    for b in range(B):
        for i in range(2):
            r.f_kv[rows * b : rows * (b + 1), D * i : D * (i + 1)] = r.gkv[i, b].astype(f32)
    wkv[...] = r.f_kv[...].astype(bf16)

    kvg = r.kvg

    def kv_copy(n, k, source, target):
        slot = kvg.at[source, n]
        return to_height(slot, slot, r.s_ksend.at[n, k], r.s_krecv.at[n, k], target)

    half = IMG * HX
    r.halo_kv[...] = (nn(r.nh[:half], wkv[...]) + bias_kv) * halo_ok[:half]

    def columns(x, b):
        pairs = x.reshape(TX // (2 * R), 2 * R, x.shape[1])
        side = pairs[b // 2 : b // 2 + KC, R * (b % 2) : R * (b % 2) + R]
        return side.reshape(T // 2, x.shape[1])

    def keys_values(n):
        kvx[n, R : R + T, :] = (nn(r.ne[n], wkv[...]) + bias_kv) * cell_mask(n)
        field = kvx[n]
        sides = [columns(field, b) for b in range(3)]
        sums = [sum(poolkv[3 * a + b : 3 * a + b + 1, :] * sides[b] for b in range(3)) for a in range(3)]
        pooled = rolled(sums[0], 1) * (iota((T // 2, 1), 0) % R > 0).astype(f32) + sums[1] + rolled(sums[2], -1)
        edge = r.halo_kv[pl.ds(pl.multiple_of(n * HX, HX), HX), :]
        edge = (
            poolkv[0:1, :] * rolled(edge, 1) + poolkv[1:2, :] * edge + poolkv[2:3, :] * rolled(edge, -1)
        )
        edge_pick = (iota((KCP, HX), 1) == 2 * iota((KCP, HX), 0)).astype(bf16)
        edge = nn(jnp.concatenate([edge_pick, edge_pick], axis=1), halves(edge, 0))
        whole = nn(r.pick[...], halves(pooled, 0))
        kvg[hh, n] = jnp.concatenate([whole[:KCP] + edge, whole[KCP:]], axis=0).astype(bf16)
        kv_copy(n, 1, hh, across).start()
        kv_copy(n, 0, hh, twin).start()

    for n in range(IMG):
        keys_values(n)

    loop(1, B, lambda k: in_arrival(1, k).wait_recv())
    for b in range(B):
        r.f_q[rows * b : rows * (b + 1), :] = r.gq_in[b].astype(f32)
    wq[...] = r.f_q[...].astype(bf16)
    qp, qa = r.qp, r.qa
    r.halo_q[...] = (nn(r.nh[...], wq[...]) + bias_q) * halo_ok
    lane = iota((T, 128), 1)
    y_at = hh * R + iota((T, 128), 0) % R
    x_at = iota((T, 128), 0) // R
    aux = lane % 32
    spot = jnp.where(aux < KR, y_at - 2 * aux + 2 * (KR - 1), 64 + x_at - 2 * (aux - KR) + 2 * (KC - 1))
    inner_top = (cell % R > 0).astype(f32)
    inner_low = (cell % R < R - 1).astype(f32)

    def beside(x):
        return [rolled(x, 1), x, rolled(x, -1)]

    def queries(n):
        qx[n, R : R + T, :] = (nn(r.ne[n], wq[...]) + bias_q) * cell_mask(n)
        field = qx[n]
        sums = [
            sum(poolq[3 * a + b : 3 * a + b + 1, :] * field[R * b : R * b + T] for b in range(3))
            for a in range(3)
        ]
        top = beside(r.halo_q[pl.ds(pl.multiple_of(n * HX, HX), HX), :])
        low = beside(r.halo_q[pl.ds(pl.multiple_of((IMG + n) * HX, HX), HX), :])
        top = sum(poolq[b : b + 1, :] * top[b] for b in range(3))
        low = sum(poolq[6 + b : 7 + b, :] * low[b] for b in range(3))
        edge = nn(r.spread[...], halves(jnp.concatenate([top, low], axis=0), 0))
        pooled = rolled(sums[0], 1) * inner_top + sums[1] + rolled(sums[2], -1) * inner_low + edge
        qp[n] = pooled
        query = pooled.astype(bf16)
        r.qh[n] = query
        along = nt(query, table[...])
        left, right = pooled[:, :128], pooled[:, 128:]
        right = jnp.concatenate([right, right], axis=1)
        for hd in range(2):
            near = along[:, 128 * hd : 128 * (hd + 1)]
            near = jnp.take_along_axis(near, spot, axis=1, mode="promise_in_bounds") * (HD**0.5)
            rest = near - near.astype(bf16).astype(f32)
            near = jnp.where(lane < 96, near, rest)
            if hd == 0:
                qa[n, hd, :, :128] = jnp.where(lane < HD, left, 0.0).astype(bf16)
                qa[n, hd, :, 128:] = jnp.where(lane < 64, 0.0, near).astype(bf16)
            else:
                qa[n, hd, :, :128] = jnp.where(lane < HD, 0.0, left).astype(bf16)
                qa[n, hd, :, 128:] = jnp.where(lane < 64, right, near).astype(bf16)

    for n in range(IMG):
        queries(n)

    def kv_on(n):
        kv_copy(n, 1, across, hh).wait_recv()
        kv_copy(n, 2, across, twin).start()

    key_at = iota((KEYS, 1), 0)
    probs, mxh = r.probs, r.mxh

    def attention(n):
        kv_copy(n, 0, twin, hh).wait_recv()
        kv_copy(n, 2, corner, hh).wait_recv()
        both = jnp.concatenate([kvg[s, n] for s in range(HG)], axis=0)
        r.ka[n, :, :D] = both[:, :D]
        r.ka[n, :, D:] = r.hot[...]
        r.va[n] = both[:, D:]
        valid = (2 * (key_at // KCP) < r.extent[0, n]) & (2 * (key_at % KCP) < r.extent[1, n])
        value = r.va[n].T
        mixed = []
        for hd in range(2):
            scores = nt(r.ka[n], qa[n, hd]) * SCALE
            scores = jnp.where(valid, scores, masked_value)
            raised = jnp.exp(scores - jnp.max(scores, axis=0, keepdims=True))
            prob = raised * (1.0 / jnp.sum(raised, axis=0, keepdims=True))
            probs[n, hd] = prob
            mixed.append(nn(value[HD * hd : HD * (hd + 1)], prob.astype(bf16)))
        mxh[n] = (jnp.concatenate(mixed, axis=0).T + qp[n]).astype(bf16)

    kv_on(0)
    kv_on(1)
    attention(0)
    kv_on(2)
    attention(1)
    loop(1, B, lambda k: rest_arrival(k).wait_recv())
    rest_handed(side, twin).start()
    attention(2)

    rest_handed(1 - side, hh).wait_recv()
    for b in range(B):
        one, two = r.grest[0, b].astype(f32), r.grest[1, b].astype(f32)
        r.f_exp[rows * b : rows * (b + 1), :] = one[:, :HID]
        for i in range(4):
            at = 4 * rows * b + rows * i
            r.f_red[at : at + rows, :] = two[:, D * i : D * (i + 1)]
        r.f_out[rows * b : rows * (b + 1), :128] = one[:, HID:]
        r.f_out[rows * b : rows * (b + 1), 128:] = two[:, 4 * D : 5 * D - 128]
    wout[...] = r.f_out[...].astype(bf16)
    wexp[...] = r.f_exp[...].astype(bf16)
    wred[...] = r.f_red[...].astype(bf16)

    def feed_forward(n):
        mask = cell_mask(n)
        middle = r.v_act[n].astype(f32) + nn(mxh[n], wout[...]) + bias_out
        hat, inverse = normalise(middle)
        second = (hat * gain_two + shift_two).astype(bf16)
        r.sh[n] = second
        expanded = nn(second, wexp[...]) + bias_exp
        half_erf = 0.5 + 0.5 * lax.erf(expanded * (0.5**0.5))
        activated = (expanded * half_erf).astype(bf16)
        slope = half_erf + expanded * jnp.exp(expanded * expanded * -0.5) * 0.3989422804014327
        r.ac[n] = activated
        r.mid[n] = middle
        upstream = r.v_cot[n].astype(f32) * mask
        up_half = upstream.astype(bf16)
        r.uh[n] = up_half
        expanded_grad = (nt(up_half, wred[...]) * slope).astype(bf16)
        r.eg[n] = expanded_grad
        second_grad = nt(expanded_grad, wexp[...])
        acc[0:1, 2 * D : 3 * D] += jnp.sum(second_grad * hat, axis=0, keepdims=True)
        acc[0:1, 3 * D : 4 * D] += jnp.sum(second_grad, axis=0, keepdims=True)
        middle_grad = upstream + normalise_back(second_grad, gain_two, hat, inverse)
        r.mgd[n] = middle_grad
        attn_grad = middle_grad.astype(bf16)
        r.ag[n] = attn_grad
        r.mg[n] = nt(attn_grad, wout[...]).astype(bf16)

    for n in range(IMG):
        feed_forward(n)

    ones = jnp.ones((16, IMG * T), bf16)

    def flat(ref):
        return ref[...].reshape(IMG * T, ref.shape[-1])

    r.f_exp[...] = tn(flat(r.sh), flat(r.eg))
    acc[2:3, :] = nn(ones, flat(r.eg))[0:1]
    r.f_red[...] = tn(flat(r.uh), flat(r.ac)).T
    acc[1:2, D : 2 * D] = nn(ones, flat(r.uh))[0:1]
    r.f_out[...] = tn(flat(mxh), flat(r.ag))
    acc[1:2, 0:D] = nn(ones, flat(r.ag))[0:1]
    spare = jnp.zeros((rows, PE - HID - 5 * D), f32)
    for b in range(B):
        r.d[1][b, :, :HID] = r.f_exp[rows * b : rows * (b + 1), :].astype(bf16)
        out_rows = r.f_out[rows * b : rows * (b + 1), :]
        r.d[1][b, :, HID:PH] = out_rows[:, :128].astype(bf16)
        blocks = [r.f_red[rows * (4 * b + i) : rows * (4 * b + i + 1), :] for i in range(4)]
        r.d[1][b, :, PH:] = jnp.concatenate(blocks + [out_rows[:, 128:], spare], axis=1).astype(bf16)

    def one_copy(i, half, target):
        return to_height(
            r.d[i].at[pl.ds(half * HB, HB)], r.p[i], r.s_onesend.at[i], r.s_onerecv.at[i], target
        )

    def two_copy(i, j, b):
        return to_batch(r.t[i].at[j], r.u[i].at[me], r.s_twosend.at[i, j], r.s_tworecv.at[i, me], b)

    def two_arrival(i, b):
        return to_batch(r.t[i].at[0], r.u[i].at[b], r.s_twosend.at[i, 0], r.s_tworecv.at[i, b], b)

    def three_own(i):
        return pltpu.make_async_copy(r.z[i].at[pair], r.o_z[i].at[pair], r.s_three.at[i])

    def three_copy(i, k, which, target):
        return to_height(r.z[i].at[which], r.o_z[i].at[which], r.s_threesend.at[i, k], r.s_threerecv.at[i, which], target)

    others = (twin, across, corner)
    owned = lax.div(me, HB) == side

    def stage_one(i):
        one_copy(i, 1 - side, twin).start()

    def stage_two(i):
        one_copy(i, side, hh).wait_recv()

        def add(j):
            b = side * HB + j
            r.t[i][j] = (r.d[i][b].astype(f32) + r.p[i][j].astype(f32)).astype(bf16)

            @pl.when(b != me)
            def _():
                two_copy(i, j, b).start()

        loop(0, HB, add)

    def stage_three(i):
        @pl.when(owned)
        def _():
            loop(1, B, lambda k: two_arrival(i, next_batch(k)).wait_recv())
            r.u[i][me] = r.t[i][me - side * HB]
            total = r.u[i][0].astype(f32)
            for b in range(1, B):
                total = total + r.u[i][b].astype(f32)
            r.z[i][pair] = total.astype(r.z[i].dtype)
            for k, target in enumerate(others):
                three_copy(i, k, pair, target).start()
            three_own(i).start()

    def stage_four(i):
        @pl.when(jnp.logical_not(owned))
        def _():
            three_copy(i, 0, pair, hh).wait_recv()

        three_copy(i, 0, 1 - pair, hh).wait_recv()

    def early_one(k, part, target):
        return to_height(r.sp[0].at[part], r.sr[0].at[k - 1], r.s_earlysend.at[k - 1], r.s_earlyrecv.at[k - 1], target)

    def late_one(half, target):
        return to_height(r.sp[1].at[half], r.sr[1].at[0], r.s_late.at[0], r.s_late.at[1], target)

    def small_two(j, k):
        slot = r.su[j].at[me]
        return to_batch(slot, slot, r.s_smalltwo.at[j, k], r.s_smalltwor.at[j, me], next_batch(k))

    def small_two_arrival(j, k):
        b = next_batch(k)
        slot = r.su[j].at[b]
        return to_batch(slot, slot, r.s_smalltwo.at[j, k], r.s_smalltwor.at[j, b], b)

    def small_own(j):
        return pltpu.make_async_copy(r.sz[j].at[hh], r.o_sz[j].at[hh], r.s_smallown.at[j])

    def small_three(j, k, which, target):
        return to_height(r.sz[j].at[which], r.o_sz[j].at[which], r.s_smallthree.at[j, k], r.s_smallthreer.at[j, which], target)

    def small_stage_one(j):
        if j == 0:
            for k in range(1, HG):
                early_one(k, next_height(k), next_height(k)).start()
        else:
            late_one(1 - side, twin).start()

    def small_stage_one_sent(j):
        if j == 0:
            for k in range(1, HG):
                early_one(k, next_height(k), next_height(k)).wait_send()
        else:
            late_one(1 - side, twin).wait_send()

    def small_stage_two(j):
        if j == 0:
            total = r.sp[0][hh]
            for k in range(1, HG):
                early_one(k, hh, hh).wait_recv()
                total = total + r.sr[0][k - 1]
        else:
            late_one(side, hh).wait_recv()
            total = r.sp[1][side] + r.sr[1][0]
        r.su[j][me] = total.astype(bf16)
        loop(1, B, lambda k: small_two(j, k).start())

    def small_stage_three(j):
        loop(1, B, lambda k: small_two_arrival(j, k).wait_recv())
        total = r.su[j][0].astype(f32)
        for b in range(1, B):
            total = total + r.su[j][b].astype(f32)
        r.sz[j][hh] = total
        for k, target in enumerate(others):
            small_three(j, k, hh, target).start()
        small_own(j).start()

    def small_stage_four(j):
        for other in others:
            small_three(j, 0, other, hh).wait_recv()

    stage_one(1)

    dkv = r.dkv
    y_lane = jnp.where(lane < 64, y_at + 2 * (KR - 1) - lane, x_at + 2 * (KC - 1) - (lane - 64))
    back_at = y_lane // 2
    back_ok = (y_lane >= 0) & (y_lane % 2 == 0) & (back_at < jnp.where(lane < 64, KR, KC))
    back_spot = jnp.where(back_ok, back_at + jnp.where(lane < 64, 64, 64 + KR), 0)
    back_ok = back_ok.astype(f32)

    def key_rows_of(ref, n, h):
        return ref.at[n, pl.ds(pl.multiple_of(h * (KL * KCP), KL * KCP), KROWS), :]

    def dkv_one(n, k, h, target):
        return to_height(key_rows_of(dkv, n, h), r.dkvr.at[k, n], r.s_dsend.at[n, k], r.s_drecv.at[n, k], target)

    def dkv_two(n, target):
        return to_height(r.dkvs.at[n], r.dkvr.at[2, n], r.s_dsend.at[n, 2], r.s_drecv.at[n, 2], target)

    def dkv_on(n):
        dkv_one(n, 0, across, hh).wait_recv()
        r.dkvs[n] = (key_rows_of(dkv, n, across)[...].astype(f32) + r.dkvr[0, n].astype(f32)).astype(bf16)
        dkv_two(n, across).start()

    def halo_back(n, k, target):
        return to_height(
            r.dqs.at[k, n], r.dqr.at[1 - k, n], r.s_qsend.at[n, k], r.s_qrecv.at[n, 1 - k], target
        )

    head = iota((T, D), 1) < HD

    def heads(x):
        x = x.astype(f32)
        return [jnp.where(head, x, 0.0).astype(bf16), jnp.where(head, 0.0, x).astype(bf16)]

    def scores_back(n):
        value = r.va[n]
        mixed_heads, query_heads = heads(r.mg[n]), heads(r.qh[n])
        key_grad, value_grad = 0.0, 0.0
        for hd in range(2):
            prob = probs[n, hd]
            prob_grad = nt(value, mixed_heads[hd])
            inner = jnp.sum(prob * prob_grad, axis=0, keepdims=True)
            score_grad = (prob * (prob_grad - inner)).astype(bf16)
            r.sg[n, hd] = score_grad
            value_grad = value_grad + nn(prob.astype(bf16), mixed_heads[hd])
            key_grad = key_grad + nn(score_grad, query_heads[hd])
        dkv[n, 0:KEYS, :D] = (key_grad * SCALE).astype(bf16)
        dkv[n, 0:KEYS, D:] = value_grad.astype(bf16)
        dkv[n, KEYS:, :] = jnp.zeros((dkv.shape[1] - KEYS, 2 * D), bf16)
        dkv_one(n, 0, corner, twin).start()
        dkv_one(n, 1, twin, twin).start()

    def rows_back(n):
        keys = r.ka[n].T
        dq, along = [], []
        for hd in range(2):
            here = jnp.concatenate([keys[HD * hd : HD * (hd + 1)], keys[D : D + 32]], axis=0)
            back = nn(here, r.sg[n, hd])
            dq.append(back[:HD])
            along.append(back[HD:])
        back = jnp.concatenate(dq + along, axis=0).T
        right = back[:, 128:]
        apart = []
        for hd in range(2):
            apart.append(
                jnp.take_along_axis(right, back_spot + 32 * hd, axis=1, mode="promise_in_bounds") * back_ok
            )
        apart = halves(jnp.concatenate(apart, axis=1), 1)
        r.dr[n] = apart
        from_tables = nn(apart, jnp.concatenate([table[...], table[...]], axis=0))
        dqx[n, R : R + T, :] = back[:, :D] * SCALE + from_tables + r.mg[n].astype(f32)
        outer = nn(edges, dqx[n, R : R + T, :].astype(bf16)).astype(bf16)
        r.dqs[0, n] = outer[:HX]
        r.dqs[1, n] = outer[HX:]
        halo_back(n, 0, above).start()
        halo_back(n, 1, below).start()

    scores_back(0)
    scores_back(1)
    dkv_on(0)
    scores_back(2)
    dkv_on(1)
    stage_two(1)
    rows_back(0)
    rows_back(1)
    dkv_on(2)
    rows_back(2)

    both = tn(flat(r.qh), flat(r.dr))
    rel = (
        both[:HD, 0:128] + both[:HD, 256:384] + both[HD:, 128:256] + both[HD:, 384:512]
    )
    rel = jnp.concatenate([rel, jnp.zeros((128 - HD, 128), f32)], axis=0).T
    early = r.early
    early[...] = jnp.zeros_like(early)
    early[0:48, 0:128] = rel[0:48]
    early[0:48, 128:256] = rel[48:96]
    early[0:32, 256:384] = rel[96:128]
    early[48:49, :] = acc[0:1, 2 * D :]
    early[49:50, :] = acc[1:2, 0 : 2 * D]
    early[50:51, :] = acc[2:3, : 2 * D]
    early[51:52, :] = acc[2:3, 2 * D :]
    for k in range(HG):
        r.sp[0][k] = early[16 * k : 16 * (k + 1), :]
    small_stage_one(0)

    has_above = (hh > 0).astype(f32)
    has_below = (hh < HG - 1).astype(f32)

    def queries_back(n):
        halo_back(n, 0, below).wait_recv()
        halo_back(n, 1, above).wait_recv()
        edge = jnp.concatenate([r.dqr[0, n].astype(f32) * has_above, r.dqr[1, n].astype(f32) * has_below], axis=0)
        edge = nn(r.spread[:, : 2 * HX], edge.astype(bf16))
        nothing = jnp.zeros((R, D), f32)
        field = dqx[n]
        whole = field[R : R + T]
        later = jnp.concatenate([nothing, rolled(whole, -1) * inner_low + edge * (1.0 - inner_low), nothing], axis=0)
        sooner = jnp.concatenate([nothing, rolled(whole, 1) * inner_top + edge * (1.0 - inner_top), nothing], axis=0)
        own = qx[n, R : R + T, :]
        total = 0.0
        for a, moved in enumerate((later, field, sooner)):
            for b in range(3):
                here = moved[R * (2 - b) : R * (2 - b) + T]
                total = total + poolq[3 * a + b : 3 * a + b + 1, :] * here
                paccq[3 * a + b] += folded(here * own)
        r.pq[n] = (total * cell_mask(n)).astype(bf16)

    def keys_values_back(n):
        dkv_one(n, 1, hh, hh).wait_recv()
        dkv_two(n, hh).wait_recv()
        total = key_rows_of(dkv, n, hh)[...].astype(f32) + r.dkvr[1, n].astype(f32) + r.dkvr[2, n].astype(f32)
        wide = nn(r.unpick[...], halves(total, 0))
        taps = [wide[T // 2 * a : T // 2 * (a + 1)] for a in range(3)]
        field = kvx[n]
        sides = [columns(field, b) for b in range(3)]
        even, odd, late = 0.0, 0.0, 0.0
        for a in range(3):
            even = even + poolkv[3 * a + 1 : 3 * a + 2, :] * taps[a]
            odd = odd + poolkv[3 * a + 2 : 3 * a + 3, :] * taps[a]
            late = late + poolkv[3 * a : 3 * a + 1, :] * taps[a]
            for b in range(3):
                pacckv[3 * a + b] += folded(sides[b] * taps[a])
        odd = odd + jnp.concatenate([late[R:], jnp.zeros((R, 2 * D), f32)], axis=0)
        pairs = [x.reshape(KC, R, 2 * D) for x in (even, odd)]
        result = jnp.concatenate(pairs, axis=1).reshape(T, 2 * D)
        r.pkv[n] = (result * cell_mask(n)).astype(bf16)

    keys_values_back(0)
    keys_values_back(1)
    for n in range(IMG):
        queries_back(n)
    r.f_q[...] = tn(flat(r.ne), flat(r.pq))
    for b in range(B):
        r.d[2][b] = r.f_q[rows * b : rows * (b + 1), :].astype(bf16)
    stage_one(2)
    small_stage_two(0)
    for n in range(IMG):
        r.gq[n] = nt(r.pq[n], wq[...])
    stage_two(2)
    keys_values_back(2)

    r.f_kv[...] = tn(flat(r.ne), flat(r.pkv))
    for b in range(B):
        r.d[0][b] = r.f_kv[rows * b : rows * (b + 1), :].astype(bf16)
    stage_one(0)

    def projection_back(n):
        grad = r.gq[n] + nt(r.pkv[n], wkv[...])
        hat = r.hat_one[n]
        acc[0:1, 0:D] += jnp.sum(grad * hat, axis=0, keepdims=True)
        acc[0:1, D : 2 * D] += jnp.sum(grad, axis=0, keepdims=True)
        r.v_ig[n] = r.mgd[n] + normalise_back(grad, gain_one, hat, r.inv_one[n])

    projection_back(0)
    projection_back(1)
    stage_two(0)
    projection_back(2)
    input_out = pltpu.make_async_copy(r.v_ig, r.o_ig, r.s_out.at[1])
    input_out.start()

    late = r.late
    for t in range(9):
        late[t : t + 1, :] = jnp.sum(pacckv[t], axis=0, keepdims=True)
        late[11 + t // 2 : 12 + t // 2, D * (t % 2) : D * (t % 2 + 1)] = jnp.sum(paccq[t], axis=0, keepdims=True)
    late[9:10, :] = nn(ones, flat(r.pkv))[0:1]
    late[10:11, :] = acc[0:1, 0 : 2 * D]
    late[15:16, D:] = nn(ones, flat(r.pq))[0:1]
    for k in range(2):
        r.sp[1][k] = late[8 * k : 8 * (k + 1), :]
    small_stage_one(1)

    def output(n):
        r.v_res[n] = (cell_mask(n) * (r.mid[n] + nn(r.ac[n], wred[...]) + bias_red)).astype(bf16)

    output(0)
    output(1)
    small_stage_two(1)
    output(2)
    result_out = pltpu.make_async_copy(r.v_res, r.o_res, r.s_out.at[0])
    result_out.start()
    stage_three(1)
    stage_three(2)
    small_stage_three(0)
    for copy in (halo_up, halo_down, in_handed(side, twin), rest_handed(side, twin)):
        copy.wait_send()

    def sent_weights(k):
        in_copy(0, k).wait_send()
        in_copy(1, k).wait_send()
        rest_copy(k).wait_send()
        for j in range(2):
            small_two(j, k).wait_send()

    loop(1, B, sent_weights)

    def sent_images(n):
        kv_copy(n, 0, hh, twin).wait_send()
        kv_copy(n, 1, hh, across).wait_send()
        kv_copy(n, 2, across, twin).wait_send()
        dkv_one(n, 0, corner, twin).wait_send()
        dkv_one(n, 1, twin, twin).wait_send()
        dkv_two(n, across).wait_send()
        halo_back(n, 0, above).wait_send()
        halo_back(n, 1, below).wait_send()

    loop(0, IMG, sent_images)
    for i in range(3):
        one_copy(i, 1 - side, twin).wait_send()
    for j in range(2):
        small_stage_one_sent(j)

    def sent_two(j):
        @pl.when(side * HB + j != me)
        def _():
            for i in range(3):
                two_copy(i, j, side * HB + j).wait_send()

    loop(0, HB, sent_two)

    stage_three(0)
    small_stage_three(1)
    for i in (1, 2, 0):
        stage_four(i)
    for j in range(2):
        small_stage_four(j)
    for j in range(2):
        small_own(j).wait()
        for k, target in enumerate(others):
            small_three(j, k, hh, target).wait_send()

    @pl.when(owned)
    def _():
        for i in range(3):
            three_own(i).wait()
            for k, target in enumerate(others):
                three_copy(i, k, pair, target).wait_send()

    result_out.wait()
    input_out.wait()


def adam_step(weight, first_state, second_state, gradient, step_rate, decay_rate):
    moment = beta_one * first_state + (1.0 - beta_one) * gradient
    square = beta_two * second_state + (1.0 - beta_two) * gradient * gradient
    unbiased = moment * (1.0 / (1.0 - beta_one**STEP))
    scaled = square * (1.0 / (1.0 - beta_two**STEP))
    updated = weight * (1.0 - step_rate * decay_rate) - step_rate * unbiased / (jnp.sqrt(scaled) + adam_eps)
    return (updated, moment, square)


def adam_kernel(tree, *refs):
    r = types.SimpleNamespace(**jax.tree.unflatten(tree, refs))

    def row(ref):
        return ref.at[0] if ref.shape[0] == 1 and len(ref.shape) == 2 else ref

    arrivals = []
    for index, (source, target) in enumerate(zip(r.given, r.v_given)):
        arrivals.append(pltpu.make_async_copy(source, row(target), r.s_in.at[index]))
        arrivals[-1].start()
    through = [(r.ig, r.v_ig, r.o_ig), (r.res, r.v_res, r.o_res)]
    through = [
        (pltpu.make_async_copy(a, b, r.s_through.at[k]), pltpu.make_async_copy(b, c, r.s_through.at[2 + k]))
        for k, (a, b, c) in enumerate(through)
    ]
    for enter, _ in through:
        enter.start()
    for i in range(5):
        arrivals[i].wait()
    planes = [x[0].astype(f32) + x[1].astype(f32) for x in r.v_given[0:3]]
    early, late = r.v_given[3:5]
    early = jnp.concatenate([early[k] for k in range(HG)], axis=0)
    late = jnp.concatenate([late[0] + late[2], late[1] + late[3]], axis=0)
    pack = planes[1]
    rel = jnp.concatenate([early[0:48, 0:128], early[0:48, 128:256], early[0:32, 256:384]], axis=0)
    for t in range(9):
        r.pgrad[t, 0:1, :] = late[11 + t // 2 : 12 + t // 2, D * (t % 2) : D * (t % 2 + 1)]
        r.pgrad[t, 1:2, :] = late[t : t + 1, 0:D]
        r.pgrad[t, 2:3, :] = late[t : t + 1, D:]
    bgrad = r.bgrad
    bgrad[0:1, 0:D] = late[10:11, D:]
    bgrad[0:1, D : 2 * D] = early[48:49, D:]
    bgrad[0:1, 2 * D : 3 * D] = late[15:16, D:]
    bgrad[0:1, 3 * D : 5 * D] = late[9:10, :]
    bgrad[0:1, 5 * D : 6 * D] = early[49:50, 0:D]
    bgrad[0:1, 6 * D : 8 * D] = early[50:51, :]
    bgrad[0:1, 8 * D : 10 * D] = early[51:52, :]
    bgrad[0:1, 10 * D :] = early[49:50, D:]
    given = [r.v_given[5 + 3 * index : 8 + 3 * index] for index in range(9)]
    gradients = [
        lambda: jnp.concatenate([planes[2], planes[0]], axis=1),
        lambda: jnp.concatenate([pack[:, HID:PH], pack[:, PH + 4 * D : PH + 5 * D - 128]], axis=1),
        lambda: pack[:, :HID],
        lambda: jnp.concatenate([pack[:, PH + D * i : PH + D * (i + 1)] for i in range(4)], axis=0),
        lambda: r.pgrad[...],
        lambda: rel[0 : given[5][0].shape[0], 0:HD],
        lambda: rel[64 : 64 + given[6][0].shape[0], 0:HD],
        lambda: jnp.concatenate([late[10:11, 0:D], early[48:49, 0:D]], axis=0),
        lambda: bgrad[...],
    ]
    leaving = []

    def leave(index):
        copy = pltpu.make_async_copy(row(r.v_fresh[index]), r.fresh[index], r.s_out.at[index])
        copy.start()
        leaving.append(copy)

    for index in range(9):
        for k in range(3):
            arrivals[5 + 3 * index + k].wait()
        weight, first, second = [x[...] for x in given[index]]
        fresh = adam_step(
            weight, first, second, gradients[index](), step_rates[index], decay_rates[index]
        )
        if index < 4:
            fresh += (fresh[0].astype(bf16),)
        at = 4 * min(index, 4) + 3 * max(index - 4, 0)
        for k, value in enumerate(fresh):
            r.v_fresh[at + k][...] = value
            leave(at + k)
        if index == 0:
            for enter, leave_again in through:
                enter.wait()
                leave_again.start()
                leaving.append(leave_again)
    for copy in leaving:
        copy.wait()


def shards(activations, cotangent, extent, *params):
    B = lax.axis_size("batch")
    assert lax.axis_size("height") == HG and activations.shape == (IMG, R, C, D)
    params = list(params)
    for k in range(12, 15):
        params[k] = params[k].transpose(1, 0, 2)
    weights = params[0::3]
    rows = weights[0].shape[0]
    HB = B // 2
    assert weights[3].shape[0] == 4 * rows

    def by_column(x):
        return x.transpose(0, 2, 1, 3).reshape(IMG, T, D)

    def like(x):
        return jax.ShapeDtypeStruct(x.shape, x.dtype)

    anywhere = pl.BlockSpec(memory_space=pl.ANY)
    vm, dma = pltpu.VMEM, pltpu.SemaphoreType.DMA

    def call(kernel, operands, results, scratch, specs, **kwargs):
        flat_operands, operand_tree = jax.tree.flatten(operands)
        flat_results, result_tree = jax.tree.flatten(results)
        whole, tree = jax.tree.flatten({**operands, **results, **scratch})
        order = {id(x): k for k, x in enumerate(flat_operands + flat_results + jax.tree.leaves(scratch))}
        places = [order[id(x)] for x in whole]

        def ordered(*refs):
            return kernel(tree, *[refs[k] for k in places])

        out = pl.pallas_call(
            ordered,
            out_shape=flat_results,
            in_specs=[specs.get(id(x), anywhere) for x in flat_operands],
            out_specs=[anywhere] * len(flat_results),
            scratch_shapes=jax.tree.leaves(scratch),
            **kwargs,
        )(*flat_operands)
        return jax.tree.unflatten(result_tree, out)

    operands = dict(
        act=by_column(activations),
        cot=by_column(cotangent),
        extent=extent.T,
        w_in=weights[0],
        w_out=weights[1],
        w_exp=weights[2],
        w_red=weights[3],
        pool=weights[4],
        relh=weights[5],
        relw=weights[6],
        gains=weights[7],
        biases=weights[8],
    )
    results = dict(
        o_res=jax.ShapeDtypeStruct((IMG, T, D), bf16),
        o_ig=jax.ShapeDtypeStruct((IMG, T, D), f32),
        o_z=[jax.ShapeDtypeStruct((2, rows, x), y) for x, y in ((2 * D, f32), (PE, bf16), (D, f32))],
        o_sz=[jax.ShapeDtypeStruct((HG, x, 2 * D), f32) for x in (16, 8)],
    )
    lanes = (2 * D, PE, D)
    scratch = dict(
        v_act=vm((IMG, T, D), bf16),
        v_cot=vm((IMG, T, D), bf16),
        v_in=vm(weights[0].shape, f32),
        v_out=vm(weights[1].shape, f32),
        v_exp=vm(weights[2].shape, f32),
        v_red=vm(weights[3].shape, f32),
        v_pool=vm(weights[4].shape, f32),
        v_relh=vm(weights[5].shape, f32),
        v_relw=vm(weights[6].shape, f32),
        v_gains=vm(weights[7].shape, f32),
        v_biases=vm((1,) + weights[8].shape, f32),
        gkv=vm((2, B, rows, D), bf16),
        gq_in=vm((B, rows, D), bf16),
        grest=vm((2, B, rows, PH), bf16),
        d=[vm((B, rows, x), bf16) for x in lanes],
        p=[vm((HB, rows, x), bf16) for x in lanes],
        t=[vm((HB, rows, x), bf16) for x in lanes],
        u=[vm((B, rows, x), bf16) for x in lanes],
        z=[vm(x.shape, x.dtype) for x in results["o_z"]],
        sp=[vm((HG, 16, 2 * D), f32), vm((2, 8, 2 * D), f32)],
        sr=[vm((HG - 1, 16, 2 * D), f32), vm((1, 8, 2 * D), f32)],
        su=[vm((B, x, 2 * D), bf16) for x in (16, 8)],
        sz=[vm(x.shape, x.dtype) for x in results["o_sz"]],
        early=vm((64, 2 * D), f32),
        late=vm((16, 2 * D), f32),
        f_q=vm((D, D), f32),
        f_kv=vm((D, 2 * D), f32),
        f_exp=vm((D, HID), f32),
        f_red=vm((HID, D), f32),
        f_out=vm((D, D), f32),
        wq=vm((D, D), bf16),
        wkv=vm((D, 2 * D), bf16),
        wout=vm((D, D), bf16),
        wexp=vm((D, HID), bf16),
        wred=vm((HID, D), bf16),
        poolq=vm((9, D), f32),
        poolkv=vm((9, 2 * D), f32),
        tablef=vm((256, D), f32),
        table=vm((256, D), bf16),
        hs=vm((2, IMG, HX, D), bf16),
        hr=vm((2, IMG, HX, D), bf16),
        nh=vm((2 * IMG * HX, D), bf16),
        halo_q=vm((2 * IMG * HX, D), f32),
        halo_kv=vm((IMG * HX, 2 * D), f32),
        spread=vm((T, 4 * HX), bf16),
        pick=vm((KL * KCP, T), bf16),
        unpick=vm((3 * T // 2, 2 * KROWS), bf16),
        hot=vm((KEYS, 64), bf16),
        acc=vm((3, HID), f32),
        paccq=vm((9, 8, D), f32),
        pacckv=vm((9, 8, 2 * D), f32),
        ne=vm((IMG, T, D), bf16),
        hat_one=vm((IMG, T, D), f32),
        inv_one=vm((IMG, T, 1), f32),
        kvx=vm((IMG, TX, 2 * D), f32),
        qx=vm((IMG, TX, D), f32),
        dqx=vm((IMG, TX, D), f32),
        kvg=vm((HG, IMG, KL * KCP, 2 * D), bf16),
        ka=vm((IMG, KEYS, 256), bf16),
        va=vm((IMG, KEYS, D), bf16),
        qp=vm((IMG, T, D), f32),
        qh=vm((IMG, T, D), bf16),
        qa=vm((IMG, 2, T, 256), bf16),
        probs=vm((IMG, 2, KEYS, T), f32),
        sg=vm((IMG, 2, KEYS, T), bf16),
        mxh=vm((IMG, T, D), bf16),
        sh=vm((IMG, T, D), bf16),
        ac=vm((IMG, T, HID), bf16),
        uh=vm((IMG, T, D), bf16),
        eg=vm((IMG, T, HID), bf16),
        mgd=vm((IMG, T, D), f32),
        mid=vm((IMG, T, D), f32),
        ag=vm((IMG, T, D), bf16),
        mg=vm((IMG, T, D), bf16),
        v_res=vm((IMG, T, D), bf16),
        v_ig=vm((IMG, T, D), f32),
        dkv=vm((IMG, KEYS + KL * KCP, 2 * D), bf16),
        dkvr=vm((3, IMG, KROWS, 2 * D), bf16),
        dkvs=vm((IMG, KROWS, 2 * D), bf16),
        dqs=vm((2, IMG, HX, D), bf16),
        dqr=vm((2, IMG, HX, D), bf16),
        dr=vm((IMG, T, 512), bf16),
        pq=vm((IMG, T, D), bf16),
        gq=vm((IMG, T, D), f32),
        pkv=vm((IMG, T, 2 * D), bf16),
        s_local=dma((11,)),
        s_out=dma((2,)),
        s_isend=dma((2, B)),
        s_irecv=dma((2, B)),
        s_wsend=dma((B,)),
        s_wrecv=dma((B,)),
        s_hand=dma((4,)),
        s_hsend=dma((2,)),
        s_hrecv=dma((2,)),
        s_ksend=dma((IMG, 3)),
        s_krecv=dma((IMG, 3)),
        s_dsend=dma((IMG, 3)),
        s_drecv=dma((IMG, 3)),
        s_qsend=dma((IMG, 2)),
        s_qrecv=dma((IMG, 2)),
        s_onesend=dma((3,)),
        s_onerecv=dma((3,)),
        s_twosend=dma((3, HB)),
        s_tworecv=dma((3, B)),
        s_three=dma((3,)),
        s_smallown=dma((2,)),
        s_threesend=dma((3, 3)),
        s_threerecv=dma((3, 2)),
        s_earlysend=dma((HG - 1,)),
        s_earlyrecv=dma((HG - 1,)),
        s_late=dma((2,)),
        s_smalltwo=dma((2, B)),
        s_smalltwor=dma((2, B)),
        s_smallthree=dma((2, 3)),
        s_smallthreer=dma((2, HG)),
    )
    main = call(
        functools.partial(main_kernel, B),
        operands,
        results,
        scratch,
        {id(operands["extent"]): pl.BlockSpec(memory_space=pltpu.SMEM)},
        compiler_params=pltpu.CompilerParams(
            collective_id=0, has_side_effects=True, vmem_limit_bytes=60 * 1024 * 1024
        ),
        name="block",
    )
    given = main["o_z"] + main["o_sz"] + params
    fresh = []
    for index in range(9):
        fresh += [like(weights[index]) for _ in range(3)]
        if index < 4:
            fresh += [jax.ShapeDtypeStruct(weights[index].shape, bf16)]

    def room(x):
        return vm((1,) + x.shape if len(x.shape) == 1 else x.shape, x.dtype)

    fresh = call(
        adam_kernel,
        dict(given=given, res=main["o_res"], ig=main["o_ig"]),
        dict(fresh=fresh, o_res=like(main["o_res"]), o_ig=like(main["o_ig"])),
        dict(
            v_given=[room(x) for x in given],
            v_fresh=[room(x) for x in fresh],
            pgrad=vm(weights[4].shape, f32),
            bgrad=vm((1,) + weights[8].shape, f32),
            s_in=dma((len(given),)),
            s_out=dma((len(fresh),)),
            s_through=dma((4,)),
            v_res=vm((IMG, T, D), bf16),
            v_ig=vm((IMG, T, D), f32),
        ),
        {},
        name="adam",
    )
    res, ig, fresh = fresh["o_res"], fresh["o_ig"], fresh["fresh"]
    for k in range(16, 19):
        fresh[k] = fresh[k].transpose(1, 0, 2)

    def by_row(x):
        return x.reshape(IMG, C, R, D).transpose(0, 2, 1, 3)

    return (by_row(res), by_row(ig)) + tuple(fresh)


def solution(mesh):
    grid = P("batch", "height", None, None)
    rows = P("batch", None)
    in_specs = (grid, grid, rows) + (rows,) * 12 + (P(),) * 15
    out_specs = (grid, grid) + (rows,) * 16 + (P(),) * 15
    return jax.shard_map(shards, mesh=mesh, in_specs=in_specs, out_specs=out_specs, check_vma=False)
```
